32 devices in a mesh: dp: 16 (over z, y, x), sub: 2 (over core).
Axes of the slice: x: 2, y: 2, z: 4, core: 2. Of those that a mesh axis runs over, the one named last changes fastest.
Arguments:
- images: bfloat16 [256, 49, 2048], P(('dp', 'sub')), may hold values from -20 to 20
- pixel_mask: int32 [256, 49], P(('dp', 'sub')), may hold values from 0 to 1, as said below
- pairing: int32 [256], replicated, may hold values from 0 to 127, as said below
- w_reduce: bfloat16 [2048, 512], replicated, may hold values from -0.125 to 0.125
- w_spatial: bfloat16 [3, 3, 512, 512], replicated, may hold values from -0.09375 to 0.09375
- w_expand: bfloat16 [512, 2048], replicated, may hold values from -0.25 to 0.25
- w_project: bfloat16 [2048, 1024], replicated, may hold values from -0.125 to 0.125
- w_code: bfloat16 [1024, 128], replicated, may hold values from -0.1875 to 0.1875
- norm_reduce: float32 [2, 512], replicated, may hold values from 0.5 to 1.5
- norm_spatial: float32 [2, 512], replicated, may hold values from 0.5 to 1.5
- norm_expand: float32 [2, 2048], replicated, may hold values from 0.5 to 1.5
- norm_project: float32 [2, 1024], replicated, may hold values from 0.5 to 1.5
Outputs:
- loss_value: float32 [], replicated
- grad_images: float32 [256, 49, 2048], P(('dp', 'sub'))
- grad_reduce: float32 [2048, 512], replicated
- grad_spatial: float32 [3, 3, 512, 512], replicated
- grad_expand: float32 [512, 2048], replicated
- grad_project: float32 [2048, 1024], replicated
- grad_code: float32 [1024, 128], replicated
- grad_norm_reduce: float32 [2, 512], replicated
- grad_norm_spatial: float32 [2, 512], replicated
- grad_norm_expand: float32 [2, 2048], replicated
- grad_norm_project: float32 [2, 1024], replicated
The draws below stay inside these ranges and needn't reach their ends.
Inputs may be any that keep to these rules, and one draw needn't show every extreme that they name: `pixel_mask`: each image's valid pixels form the top-left block of 4 to 7 rows and 4 to 7 columns. `pairing`: every pair is named by exactly two images.
All inputs are finite; a program needn't handle non-finite values.
Results may differ from the reference program's by a relative error of at most 0.012.
Values sent between devices are 32-bit elements; how exact they have to be, the bound alone decides.
A program may use at most 320 MiB of HBM per device.

```python
import jax
import jax.numpy as jnp
from jax import lax

WIDTH = 2048
INNER = 512
PROJ_WIDTH = 1024
CODE = 128
SIDE = 7
PIXELS = 49
IMAGES = 256


def draw_images(key, part):
    key = jax.random.fold_in(key, 11)
    position = jnp.arange(IMAGES, dtype=jnp.float32) / (IMAGES - 1)
    level_scale = 1.0 + 4.0 * position
    noise_draw = jnp.clip(jax.random.normal(key, (IMAGES, PIXELS, WIDTH), jnp.float32), -4.0, 4.0)
    return (noise_draw * level_scale[:, None, None]).astype(jnp.bfloat16)


def draw_pixel_mask(key, part):
    key = jax.random.fold_in(key, 23)
    heights = jax.random.randint(jax.random.fold_in(key, 1), (IMAGES, 1), 4, SIDE + 1)
    widths_drawn = jax.random.randint(jax.random.fold_in(key, 2), (IMAGES, 1), 4, SIDE + 1)
    places = jnp.arange(PIXELS, dtype=jnp.int32)[None, :]
    inside = (places // SIDE < heights) & (places % SIDE < widths_drawn)
    return inside.astype(jnp.int32)


def draw_pairing(key, part):
    key = jax.random.fold_in(key, 37)
    return (jax.random.permutation(key, IMAGES) // 2).astype(jnp.int32)


def normal_values(rng, extent, width, most, held_as=jnp.bfloat16):
    drawn = jax.random.normal(rng, extent, jnp.float32) * width
    return jnp.minimum(jnp.maximum(drawn, -most), most).astype(held_as)


def setup_inputs(seed: int = 0) -> dict:
    keys = jax.random.split(jax.random.key(seed), 13)
    return {
        "images": draw_images(jax.random.fold_in(keys[12], 71), 0),
        "pixel_mask": draw_pixel_mask(jax.random.fold_in(keys[12], 71), 0),
        "pairing": draw_pairing(jax.random.fold_in(keys[12], 71), 0),
        "w_reduce": normal_values(keys[3], (WIDTH, INNER), WIDTH ** -0.5, 0.125),
        "w_spatial": normal_values(keys[4], (3, 3, INNER, INNER), (9 * INNER) ** -0.5, 0.09375),
        "w_expand": normal_values(keys[5], (INNER, WIDTH), INNER ** -0.5, 0.25),
        "w_project": normal_values(keys[6], (WIDTH, PROJ_WIDTH), WIDTH ** -0.5, 0.125),
        "w_code": normal_values(keys[7], (PROJ_WIDTH, CODE), PROJ_WIDTH ** -0.5, 0.1875),
        "norm_reduce": jnp.clip(jax.random.uniform(keys[8], (2, INNER), jnp.float32, 0.5, 1.5), 0.5, 1.5),
        "norm_spatial": jnp.clip(jax.random.uniform(keys[9], (2, INNER), jnp.float32, 0.5, 1.5), 0.5, 1.5),
        "norm_expand": jnp.clip(jax.random.uniform(keys[10], (2, WIDTH), jnp.float32, 0.5, 1.5), 0.5, 1.5),
        "norm_project": jnp.clip(jax.random.uniform(keys[11], (2, PROJ_WIDTH), jnp.float32, 0.5, 1.5), 0.5, 1.5),
    }


@jax.custom_vjp
def low(v):
    return lax.optimization_barrier(v.astype(jnp.bfloat16)).astype(jnp.float32)

@jax.custom_vjp
def low_back(v):
    return v

def low_keep(v):
    return (low(v), None)

def low_pass(kept, grad):
    return (grad,)

def back_keep(v):
    return (v, None)

def back_low(kept, grad):
    return (low(grad),)
low.defvjp(low_keep, low_pass)
low_back.defvjp(back_keep, back_low)
epsilon = 1e-05
whiten_floor = 0.001

def masked_norm(values, weight, params, total_valid):
    centre = lax.optimization_barrier(jnp.sum(values * weight, axis=(0, 1))) / total_valid
    second = lax.optimization_barrier(jnp.sum(values * values * weight, axis=(0, 1))) / total_valid
    scale_value = lax.rsqrt(second - centre * centre + epsilon)
    return params[0] * ((values - centre) * scale_value) + params[1]

def whiten_loss(codes, pairing):
    rows_total = codes.shape[0]
    centre = lax.optimization_barrier(jnp.sum(codes, axis=0)) / rows_total
    covariance = jnp.dot(codes.T, codes, precision=lax.Precision.HIGHEST) / rows_total - jnp.outer(centre, centre)
    covariance = covariance + whiten_floor * jnp.eye(codes.shape[1], dtype=jnp.float32)
    factor = jnp.linalg.cholesky(covariance)
    whitened = lax.linalg.triangular_solve(factor, (codes - centre).T, left_side=True, lower=True).T
    unit_rows = whitened * lax.rsqrt(lax.optimization_barrier(jnp.sum(whitened * whitened, axis=1, keepdims=True)) + epsilon)
    partner_sum = jax.ops.segment_sum(unit_rows, pairing, num_segments=rows_total // 2)
    pair_gap = 2.0 * unit_rows - partner_sum[pairing]
    return jnp.sum(pair_gap * pair_gap) / rows_total

def forward(images, w_reduce, w_spatial, w_expand, w_project, w_code, norm_reduce, norm_spatial, norm_expand, norm_project, weight, counts, total_valid, pairing):
    highest = lax.Precision.HIGHEST
    masked = images * weight
    reduced = low_back(jnp.einsum('npc,cm->npm', masked, w_reduce, precision=highest))
    act_reduce = low(weight * jax.nn.silu(masked_norm(reduced, weight, norm_reduce, total_valid)))
    grid_map = act_reduce.reshape(IMAGES, SIDE, SIDE, INNER)
    spatial = lax.conv_general_dilated(grid_map, w_spatial, (1, 1), 'SAME', dimension_numbers=('NHWC', 'HWIO', 'NHWC'), precision=highest)
    spatial = low_back(spatial.reshape(IMAGES, PIXELS, INNER))
    act_spatial = low(weight * jax.nn.silu(masked_norm(spatial, weight, norm_spatial, total_valid)))
    expanded = low_back(jnp.einsum('npm,mc->npc', act_spatial, w_expand, precision=highest))
    summed = masked + masked_norm(expanded, weight, norm_expand, total_valid)
    output = weight * jax.nn.silu(summed)
    pooled = lax.optimization_barrier(jnp.sum(output, axis=1)) / counts
    projected = jnp.dot(pooled, w_project, precision=highest)
    centre = lax.optimization_barrier(jnp.mean(projected, axis=0))
    spread = lax.optimization_barrier(jnp.mean(projected * projected, axis=0)) - centre * centre
    normed = (projected - centre) * lax.rsqrt(spread + epsilon)
    hidden = jax.nn.silu(norm_project[0] * normed + norm_project[1])
    codes = jnp.dot(hidden, w_code, precision=highest)
    return whiten_loss(codes, pairing)

def reference(images, pixel_mask, pairing, w_reduce, w_spatial, w_expand, w_project, w_code, norm_reduce, norm_spatial, norm_expand, norm_project):
    weight = pixel_mask.astype(jnp.float32)[:, :, None]
    counts = lax.optimization_barrier(jnp.sum(weight, axis=1))
    total_valid = jnp.sum(weight)
    loss_scale = IMAGES / 4.0

    def scaled(image_values, reduce_values, spatial_values, expand_values, project_values, code_values, gain_reduce, gain_spatial, gain_expand, gain_project):
        return loss_scale * forward(image_values, reduce_values, spatial_values, expand_values, project_values, code_values, gain_reduce, gain_spatial, gain_expand, gain_project, weight, counts, total_valid, pairing)
    scaled_loss, pullback = jax.vjp(scaled, images.astype(jnp.float32), w_reduce.astype(jnp.float32), w_spatial.astype(jnp.float32), w_expand.astype(jnp.float32), w_project.astype(jnp.float32), w_code.astype(jnp.float32), norm_reduce, norm_spatial, norm_expand, norm_project)
    gradients = pullback(jnp.ones((), jnp.float32))
    return (scaled_loss / loss_scale, gradients[0], gradients[1], gradients[2], gradients[3], gradients[4], gradients[5], gradients[6], gradients[7], gradients[8], gradients[9])
```

```python
import functools

import jax
import jax.numpy as jnp
from jax import lax
from jax.experimental import pallas as pl
from jax.experimental.pallas import tpu as pltpu
from jax.sharding import PartitionSpec as P

MESH = pl.DeviceIdType.MESH
SIDE = 7

def place():
    dp = lax.axis_index("dp")
    sub = lax.axis_index("sub")
    z = dp // 4
    y = lax.rem(dp // 2, 2)
    x = lax.rem(dp, 2)
    ring = 3 * y + x - 2 * x * y
    return dp, sub, z, ring

def ring_dp(z, ring):
    ring = lax.rem(ring + 4, 4)
    y = ring // 2
    odd = lax.rem(ring, 2)
    x = odd + y - 2 * odd * y
    return z * 4 + y * 2 + x

def dev(dp, sub):
    return {"dp": dp, "sub": sub}

def greet_all():
    dp, sub, _, _ = place()
    me = dp * 2 + sub
    total = lax.axis_size("dp") * lax.axis_size("sub")
    barrier = pltpu.get_barrier_semaphore()
    @pl.loop(1, total)
    def _(step):
        other = lax.rem(me + step, total)
        pl.semaphore_signal(barrier, inc=1, device_id=dev(other // 2, lax.rem(other, 2)), device_id_type=MESH)
    pl.semaphore_wait(barrier, total - 1)

def remote(src, dst, send, recv, where):
    return pltpu.make_async_remote_copy(src_ref=src, dst_ref=dst, send_sem=send, recv_sem=recv, device_id=dev(*where), device_id_type=MESH)

def arrived(ref, sem):
    pltpu.make_async_copy(ref, ref, sem).wait()

def add_into(dst, src, rows):
    step = 16 if rows % 16 == 0 else 8
    @pl.loop(0, rows // step)
    def _(k):
        at = pl.ds(pl.multiple_of(k * step, 8), step)
        dst[at, :] = dst[at, :] + src[at, :]

def rows_at(ref, start, size):
    return ref.at[pl.ds(pl.multiple_of(start, 8), size)]

class Line:
    pass

SEMS = 24
def when(cond, body):
    pl.when(cond)(body)

class Job:
    def __init__(self, ring_first, rows, acc, other, out, sbuf, rbuf, send, recv, loc):
        self.__dict__.update(locals())

    def run(self):
        dp, sub, z, q = place()
        rows, acc, out, rbuf, send, recv, loc = self.rows, self.acc, self.out, self.rbuf, self.send, self.recv, self.loc
        nxt, prv = (ring_dp(z, q + 1), sub), (ring_dp(z, q + 3), sub)
        up, dn = (dp + 4, sub), (dp - 4, sub)
        sib = (dp, 1 - sub)
        pending = []
        def go(cond, src, dst, s, r, where):
            def body(): remote(src, dst, send.at[s], recv.at[r], where).start()
            if cond is None: body()
            else: when(cond, body)
            pending.append((cond, src, s))
        def got(cond, ref, r, then=None):
            def body():
                arrived(ref, recv.at[r])
                if then is not None: then()
            if cond is None: body()
            else: when(cond, body)
        go(None, self.other, self.sbuf, 0, 0, sib)
        yield
        got(None, self.sbuf, 0)
        add_into(acc, self.sbuf, rows)
        D = rows
        big = D // 4
        small = D // 16
        def ring_rs(base, block):
            half = block // 2
            r0a = rows_at(rbuf, self.off, half); r0b = rows_at(rbuf, self.off + half, half)
            r1a = rows_at(rbuf, self.off + 2 * half, block); r1b = rows_at(rbuf, self.off + 2 * half + block, block)
            self.off += 2 * half + 2 * block
            blk = lambda k, h=0, n=block: rows_at(acc, base + lax.rem(q + k, 4) * block + h, n)
            go(None, blk(2, 0, half), r0a, 1, 1, nxt)
            go(None, blk(2, half, half), r0b, 2, 2, prv)
            yield
            got(None, r0a, 1); add_into(blk(1, 0, half), r0a, half)
            go(None, blk(1), r1a, 3, 3, nxt)
            got(None, r0b, 2); add_into(blk(3, half, half), r0b, half)
            go(None, blk(3), r1b, 4, 4, prv)
            yield
            got(None, r1a, 3); add_into(blk(0), r1a, block)
            got(None, r1b, 4); add_into(blk(0), r1b, block)
        def line_rs(base, chunk):
            la = [rows_at(rbuf, self.off + k * chunk, chunk) for k in range(3)]
            ra = [rows_at(rbuf, self.off + (3 + k) * chunk, chunk) for k in range(3)]
            self.off += 6 * chunk
            at = lambda j: rows_at(acc, base + jnp.clip(j, 0, 3) * chunk, chunk)
            for t in range(3):
                go(z <= t, at(3 + z - t), la[t], 5 + t, 5 + t, up)
                go(z >= 3 - t, at(z - 3 + t), ra[t], 8 + t, 8 + t, dn)
                yield
                got(jnp.logical_and(z >= 1, z <= t + 1), la[t], 5 + t, lambda: add_into(at(2 + z - t), la[t], chunk))
                got(jnp.logical_and(z <= 2, z >= 2 - t), ra[t], 8 + t, lambda: add_into(at(z - 2 + t), ra[t], chunk))
        def line_ag(base, chunk, first):
            at = lambda j: rows_at(out, base + jnp.clip(j, 0, 3) * chunk, chunk)
            for t in range(3):
                src_r = first if t == 0 and first is not None else at(z - t)
                src_l = first if t == 0 and first is not None else at(z + t)
                go(jnp.logical_and(z <= 2, z >= t), src_r, at(z - t), 11 + t, 11 + t, up)
                go(jnp.logical_and(z >= 1, z <= 3 - t), src_l, at(z + t), 14 + t, 14 + t, dn)
                yield
                got(z >= t + 1, at(z - 1 - t), 11 + t)
                got(z <= 2 - t, at(z + 1 + t), 14 + t)
        def ring_ag(base, block, first, after):
            half = block // 2
            blk = lambda k, h=0, n=block: rows_at(out, base + lax.rem(q + k, 4) * block + h, n)
            src = first if first is not None else blk(0)
            go(None, src, blk(0), 17, 17, nxt)
            go(None, src, blk(0), 18, 18, prv)
            yield
            got(None, blk(3), 17)
            go(None, blk(3, 0, half), blk(3, 0, half), 19, 19, nxt)
            after(blk(3), 21)
            got(None, blk(1), 18)
            go(None, blk(1, half, half), blk(1, half, half), 20, 20, prv)
            after(blk(1), 22)
            yield
            got(None, blk(2, 0, half), 19)
            got(None, blk(2, half, half), 20)
            after(blk(2), 23)
        self.off = 0
        share = lambda ref, s: go(None, ref, ref, s, 21, sib)
        if self.ring_first:
            yield from ring_rs(0, big)
            yield from line_rs(q * big, small)
            mine = rows_at(acc, q * big + z * small, small)
            own = rows_at(out, q * big + z * small, small)
            pltpu.make_async_copy(mine, own, loc).start()
            yield from line_ag(q * big, small, mine)
            pltpu.make_async_copy(mine, own, loc).wait()
            share(rows_at(out, q * big, big), 24)
            yield from ring_ag(0, big, None, share)
        else:
            yield from line_rs(0, big)
            yield from ring_rs(z * big, small)
            mine = rows_at(acc, z * big + q * small, small)
            own = rows_at(out, z * big + q * small, small)
            pltpu.make_async_copy(mine, own, loc).start()
            yield from ring_ag(z * big, small, mine, lambda ref, s: None)
            pltpu.make_async_copy(mine, own, loc).wait()
            share(rows_at(out, z * big, big), 21)
            yield from line_ag(0, big, None)
            for k, s in ((1, 22), (2, 23), (3, 24)):
                share(rows_at(out, lax.rem(z + k, 4) * big, big), s)
        yield
        arrived(self.sib_out, recv.at[21])
        for cond, ref, s in pending:
            def body(ref=ref, s=s): arrived(ref, send.at[s])
            if cond is None: body()
            else: when(cond, body)

SEMS = 25

def rbuf_rows(ring_first, rows):
    big, small = rows // 4, rows // 16
    if ring_first: return big * 3 + 6 * small
    return small * 3 + 6 * big
def plan():
    return [(0, 0, 896, 0, 512, True), (0, 896, 256, 0, 512, False), (0, 1152, 896, 0, 512, True), (0, 2048, 256, 0, 512, False),
            (1, 0, 768, 0, 512, True), (1, 768, 256, 0, 512, False), (2, 0, 256, 0, 1536, True), (2, 0, 256, 1536, 512, False)]
STARTS = [0, 0, 2, 2, 4, 4, 6, 6]
def bulk_kernel(starts, *refs):
    n = 3
    g = refs[:n]; out = refs[n:2 * n]; acc = refs[2 * n:3 * n]; sbuf = refs[3 * n:4 * n]
    jobs_p = plan()
    rb = refs[4 * n:4 * n + len(jobs_p)]
    send, recv, loc, load = refs[4 * n + len(jobs_p):]
    dp, sub, z, q = place()
    half = [r.shape[0] // 2 for r in g]
    for k in range(n):
        pltpu.make_async_copy(g[k].at[pl.ds(pl.multiple_of(sub * half[k], 8), half[k])], acc[k], load.at[k]).start()
    greet_all()
    for k in range(n):
        pltpu.make_async_copy(g[k].at[pl.ds(pl.multiple_of(sub * half[k], 8), half[k])], acc[k], load.at[k]).wait()
    gens = []
    for j, (k, r0, rows, c0, cols, rf) in enumerate(jobs_p):
        cut = lambda ref, base: ref.at[pl.ds(pl.multiple_of(base + r0, 8), rows), pl.ds(c0, cols)]
        job = Job(rf, rows, cut(acc[k], 0), cut(g[k], (1 - sub) * half[k]), cut(out[k], sub * half[k]), cut(sbuf[k], 0), rb[j], send.at[j], recv.at[j], loc.at[j])
        job.sib_out = cut(out[k], (1 - sub) * half[k])
        gens.append(job.run())
    tick = 0
    live = dict(enumerate(gens))
    while live:
        for j in sorted(live):
            if tick >= starts[j]:
                try: next(live[j])
                except StopIteration: live.pop(j)
        tick += 1

def bulk(gs, starts=STARTS, cid=3):
    jobs_p = plan()
    n = 3
    shapes = [x.shape for x in gs]
    scratch = [pltpu.VMEM((s[0] // 2, s[1]), jnp.float32) for s in shapes] * 2
    scratch += [pltpu.VMEM((rbuf_rows(rf, rows), cols), jnp.float32) for (k, r0, rows, c0, cols, rf) in jobs_p]
    scratch += [pltpu.SemaphoreType.DMA((len(jobs_p), SEMS)), pltpu.SemaphoreType.DMA((len(jobs_p), SEMS)), pltpu.SemaphoreType.DMA((len(jobs_p),)), pltpu.SemaphoreType.DMA((n,))]
    return pl.pallas_call(functools.partial(bulk_kernel, starts),
        out_shape=[jax.ShapeDtypeStruct(s, jnp.float32) for s in shapes],
        in_specs=[pl.BlockSpec(memory_space=pl.ANY)] * n, out_specs=[pl.BlockSpec(memory_space=pl.ANY)] * n,
        scratch_shapes=scratch,
        compiler_params=pltpu.CompilerParams(collective_id=cid, has_side_effects=True, vmem_limit_bytes=56 << 20))(*gs)


def sums_kernel(x_ref, o_ref, buf, send, recv):
    dp, sub, _, _ = place()
    me = dp * 2 + sub
    greet_all()
    buf[me] = x_ref[...]
    @pl.loop(1, 32)
    def _(step):
        other = lax.rem(me + step, 32)
        remote(buf.at[me], buf.at[me], send, recv, (other // 2, lax.rem(other, 2))).start()
    many = buf.at[pl.ds(0, 31)]
    arrived(many, recv)
    o_ref[...] = jnp.sum(buf[...], axis=0)
    arrived(many, send)


def sums(parts, ident):
    if lax.axis_size("dp") != 16 or lax.axis_size("sub") != 2:
        return lax.psum(parts, ("dp", "sub"))
    flat = jnp.concatenate([part.reshape(-1) for part in parts])
    rows = -(-flat.shape[0] // 1024) * 8
    flat = jnp.pad(flat, (0, rows * 128 - flat.shape[0])).reshape(rows, 128)
    total = pl.pallas_call(
        sums_kernel,
        out_shape=jax.ShapeDtypeStruct((rows, 128), jnp.float32),
        in_specs=[pl.BlockSpec(memory_space=pltpu.VMEM)],
        out_specs=pl.BlockSpec(memory_space=pltpu.VMEM),
        scratch_shapes=[pltpu.VMEM((32, rows, 128), jnp.float32), pltpu.SemaphoreType.DMA, pltpu.SemaphoreType.DMA],
        compiler_params=pltpu.CompilerParams(collective_id=ident, has_side_effects=True),
    )(flat).reshape(-1)
    results = []
    offset = 0
    for part in parts:
        results.append(total[offset : offset + part.size].reshape(part.shape))
        offset += part.size
    return results


def weight_sums(spatial, reduce, expand):
    if lax.axis_size("dp") != 16 or lax.axis_size("sub") != 2:
        return lax.psum((spatial, reduce, expand), ("dp", "sub"))
    return bulk((spatial, reduce, expand))


def whiten(codes, pairing):
    highest = lax.Precision.HIGHEST
    total = codes.shape[0]
    centre = jnp.sum(codes, axis=0) / total
    moved = codes - centre
    covariance = jnp.dot(moved.T, moved, precision=highest) / total
    covariance = covariance + whiten_floor * jnp.eye(codes.shape[1], dtype=jnp.float32)
    factor = jnp.linalg.cholesky(covariance)
    inverse = lax.linalg.triangular_solve(factor, jnp.eye(codes.shape[1], dtype=jnp.float32), left_side=True, lower=True)
    white = jnp.dot(moved, inverse.T, precision=highest)
    scale = lax.rsqrt(jnp.sum(white * white, axis=1, keepdims=True) + epsilon)
    unit = white * scale
    same = (pairing[:, None] == pairing[None, :]).astype(jnp.float32)
    gap = 2.0 * unit - jnp.dot(same, unit, precision=highest)
    loss_value = jnp.sum(gap * gap) / total
    grad_unit = 0.5 * (2.0 * gap - jnp.dot(same, gap, precision=highest))
    grad_white = scale * grad_unit - white * scale * scale * scale * jnp.sum(white * grad_unit, axis=1, keepdims=True)
    gram = jnp.dot(grad_white.T, white, precision=highest)
    row = lax.broadcasted_iota(jnp.int32, gram.shape, 0)
    column = lax.broadcasted_iota(jnp.int32, gram.shape, 1)
    lower = jnp.where(row > column, gram, jnp.where(row == column, 0.5 * gram, 0.0))
    both = lower + lower.T
    grad_moved = jnp.dot(grad_white - jnp.dot(white, both, precision=highest) / total, inverse, precision=highest)
    return loss_value, grad_moved - jnp.sum(grad_moved, axis=0) / total


epsilon = 1e-05
whiten_floor = 0.001


def silu_slope(values):
    sigmoid_value = jax.nn.sigmoid(values)
    return sigmoid_value * (1.0 + values * (1.0 - sigmoid_value))


def moments(sum_value, sum_square, total_count):
    centre = sum_value / total_count
    return (centre, lax.rsqrt(sum_square / total_count - centre * centre + epsilon))


def make_columns(activation):
    images_here, pixel_count, inner_width = activation.shape
    grid_map = activation.reshape(images_here, SIDE, SIDE, inner_width)
    padded = jnp.pad(grid_map, ((0, 0), (1, 1), (1, 1), (0, 0)))
    pieces = [
        padded[:, tap_row : tap_row + SIDE, tap_col : tap_col + SIDE, :]
        for tap_row in range(3)
        for tap_col in range(3)
    ]
    return jnp.concatenate(pieces, axis=3).reshape(images_here * pixel_count, 9 * inner_width)


def fold_columns(columns, images_here, inner_width):
    tap_grads = columns.reshape(images_here, SIDE, SIDE, 9, inner_width)
    padded = jnp.zeros((images_here, SIDE + 2, SIDE + 2, inner_width), jnp.float32)
    for tap_row in range(3):
        for tap_col in range(3):
            padded = padded.at[:, tap_row : tap_row + SIDE, tap_col : tap_col + SIDE, :].add(
                tap_grads[:, :, :, 3 * tap_row + tap_col, :]
            )
    return padded[:, 1 : SIDE + 1, 1 : SIDE + 1, :].reshape(images_here, SIDE * SIDE, inner_width)


def pixel_sums(values, weight):
    return (jnp.sum(values * weight, axis=(0, 1)), jnp.sum(values * values * weight, axis=(0, 1)))


def front(
    masked_low,
    weight,
    counts,
    w_reduce,
    w_spatial,
    w_expand,
    norm_reduce,
    norm_spatial,
    norm_expand,
):
    images_here, pixel_count, width = masked_low.shape
    inner_width = w_reduce.shape[1]
    rows_here = images_here * pixel_count
    reduced = jnp.dot(
        masked_low.reshape(rows_here, width), w_reduce, preferred_element_type=jnp.float32
    ).reshape(images_here, pixel_count, inner_width)
    sum_reduce, square_reduce = pixel_sums(reduced, weight)
    sum_reduce, square_reduce, valid_total = sums((sum_reduce, square_reduce, jnp.sum(counts)), 10)
    centre_reduce, scale_reduce = moments(sum_reduce, square_reduce, valid_total)
    normed_reduce = (reduced - centre_reduce) * scale_reduce
    level_reduce = norm_reduce[0] * normed_reduce + norm_reduce[1]
    act_reduce = (weight * jax.nn.silu(level_reduce)).astype(jnp.bfloat16)
    columns = make_columns(act_reduce)
    spatial = jnp.dot(
        columns, w_spatial.reshape(9 * inner_width, inner_width), preferred_element_type=jnp.float32
    ).reshape(images_here, pixel_count, inner_width)
    sum_spatial, square_spatial = pixel_sums(spatial, weight)
    sum_spatial, square_spatial = sums((sum_spatial, square_spatial), 11)
    centre_spatial, scale_spatial = moments(sum_spatial, square_spatial, valid_total)
    normed_spatial = (spatial - centre_spatial) * scale_spatial
    level_spatial = norm_spatial[0] * normed_spatial + norm_spatial[1]
    act_spatial = (weight * jax.nn.silu(level_spatial)).astype(jnp.bfloat16)
    expanded = jnp.dot(
        act_spatial.reshape(rows_here, inner_width), w_expand, preferred_element_type=jnp.float32
    ).reshape(images_here, pixel_count, width)
    sum_expand, square_expand = pixel_sums(expanded, weight)
    sum_expand, square_expand = sums((sum_expand, square_expand), 12)
    centre_expand, scale_expand = moments(sum_expand, square_expand, valid_total)
    normed_expand = (expanded - centre_expand) * scale_expand
    summed = masked_low.astype(jnp.float32) + norm_expand[0] * normed_expand + norm_expand[1]
    stats = (
        valid_total,
        centre_reduce,
        scale_reduce,
        centre_spatial,
        scale_spatial,
        centre_expand,
        scale_expand,
    )
    return (
        (
            normed_reduce,
            level_reduce,
            columns,
            normed_spatial,
            level_spatial,
            act_spatial,
            normed_expand,
            summed,
        ),
        stats,
    )


def norm_back(upstream, normed, gain, scale_value, sum_grad, dot_grad, total_count):
    return gain * scale_value * (upstream - (sum_grad + normed * dot_grad) / total_count)


def shards(
    images,
    pixel_mask,
    pairing,
    w_reduce,
    w_spatial,
    w_expand,
    w_project,
    w_code,
    norm_reduce,
    norm_spatial,
    norm_expand,
    norm_project,
):
    images_here, pixel_count, width = images.shape
    inner_width = w_reduce.shape[1]
    images_total = pairing.shape[0]
    rows_here = images_here * pixel_count
    highest = lax.Precision.HIGHEST
    weight = pixel_mask.astype(jnp.float32)[:, :, None]
    counts = jnp.sum(weight, axis=1)
    masked_low = images * weight.astype(jnp.bfloat16)
    project_full = w_project.astype(jnp.float32)
    code_full = w_code.astype(jnp.float32)
    saved, stats = front(
        masked_low,
        weight,
        counts,
        w_reduce,
        w_spatial,
        w_expand,
        norm_reduce,
        norm_spatial,
        norm_expand,
    )
    (
        normed_reduce,
        level_reduce,
        columns,
        normed_spatial,
        level_spatial,
        act_spatial,
        normed_expand,
        summed,
    ) = saved
    (
        valid_total,
        centre_reduce,
        scale_reduce,
        centre_spatial,
        scale_spatial,
        centre_expand,
        scale_expand,
    ) = stats
    output = weight * jax.nn.silu(summed)
    own_pooled = jnp.sum(output, axis=1) / counts
    pooled = lax.all_gather(own_pooled, ("dp", "sub"), axis=0, tiled=True)
    projected = jnp.dot(pooled, project_full, precision=highest)
    centre_project, scale_project = moments(
        jnp.sum(projected, axis=0), jnp.sum(projected * projected, axis=0), float(images_total)
    )
    normed_project = (projected - centre_project) * scale_project
    level_project = norm_project[0] * normed_project + norm_project[1]
    hidden = jax.nn.silu(level_project)
    codes = jnp.dot(hidden, code_full, precision=highest)
    loss_value, grad_codes = whiten(codes, pairing)
    grad_w_code = jnp.dot(hidden.T, grad_codes, precision=highest)
    grad_hidden = jnp.dot(grad_codes, code_full.T, precision=highest)
    grad_level_project = grad_hidden * silu_slope(level_project)
    sum_project_grad = jnp.sum(grad_level_project, axis=0)
    dot_project_grad = jnp.sum(grad_level_project * normed_project, axis=0)
    grad_norm_project = jnp.stack([dot_project_grad, sum_project_grad])
    grad_projected = norm_back(
        grad_level_project,
        normed_project,
        norm_project[0],
        scale_project,
        sum_project_grad,
        dot_project_grad,
        float(images_total),
    )
    grad_w_project = jnp.dot(pooled.T, grad_projected, precision=highest)
    own_start = lax.axis_index(("dp", "sub")) * images_here
    own_projected = lax.dynamic_slice_in_dim(grad_projected, own_start, images_here, 0)
    grad_pooled = jnp.dot(own_projected, project_full.T, precision=highest)
    grad_summed = weight * (grad_pooled / counts)[:, None, :] * silu_slope(summed)
    sum_expand_grad, dot_expand_grad = sums(
        (jnp.sum(grad_summed, axis=(0, 1)), jnp.sum(grad_summed * normed_expand, axis=(0, 1))), 13
    )
    grad_norm_expand = jnp.stack([dot_expand_grad, sum_expand_grad])
    grad_expanded = (
        (
            weight
            * norm_back(
                grad_summed,
                normed_expand,
                norm_expand[0],
                scale_expand,
                sum_expand_grad,
                dot_expand_grad,
                valid_total,
            )
        )
        .astype(jnp.bfloat16)
        .reshape(rows_here, width)
    )
    grad_w_expand = jnp.einsum(
        "rm,rc->mc",
        act_spatial.reshape(rows_here, inner_width),
        grad_expanded,
        preferred_element_type=jnp.float32,
    )
    grad_act_spatial = jnp.einsum(
        "rc,mc->rm", grad_expanded, w_expand, preferred_element_type=jnp.float32
    ).reshape(images_here, pixel_count, inner_width)
    grad_level_spatial = grad_act_spatial * weight * silu_slope(level_spatial)
    sum_spatial_grad, dot_spatial_grad = sums(
        (
            jnp.sum(grad_level_spatial, axis=(0, 1)),
            jnp.sum(grad_level_spatial * normed_spatial, axis=(0, 1)),
        ),
        14,
    )
    grad_norm_spatial = jnp.stack([dot_spatial_grad, sum_spatial_grad])
    grad_spatial_out = (
        (
            weight
            * norm_back(
                grad_level_spatial,
                normed_spatial,
                norm_spatial[0],
                scale_spatial,
                sum_spatial_grad,
                dot_spatial_grad,
                valid_total,
            )
        )
        .astype(jnp.bfloat16)
        .reshape(rows_here, inner_width)
    )
    grad_w_spatial = jnp.einsum(
        "rk,rm->km", columns, grad_spatial_out, preferred_element_type=jnp.float32
    ).reshape(3, 3, inner_width, inner_width)
    grad_columns = jnp.einsum(
        "rm,km->rk",
        grad_spatial_out,
        w_spatial.reshape(9 * inner_width, inner_width),
        preferred_element_type=jnp.float32,
    )
    grad_act_reduce = fold_columns(grad_columns, images_here, inner_width)
    grad_level_reduce = grad_act_reduce * weight * silu_slope(level_reduce)
    sum_reduce_grad, dot_reduce_grad = sums(
        (
            jnp.sum(grad_level_reduce, axis=(0, 1)),
            jnp.sum(grad_level_reduce * normed_reduce, axis=(0, 1)),
        ),
        15,
    )
    grad_norm_reduce = jnp.stack([dot_reduce_grad, sum_reduce_grad])
    grad_reduced = (
        (
            weight
            * norm_back(
                grad_level_reduce,
                normed_reduce,
                norm_reduce[0],
                scale_reduce,
                sum_reduce_grad,
                dot_reduce_grad,
                valid_total,
            )
        )
        .astype(jnp.bfloat16)
        .reshape(rows_here, inner_width)
    )
    grad_w_reduce = jnp.einsum(
        "rc,rm->cm",
        masked_low.reshape(rows_here, width),
        grad_reduced,
        preferred_element_type=jnp.float32,
    )
    grad_input = jnp.einsum(
        "rm,cm->rc", grad_reduced, w_reduce, preferred_element_type=jnp.float32
    ).reshape(images_here, pixel_count, width)
    grad_images = weight * (grad_summed + grad_input)
    grad_w_spatial, grad_w_reduce, grad_w_expand = weight_sums(
        grad_w_spatial.reshape(9 * inner_width, inner_width), grad_w_reduce, grad_w_expand
    )
    return (
        loss_value,
        grad_images,
        grad_w_reduce,
        grad_w_spatial.reshape(3, 3, inner_width, inner_width),
        grad_w_expand,
        grad_w_project,
        grad_w_code,
        grad_norm_reduce,
        grad_norm_spatial,
        grad_norm_expand,
        grad_norm_project,
    )


def solution(mesh):
    placed = (
        P(("dp", "sub"), None, None),
        P(("dp", "sub"), None),
        P(),
        P(),
        P(),
        P(),
        P(),
        P(),
        P(),
        P(),
        P(),
        P(),
    )
    return jax.shard_map(
        shards,
        mesh=mesh,
        in_specs=placed,
        out_specs=(P(), P(("dp", "sub"), None, None), P(), P(), P(), P(), P(), P(), P(), P(), P()),
        check_vma=False,
    )
```

```python
import jax
import jax.numpy as jnp
from jax import lax
from jax.experimental import pallas as pl
from jax.experimental.pallas import tpu as pltpu
from jax.sharding import PartitionSpec as P

MESH = pl.DeviceIdType.MESH
SIDE = 7
SLOTS = 56
ROWS = 448
epsilon = 1e-05
whiten_floor = 0.001
f32 = jnp.float32
bf16 = jnp.bfloat16


def place():
    dp = lax.axis_index("dp")
    sub = lax.axis_index("sub")
    z = dp // 4
    y = lax.rem(dp // 2, 2)
    x = lax.rem(dp, 2)
    ring = 3 * y + x - 2 * x * y
    return dp, sub, z, ring


def plane_of(ring):
    ring = lax.rem(ring + 4, 4)
    y = ring // 2
    odd = lax.rem(ring, 2)
    return y * 2 + odd + y - 2 * odd * y


def ring_dp(z, ring):
    return z * 4 + plane_of(ring)


def dev(dp, sub):
    return {"dp": dp, "sub": sub}


def greet_start():
    dp, sub, _, _ = place()
    me = dp * 2 + sub
    barrier = pltpu.get_barrier_semaphore()

    @pl.loop(1, 32)
    def _(step):
        other = lax.rem(me + step, 32)
        pl.semaphore_signal(
            barrier, inc=1, device_id=dev(other // 2, lax.rem(other, 2)), device_id_type=MESH
        )


def greet_wait():
    pl.semaphore_wait(pltpu.get_barrier_semaphore(), 31)


def remote(src, dst, send, recv, where):
    return pltpu.make_async_remote_copy(
        src_ref=src,
        dst_ref=dst,
        send_sem=send,
        recv_sem=recv,
        device_id=dev(*where),
        device_id_type=MESH,
    )


def arrived(ref, sem):
    pltpu.make_async_copy(ref, ref, sem).wait()


def direct_start(buf, send, recv):
    dp, sub, _, _ = place()
    me = dp * 2 + sub

    @pl.loop(1, 32)
    def _(step):
        other = lax.rem(me + step, 32)
        remote(buf.at[me], buf.at[me], send, recv, (other // 2, lax.rem(other, 2))).start()


def direct_finish(buf, send, recv):
    many = buf.at[pl.ds(0, 31)]
    arrived(many, recv)
    total = jnp.sum(buf[...], axis=0)
    arrived(many, send)
    return total


def tree_sums(value, pair, plane, line, send, recv, base=3):
    dp, sub, z, _ = place()
    w = lax.rem(dp, 4)
    if value is not None:
        pair[sub] = value
    remote(pair.at[sub], pair.at[sub], send.at[base + 0], recv.at[base + 0], (dp, 1 - sub)).start()
    arrived(pair.at[0], recv.at[base + 0])
    plane[w] = pair[0] + pair[1]
    for k in range(1, 4):
        remote(
            plane.at[w], plane.at[w], send.at[base + 1], recv.at[base + 1], (z * 4 + lax.rem(w + k, 4), sub)
        ).start()
    arrived(plane.at[pl.ds(0, 3)], recv.at[base + 1])
    line[z] = (plane[0] + plane[1]) + (plane[2] + plane[3])
    for k in range(1, 4):
        remote(
            line.at[z], line.at[z], send.at[base + 2], recv.at[base + 2], (lax.rem(z + k, 4) * 4 + w, sub)
        ).start()
    arrived(line.at[pl.ds(0, 3)], recv.at[base + 2])
    total = (line[0] + line[1]) + (line[2] + line[3])
    arrived(pair.at[0], send.at[base + 0])
    arrived(plane.at[pl.ds(0, 3)], send.at[base + 1])
    arrived(line.at[pl.ds(0, 3)], send.at[base + 2])
    return total


class Mover:
    def __init__(self, send, recv):
        self.send, self.recv, self.pending = send, recv, []

    def go(self, cond, src, dst, s, r, where):
        def body():
            remote(src, dst, self.send.at[s], self.recv.at[r], where).start()

        if cond is None:
            body()
        else:
            pl.when(cond)(body)
        self.pending.append((cond, src, s))

    def got(self, cond, ref, r, then=None):
        def body():
            arrived(ref, self.recv.at[r])
            if then is not None:
                then()

        if cond is None:
            body()
        else:
            pl.when(cond)(body)

    def drain(self):
        for cond, ref, s in self.pending:

            def body(ref=ref, s=s):
                arrived(ref, self.send.at[s])

            if cond is None:
                body()
            else:
                pl.when(cond)(body)
        self.pending = []

    def line_gather(self, at, first, base):
        dp, sub, z, _ = place()
        up, down = (dp + 4, sub), (dp - 4, sub)
        hold = lambda j: at(jnp.clip(j, 0, 3))
        for t in range(3):
            from_up = first if t == 0 and first is not None else hold(z - t)
            from_down = first if t == 0 and first is not None else hold(z + t)
            self.go(jnp.logical_and(z <= 2, z >= t), from_up, hold(z - t), base + t, base + t, up)
            self.go(
                jnp.logical_and(z >= 1, z <= 3 - t),
                from_down,
                hold(z + t),
                base + 3 + t,
                base + 3 + t,
                down,
            )
            yield
            self.got(z >= t + 1, hold(z - 1 - t), base + t)
            self.got(z <= 2 - t, hold(z + 1 + t), base + 3 + t)

    def ring_gather(self, blk, first, base, after):
        dp, sub, z, q = place()
        after_me, before_me = (ring_dp(z, q + 1), sub), (ring_dp(z, q + 3), sub)
        src = first if first is not None else blk(0, None)
        self.go(None, src, blk(0, None), base, base, after_me)
        self.go(None, src, blk(0, None), base + 1, base + 1, before_me)
        yield
        self.got(None, blk(3, None), base)
        self.go(None, blk(3, 0), blk(3, 0), base + 2, base + 2, after_me)
        after(blk(3, None), 0)
        self.got(None, blk(1, None), base + 1)
        self.go(None, blk(1, 1), blk(1, 1), base + 3, base + 3, before_me)
        after(blk(1, None), 1)
        yield
        self.got(None, blk(2, 0), base + 2)
        self.got(None, blk(2, 1), base + 3)
        after(blk(2, None), 2)


def run_all(gens, starts=None):
    live = dict(enumerate(gens))
    tick = 0
    while live:
        for j in sorted(live):
            if starts is None or tick >= starts[j]:
                try:
                    next(live[j])
                except StopIteration:
                    live.pop(j)
        tick += 1


def gather_pooled(own, out, send, recv, split):
    dp, sub, z, q = place()
    width = out.shape[-1]
    sib = (dp, 1 - sub)

    def first_line():
        cols = pl.ds(0, split)
        mover = Mover(send.at[0], recv.at[0])
        at = lambda j: out.at[j, plane_of(q), sub, :, cols]

        def blk(k, h):
            ring = plane_of(q + k)
            if h is None:
                return out.at[:, ring, sub, :, cols]
            return out.at[pl.ds(2 * h, 2), ring, sub, :, cols]

        def share(ref, s):
            mover.go(None, ref, ref, 10 + s, 10, sib)

        yield from mover.line_gather(at, own.at[:, cols], 0)
        share(blk(0, None), 3)
        yield from mover.ring_gather(blk, None, 6, share)
        yield
        arrived(out.at[:, :, 1 - sub, :, cols], recv.at[0, 10])
        mover.drain()

    def first_ring():
        cols = pl.ds(split, width - split)
        mid = (width - split) // 2
        mover = Mover(send.at[1], recv.at[1])

        def blk(k, h):
            ring = plane_of(q + k)
            if h is None:
                return out.at[z, ring, sub, :, cols]
            return out.at[z, ring, sub, :, pl.ds(split + h * mid, mid)]

        at = lambda j: out.at[j, :, sub, :, cols]

        def share(ref, s):
            mover.go(None, ref, ref, 10 + s, 10, sib)

        yield from mover.ring_gather(blk, own.at[:, cols], 0, lambda ref, s: None)
        share(at(z), 3)
        yield from mover.line_gather(at, None, 4)
        for k in range(1, 4):
            share(at(lax.rem(z + k, 4)), k - 1)
        yield
        arrived(out.at[:, :, 1 - sub, :, cols], recv.at[1, 10])
        mover.drain()

    return [first_line(), first_ring()]


def mm(a, b):
    return jnp.dot(a, b, preferred_element_type=f32)


def mm_nt(a, b):
    return lax.dot_general(a, b, (((1,), (1,)), ((), ())), preferred_element_type=f32)


def mm_tn(a, b):
    return lax.dot_general(a, b, (((0,), (0,)), ((), ())), preferred_element_type=f32)


def sigmoid(v):
    return 0.5 + 0.5 * jnp.tanh(0.5 * v)


def split(v):
    high = v.astype(bf16)
    return high, (v - high.astype(f32)).astype(bf16)


def exact(a, b, dims):
    return lax.dot_general(
        a, b, (dims, ((), ())), precision=lax.Precision.HIGHEST, preferred_element_type=f32
    )


def factor_inverse(cov, block=8):
    size = cov.shape[0]
    tiles = size // 8
    row = lax.broadcasted_iota(jnp.int32, (8, size), 0)
    column = lax.broadcasted_iota(jnp.int32, (8, size), 1)
    left = [cov[8 * t : 8 * t + 8, :] for t in range(tiles)]
    right = [jnp.where(row + 8 * t == column, 1.0, 0.0) for t in range(tiles)]
    wide = lambda v: jnp.broadcast_to(v, (8, size))
    for j in range(0, size, block):
        t0, s = j // 8, j % 8
        columns = [[wide(left[t][:, j + k : j + k + 1]) for k in range(block)] for t in range(t0, tiles)]
        lefts = [wide(left[t0][s + k : s + k + 1, :]) for k in range(block)]
        rights = [wide(right[t0][s + k : s + k + 1, :]) for k in range(block)]
        entry = [[wide(columns[0][k][s + m : s + m + 1, :]) for k in range(m + 1)] for m in range(block)]
        lower = [[None] * block for _ in range(block)]
        inverses = []
        for k in range(block):
            inverse = 1.0 / entry[k][k]
            inverses.append(inverse)
            for m in range(k + 1, block):
                lower[m][k] = entry[m][k] * inverse
            for m in range(k + 1, block):
                for n in range(k + 1, m + 1):
                    entry[m][n] = entry[m][n] - lower[m][k] * entry[n][k]
        for m in range(block):
            for k in range(m):
                lefts[m] = lefts[m] - lower[m][k] * lefts[k]
                rights[m] = rights[m] - lower[m][k] * rights[k]
        scaled_left = [a * b for a, b in zip(lefts, inverses)]
        scaled_right = [a * b for a, b in zip(rights, inverses)]
        for t in range(t0, tiles):
            if t == t0 and s + block == 8 and block == 1:
                continue
            own = columns[t - t0]
            for m in range(block):
                for k in range(m):
                    own[m] = own[m] - lower[m][k] * own[k]
            for m in range(block):
                factor = own[m]
                if t == t0:
                    factor = jnp.where(row > s + m, factor, 0.0)
                left[t] = left[t] - factor * scaled_left[m]
                right[t] = right[t] - factor * scaled_right[m]
    out = []
    for t in range(tiles):
        pivots = jnp.sum(jnp.where(row + 8 * t == column, left[t], 0.0), axis=1, keepdims=True)
        out.append(right[t] * lax.rsqrt(pivots))
    return jnp.concatenate(out, axis=0)


def fold8(v):
    rows, cols = v.shape
    return jnp.sum(v.reshape(rows // 8, 8, cols), axis=0)


def columns_of(mask, cols):
    return jnp.concatenate([mask] * (cols // 128), axis=1)


def fwd_kernel(
    images, pixel_mask, pair_column, pair_row, w_reduce, w_spatial, w_expand, w_project, w_code,
    norm_reduce, norm_spatial, norm_expand, norm_project,
    pooled_out, hidden_out, dprojected_out, dcodes_out, loss_out, grad_norm_out, upstream,
    masked_out, reduced_out, act1_out, spatial_out, act2_out, normed_out, slope_out, mask, stats, sums_out,
    img, masked, wr, ws, we, wp, wc, reduced, wide, shifted, spatial, act2, normed, slope, own,
    pooled_all, pool_high, pool_low, level, normal, hidden, dproj, counts,
    counts_buf, buf1, buf2, pair, plane, line,
    load, save, send, recv, gsend, grecv,
):
    dp, sub, z, q = place()
    me = dp * 2 + sub
    inner = wr.shape[1]
    width = wr.shape[0]
    loads = [pltpu.make_async_copy(a, b, load.at[k]) for k, (a, b) in enumerate(
        [(images, img), (w_reduce, wr), (w_spatial, ws), (w_expand, we), (w_project, wp), (w_code, wc)])]
    for copy in loads:
        copy.start()
    greet_start()
    here = pixel_mask[...].astype(f32)
    counts[...] = jnp.broadcast_to(jnp.sum(here, axis=1, keepdims=True), (8, 128))
    for slot in range(SLOTS):
        r, c = slot // 8, slot % 8
        if c == SIDE:
            value = jnp.zeros((8, 128), f32)
        else:
            value = jnp.broadcast_to(here[:, SIDE * r + c : SIDE * r + c + 1], (8, 128))
        mask[pl.ds(8 * slot, 8), :] = value
    wide[pl.ds(0, 8), :] = jnp.zeros((8, inner), f32)
    wide[pl.ds(ROWS + 8, 8), :] = jnp.zeros((8, inner), f32)
    for b in range(3):
        shifted[b, pl.ds(0, 64), :] = jnp.zeros((64, inner), bf16)
        shifted[b, pl.ds(512, 64), :] = jnp.zeros((64, inner), bf16)
    greet_wait()
    counts_buf[me] = counts[...]
    direct_start(counts_buf, send.at[0], recv.at[0])
    loads[0].wait()
    gap = jnp.zeros((8, 256), f32)

    @pl.loop(0, width // 256)
    def _(n):
        cols = pl.ds(pl.multiple_of(n * 256, 256), 256)
        for r in range(SIDE):
            rows = img[pl.ds(SIDE * r, SIDE), :, cols].astype(f32).reshape(SIDE * 8, 256)
            rows = rows * columns_of(mask[pl.ds(64 * r, 56), :], 256)
            masked[pl.ds(64 * r, 64), cols] = jnp.concatenate([rows, gap], axis=0).astype(bf16)

    saves = []

    def keep(a, b):
        copy = pltpu.make_async_copy(a, b, save.at[len(saves)])
        copy.start()
        saves.append(copy)

    keep(masked, masked_out)
    loads[1].wait()

    @pl.loop(0, inner // 256)
    def _(n):
        cols = pl.ds(pl.multiple_of(n * 256, 256), 256)
        got = mm(masked[...], wr[:, cols])
        reduced[:, cols] = got
        buf1[me, pl.ds(0, 1), cols] = jnp.sum(got, axis=0, keepdims=True)
        buf1[me, pl.ds(1, 1), cols] = jnp.sum(got * got, axis=0, keepdims=True)

    direct_start(buf1, send.at[1], recv.at[1])
    keep(reduced, reduced_out)
    valid = jnp.sum(direct_finish(counts_buf, send.at[0], recv.at[0]), axis=0, keepdims=True)[:, 0:1]
    inverse_valid = 1.0 / valid

    def moments(total):
        centre = total[0:1] * inverse_valid
        return centre, lax.rsqrt(total[1:2] * inverse_valid - centre * centre + epsilon)

    def activate(src, norm, centre, scale, store):
        gain = norm[0:1, :] * scale
        bias = norm[1:2, :] - centre * gain

        @pl.loop(0, ROWS // 32)
        def _(k):
            rows = pl.ds(pl.multiple_of(k * 32, 32), 32)
            level = src[rows, :] * gain + bias
            store(k, columns_of(mask[rows, :], inner) * (level * sigmoid(level)))

    centre1, scale1 = moments(direct_finish(buf1, send.at[1], recv.at[1]))
    stats[pl.ds(0, 1), pl.ds(0, inner)] = centre1
    stats[pl.ds(1, 1), pl.ds(0, inner)] = scale1

    def store_wide(k, value):
        wide[pl.ds(pl.multiple_of(k * 32 + 8, 8), 32), :] = value
        shifted[1, pl.ds(pl.multiple_of(k * 32 + 64, 32), 32), :] = value.astype(bf16)

    activate(reduced, norm_reduce, centre1, scale1, store_wide)

    @pl.loop(0, ROWS // 32)
    def _(k):
        for b in (0, 2):
            rows = wide[pl.ds(pl.multiple_of(k * 32 + 8 * b, 8), 32), :]
            shifted[b, pl.ds(pl.multiple_of(k * 32 + 64, 32), 32), :] = rows.astype(bf16)

    keep(shifted.at[1, pl.ds(64, ROWS)], act1_out)
    loads[2].wait()

    @pl.loop(0, inner // 256)
    def _(n):
        cols = pl.ds(pl.multiple_of(n * 256, 256), 256)

        def taps(a, total):
            for b in range(3):
                left = shifted[b, pl.ds(pl.multiple_of(a * 64, 64), ROWS), :]
                right = ws[pl.ds(pl.multiple_of((a * 3 + b) * inner, inner), inner), cols]
                total = total + mm(left, right)
            return total

        spatial[:, cols] = taps(0, jnp.zeros((ROWS, 256), f32))
        spatial[:, cols] = taps(1, spatial[:, cols])
        got = taps(2, spatial[:, cols]) * columns_of(mask[...], 256)
        spatial[:, cols] = got
        buf2[me, pl.ds(0, 1), cols] = jnp.sum(got, axis=0, keepdims=True)
        buf2[me, pl.ds(1, 1), cols] = jnp.sum(got * got, axis=0, keepdims=True)

    direct_start(buf2, send.at[2], recv.at[2])
    keep(spatial, spatial_out)
    centre2, scale2 = moments(direct_finish(buf2, send.at[2], recv.at[2]))
    stats[pl.ds(2, 1), pl.ds(0, inner)] = centre2
    stats[pl.ds(3, 1), pl.ds(0, inner)] = scale2

    def store_act2(k, value):
        act2[pl.ds(pl.multiple_of(k * 32, 32), 32), :] = value.astype(bf16)

    activate(spatial, norm_spatial, centre2, scale2, store_act2)
    keep(act2, act2_out)
    loads[3].wait()

    @pl.loop(0, width // 256)
    def _(n):
        cols = pl.ds(pl.multiple_of(n * 256, 256), 256)
        got = mm(act2[...], we[:, cols])
        normed[:, cols] = got
        pair[sub, pl.ds(0, 1), cols] = jnp.sum(got, axis=0, keepdims=True)
        pair[sub, pl.ds(1, 1), cols] = jnp.sum(got * got, axis=0, keepdims=True)

    centre3, scale3 = moments(tree_sums(None, pair, plane, line, send, recv))
    stats[pl.ds(4, 1), :] = centre3
    stats[pl.ds(5, 1), :] = scale3
    stats[pl.ds(6, 1), :] = jnp.broadcast_to(valid, (1, width))
    stats[pl.ds(7, 1), :] = jnp.zeros((1, width), f32)
    inverse_counts = 1.0 / counts[...]

    @pl.loop(0, width // 256)
    def _(n):
        cols = pl.ds(pl.multiple_of(n * 256, 256), 256)
        centre, scale = stats[pl.ds(4, 1), cols], stats[pl.ds(5, 1), cols]
        gain, bias = norm_expand[pl.ds(0, 1), cols], norm_expand[pl.ds(1, 1), cols]

        def block(k, carry):
            pool, s1, s2 = carry
            rows = pl.ds(pl.multiple_of(k * 64, 64), 64)
            here = columns_of(mask[rows, :], 256)
            n3 = (normed[rows, cols] - centre) * scale
            total = masked[rows, cols].astype(f32) + gain * n3 + bias
            sig = sigmoid(total)
            out = total * sig
            slope3 = here * (sig + out * (1.0 - sig))
            normed[rows, cols] = n3
            slope[rows, cols] = slope3
            return pool + fold8(here * out), s1 + fold8(slope3), s2 + fold8(slope3 * n3)

        zero = jnp.zeros((8, 256), f32)
        pool, s1, s2 = lax.fori_loop(0, ROWS // 64, block, (zero, zero, zero))
        own[:, cols] = pool * columns_of(inverse_counts, 256)
        sums_out[pl.ds(0, 8), cols] = s1
        sums_out[pl.ds(8, 8), cols] = s2

    keep(normed, normed_out)
    keep(slope, slope_out)
    movers = gather_pooled(own, pooled_all, gsend, grecv, 1536)
    for mover in movers:
        next(mover)
    pooled_all[z, lax.rem(dp, 4), sub] = own[...]
    run_all(movers)
    rows_all = 256
    keep(pooled_all, pooled_out)
    loads[4].wait()
    loads[5].wait()

    @pl.loop(0, rows_all // 8)
    def _(k):
        value = pooled_all[k // 8, lax.rem(k // 2, 4), lax.rem(k, 2)]
        level[pl.ds(pl.multiple_of(k * 8, 8), 8), :] = value

    @pl.loop(0, rows_all // 32)
    def _(k):
        rows = pl.ds(pl.multiple_of(k * 32, 32), 32)
        high, low = split(level[rows, :])
        pool_high[rows, :] = high
        pool_low[rows, :] = low

    proj = hidden.shape[1]
    share = 1.0 / rows_all

    @pl.loop(0, proj // 256)
    def _(n):
        cols = pl.ds(pl.multiple_of(n * 256, 256), 256)
        right = wp[:, cols]
        value = mm(pool_high[...], right) + mm(pool_low[...], right)
        centre = jnp.sum(value, axis=0, keepdims=True) * share
        square = jnp.sum(value * value, axis=0, keepdims=True) * share
        scale = lax.rsqrt(square - centre * centre + epsilon)
        normal_here = (value - centre) * scale
        level_here = norm_project[pl.ds(0, 1), cols] * normal_here + norm_project[pl.ds(1, 1), cols]
        normal[:, cols] = normal_here
        level[:, cols] = level_here
        hidden[:, cols] = level_here * sigmoid(level_here)
        upstream[pl.ds(0, 1), cols] = scale * norm_project[pl.ds(0, 1), cols]

    keep(hidden, hidden_out)
    high, low = split(hidden[...])
    codes = mm(high, wc[...]) + mm(low, wc[...])

    centre = jnp.sum(codes, axis=0, keepdims=True) * share
    moved = codes - centre
    cov = exact(moved, moved, ((0,), (0,))) * share
    size = cov.shape[0]
    row = lax.broadcasted_iota(jnp.int32, (size, size), 0)
    column = lax.broadcasted_iota(jnp.int32, (size, size), 1)
    inverse = factor_inverse(cov + jnp.where(row == column, whiten_floor, 0.0))
    white = exact(moved, inverse, ((1,), (1,)))
    unit_scale = lax.rsqrt(jnp.sum(white * white, axis=1, keepdims=True) + epsilon)
    unit = white * unit_scale
    same = (pair_column[...] == pair_row[...]).astype(f32)
    gap = 2.0 * unit - exact(same, unit, ((1,), (0,)))
    loss_out[...] = jnp.broadcast_to(jnp.sum(jnp.sum(gap * gap, axis=1, keepdims=True), axis=0, keepdims=True) * share, (8, 128))
    grad_white = unit_scale * (gap - unit * jnp.sum(unit * gap, axis=1, keepdims=True))
    gram = exact(grad_white, white, ((0,), (0,)))
    half = jnp.where(row > column, gram, jnp.where(row == column, 0.5 * gram, 0.0))
    both = half + jnp.transpose(half)
    grad_moved = exact(grad_white - exact(white, both, ((1,), (0,))) * share, inverse, ((1,), (0,)))
    dcodes = grad_moved - jnp.sum(grad_moved, axis=0, keepdims=True) * share
    dcodes_out[...] = dcodes

    high, low = split(dcodes)

    @pl.loop(0, proj // 256)
    def _(n):
        cols = pl.ds(pl.multiple_of(n * 256, 256), 256)
        right = wc[cols, :]
        grad = mm_nt(high, right) + mm_nt(low, right)
        level_here = level[:, cols]
        sig = sigmoid(level_here)
        grad = grad * (sig * (1.0 + level_here * (1.0 - sig)))
        normal_here = normal[:, cols]
        total = jnp.sum(grad, axis=0, keepdims=True)
        dot = jnp.sum(grad * normal_here, axis=0, keepdims=True)
        grad_norm_out[pl.ds(0, 1), cols] = dot
        grad_norm_out[pl.ds(1, 1), cols] = total
        dproj[:, cols] = upstream[pl.ds(0, 1), cols] * (grad - (total + normal_here * dot) * share)

    keep(dproj, dprojected_out)
    mine = dproj[pl.ds(pl.multiple_of(me * 8, 8), 8), :]
    high = mine.astype(bf16).astype(f32)
    both_terms = jnp.concatenate([high, mine - high], axis=0).astype(bf16)

    @pl.loop(0, width // 256)
    def _(n):
        cols = pl.ds(pl.multiple_of(n * 256, 256), 256)
        value = mm_nt(both_terms, wp[cols, :])
        upstream[:, cols] = (value[0:8] + value[8:16]) * columns_of(inverse_counts, 256)

    for copy in saves:
        copy.wait()


def forward(
    images, pixel_mask, pair_column, pair_row, w_reduce, w_spatial, w_expand, w_project, w_code,
    norm_reduce, norm_spatial, norm_expand, norm_project,
):
    width, inner = w_reduce.shape
    proj, code = w_code.shape
    hbm = pl.BlockSpec(memory_space=pl.ANY)
    vmem = pl.BlockSpec(memory_space=pltpu.VMEM)
    shape = jax.ShapeDtypeStruct
    return pl.pallas_call(
        fwd_kernel,
        out_shape=[
            shape((4, 4, 2, 8, width), f32),
            shape((256, proj), f32),
            shape((256, proj), f32),
            shape((256, code), f32),
            shape((8, 128), f32),
            shape((2, proj), f32),
            shape((8, width), f32),
            shape((ROWS, width), bf16),
            shape((ROWS, inner), f32),
            shape((ROWS, inner), bf16),
            shape((ROWS, inner), f32),
            shape((ROWS, inner), bf16),
            shape((ROWS, width), f32),
            shape((ROWS, width), f32),
            shape((ROWS, 128), f32),
            shape((8, width), f32),
            shape((16, width), f32),
        ],
        in_specs=[hbm, vmem, vmem, vmem, hbm, hbm, hbm, hbm, hbm, vmem, vmem, vmem, vmem],
        out_specs=[hbm, hbm, hbm, vmem, vmem, vmem, vmem] + [hbm] * 7 + [vmem] * 3,
        scratch_shapes=[
            pltpu.VMEM((49, 8, width), bf16),
            pltpu.VMEM((ROWS, width), bf16),
            pltpu.VMEM((width, inner), bf16),
            pltpu.VMEM((9 * inner, inner), bf16),
            pltpu.VMEM((inner, width), bf16),
            pltpu.VMEM((width, proj), bf16),
            pltpu.VMEM((proj, code), bf16),
            pltpu.VMEM((ROWS, inner), f32),
            pltpu.VMEM((ROWS + 16, inner), f32),
            pltpu.VMEM((3, ROWS + 128, inner), bf16),
            pltpu.VMEM((ROWS, inner), f32),
            pltpu.VMEM((ROWS, inner), bf16),
            pltpu.VMEM((ROWS, width), f32),
            pltpu.VMEM((ROWS, width), f32),
            pltpu.VMEM((8, width), f32),
            pltpu.VMEM((4, 4, 2, 8, width), f32),
            pltpu.VMEM((256, width), bf16),
            pltpu.VMEM((256, width), bf16),
            pltpu.VMEM((256, width), f32),
            pltpu.VMEM((256, proj), f32),
            pltpu.VMEM((256, proj), f32),
            pltpu.VMEM((256, proj), f32),
            pltpu.VMEM((8, 128), f32),
            pltpu.VMEM((32, 8, 128), f32),
            pltpu.VMEM((32, 2, inner), f32),
            pltpu.VMEM((32, 2, inner), f32),
            pltpu.VMEM((2, 2, width), f32),
            pltpu.VMEM((4, 2, width), f32),
            pltpu.VMEM((4, 2, width), f32),
            pltpu.SemaphoreType.DMA((6,)),
            pltpu.SemaphoreType.DMA((10,)),
            pltpu.SemaphoreType.DMA((6,)),
            pltpu.SemaphoreType.DMA((6,)),
            pltpu.SemaphoreType.DMA((2, 14)),
            pltpu.SemaphoreType.DMA((2, 14)),
        ],
        compiler_params=pltpu.CompilerParams(
            collective_id=20, has_side_effects=True, vmem_limit_bytes=58 << 20
        ),
    )(
        images, pixel_mask, pair_column, pair_row, w_reduce, w_spatial, w_expand, w_project, w_code,
        norm_reduce, norm_spatial, norm_expand, norm_project,
    )


class Job:
    def __init__(self, ring_first, rows, acc, other, out, sib_out, land, scratch, send, recv, loc):
        self.ring_first, self.rows, self.acc, self.other = ring_first, rows, acc, other
        self.out, self.sib_out, self.land, self.scratch = out, sib_out, land, scratch
        self.mover = Mover(send, recv)
        self.loc = loc
        self.taken = 0

    def take(self, rows):
        ref = rows_at(self.scratch, self.taken, rows)
        self.taken += rows
        return ref

    def start(self):
        dp, sub, _, _ = place()
        self.mover.go(None, self.other, self.land, 0, 0, (dp, 1 - sub))

    def ring_reduce(self, base, block):
        dp, sub, z, q = place()
        go, got = self.mover.go, self.mover.got
        after_me, before_me = (ring_dp(z, q + 1), sub), (ring_dp(z, q + 3), sub)
        half = block // 2
        r0a, r0b, r1a, r1b = self.take(half), self.take(half), self.take(block), self.take(block)

        def blk(k, h=0, n=block):
            return rows_at(self.acc, base + lax.rem(q + k, 4) * block + h, n)

        go(None, blk(2, 0, half), r0a, 1, 1, after_me)
        go(None, blk(2, half, half), r0b, 2, 2, before_me)
        yield
        got(None, r0a, 1)
        add_into(blk(1, 0, half), r0a, half)
        go(None, blk(1), r1a, 3, 3, after_me)
        got(None, r0b, 2)
        add_into(blk(3, half, half), r0b, half)
        go(None, blk(3), r1b, 4, 4, before_me)
        yield
        got(None, r1a, 3)
        add_into(blk(0), r1a, block)
        got(None, r1b, 4)
        add_into(blk(0), r1b, block)

    def line_reduce(self, base, chunk):
        dp, sub, z, _ = place()
        go, got = self.mover.go, self.mover.got
        up, down = (dp + 4, sub), (dp - 4, sub)
        low = [self.take(chunk) for _ in range(3)]
        high = [self.take(chunk) for _ in range(3)]

        def at(j):
            return rows_at(self.acc, base + jnp.clip(j, 0, 3) * chunk, chunk)

        for t in range(3):
            go(z <= t, at(3 + z - t), low[t], 5 + t, 5 + t, up)
            go(z >= 3 - t, at(z - 3 + t), high[t], 8 + t, 8 + t, down)
            yield
            got(
                jnp.logical_and(z >= 1, z <= t + 1),
                low[t],
                5 + t,
                lambda: add_into(at(2 + z - t), low[t], chunk),
            )
            got(
                jnp.logical_and(z <= 2, z >= 2 - t),
                high[t],
                8 + t,
                lambda: add_into(at(z - 2 + t), high[t], chunk),
            )

    def run(self):
        dp, sub, z, q = place()
        sib = (dp, 1 - sub)
        mover, out, rows = self.mover, self.out, self.rows
        self.start()
        yield
        mover.got(None, self.land, 0)
        add_into(self.acc, self.land, rows)
        big, small = rows // 4, rows // 16
        half_small = small // 2
        half_big = big // 2

        def share(ref, k):
            mover.go(None, ref, ref, 21 + k, 21, sib)

        if self.ring_first:
            yield from self.ring_reduce(0, big)
            yield from self.line_reduce(q * big, small)
            mine = rows_at(self.acc, q * big + z * small, small)
            own = rows_at(out, q * big + z * small, small)
            local = pltpu.make_async_copy(mine, own, self.loc)
            local.start()
            at = lambda j: rows_at(out, q * big + j * small, small)
            yield from mover.line_gather(at, mine, 11)
            local.wait()
            share(rows_at(out, q * big, big), 3)

            def blk(k, h):
                start = lax.rem(q + k, 4) * big
                if h is None:
                    return rows_at(out, start, big)
                return rows_at(out, start + h * half_big, half_big)

            yield from mover.ring_gather(blk, None, 17, share)
        else:
            yield from self.line_reduce(0, big)
            yield from self.ring_reduce(z * big, small)
            mine = rows_at(self.acc, z * big + q * small, small)
            own = rows_at(out, z * big + q * small, small)
            local = pltpu.make_async_copy(mine, own, self.loc)
            local.start()

            def blk(k, h):
                start = z * big + lax.rem(q + k, 4) * small
                if h is None:
                    return rows_at(out, start, small)
                return rows_at(out, start + h * half_small, half_small)

            yield from mover.ring_gather(blk, mine, 17, lambda ref, k: None)
            local.wait()
            share(rows_at(out, z * big, big), 3)
            at = lambda j: rows_at(out, j * big, big)
            yield from mover.line_gather(at, None, 11)
            for k in range(1, 4):
                share(rows_at(out, lax.rem(z + k, 4) * big, big), k - 1)
        yield
        arrived(self.sib_out, mover.recv.at[21])
        mover.drain()


JOB_SEMS = 25


def add_into(dst, src, rows):
    step = 16 if rows % 16 == 0 else 8

    @pl.loop(0, rows // step)
    def _(k):
        at = pl.ds(pl.multiple_of(k * step, 8), step)
        dst[at, :] = dst[at, :] + src[at, :]


def rows_at(ref, start, size):
    return ref.at[pl.ds(pl.multiple_of(start, 8), size)]


def landing_rows(ring_first, rows):
    big, small = rows // 4, rows // 16
    return 3 * big + 6 * small if ring_first else 3 * small + 6 * big


JOBS = (
    (2, 0, 256, 0, 1536, True),
    (2, 0, 256, 1536, 512, False),
    (0, 0, 896, 0, 512, True),
    (0, 896, 256, 0, 512, False),
    (0, 1152, 896, 0, 512, True),
    (0, 2048, 256, 0, 512, False),
    (1, 0, 768, 0, 512, True),
    (1, 768, 256, 0, 512, False),
)


def tree_gen(pair, plane, line, send, recv, result):
    dp, sub, z, _ = place()
    w = lax.rem(dp, 4)
    remote(pair.at[sub], pair.at[sub], send.at[0], recv.at[0], (dp, 1 - sub)).start()
    yield
    arrived(pair.at[0], recv.at[0])
    plane[w] = pair[0] + pair[1]
    for k in range(1, 4):
        where = (z * 4 + lax.rem(w + k, 4), sub)
        remote(plane.at[w], plane.at[w], send.at[1], recv.at[1], where).start()
    yield
    arrived(plane.at[pl.ds(0, 3)], recv.at[1])
    line[z] = (plane[0] + plane[1]) + (plane[2] + plane[3])
    for k in range(1, 4):
        where = (lax.rem(z + k, 4) * 4 + w, sub)
        remote(line.at[z], line.at[z], send.at[2], recv.at[2], where).start()
    yield
    arrived(line.at[pl.ds(0, 3)], recv.at[2])
    result[...] = (line[0] + line[1]) + (line[2] + line[3])
    arrived(pair.at[0], send.at[0])
    arrived(plane.at[pl.ds(0, 3)], send.at[1])
    arrived(line.at[pl.ds(0, 3)], send.at[2])


def back_kernel(
    upstream, masked_in, reduced_in, act1_in, spatial_in, act2_in, normed_in, slope_in, mask, stats, sums_in,
    w_reduce, w_spatial, w_expand, norm_reduce, norm_spatial, norm_expand,
    grad_images, grad_spatial, grad_reduce, grad_expand, grad_norm_reduce, grad_norm_spatial, grad_norm_expand,
    wr, ws, we, masked, reduced, act1, spatial, act2, big, dsum, dexp, level, wide, shifted, dred,
    gs, gr, land_s, land_r, land_e, *rest,
):
    scratches = rest[: len(JOBS)]
    buf5, buf6, pair, plane, line, load, send, recv, jsend, jrecv, jloc, osem = rest[len(JOBS) :]
    dp, sub, z, q = place()
    me = dp * 2 + sub
    width, inner = wr.shape
    normed = big.at[pl.ds(0, ROWS)]
    loads = {}
    for k, (name, a, b) in enumerate(
        [
            ("slope", slope_in, dsum),
            ("normed", normed_in, normed),
            ("we", w_expand, we),
            ("act2", act2_in, act2),
            ("spatial", spatial_in, spatial),
            ("ws", w_spatial, ws),
            ("act1", act1_in, act1),
            ("reduced", reduced_in, reduced),
            ("masked", masked_in, masked),
            ("wr", w_reduce, wr),
        ]
    ):
        loads[name] = pltpu.make_async_copy(a, b, load.at[k])
        loads[name].start()
    greet_start()

    @pl.loop(0, width // 512)
    def _(n):
        cols = pl.ds(pl.multiple_of(n * 512, 512), 512)
        up = upstream[:, cols]
        pair[sub, pl.ds(0, 1), cols] = jnp.sum(up * sums_in[pl.ds(0, 8), cols], axis=0, keepdims=True)
        pair[sub, pl.ds(1, 1), cols] = jnp.sum(up * sums_in[pl.ds(8, 8), cols], axis=0, keepdims=True)

    wide[pl.ds(0, 8), :] = jnp.zeros((8, inner), f32)
    wide[pl.ds(ROWS + 8, 8), :] = jnp.zeros((8, inner), f32)
    for b in range(3):
        shifted[b, pl.ds(0, 64), :] = jnp.zeros((64, inner), bf16)
        shifted[b, pl.ds(512, 64), :] = jnp.zeros((64, inner), bf16)
    greet_wait()
    third = tree_gen(pair, plane, line, send, recv, grad_norm_expand)
    next(third)
    loads["slope"].wait()

    def scale_slope(lo, hi):
        @pl.loop(lo, hi)
        def _(n):
            cols = pl.ds(pl.multiple_of(n * 256, 256), 256)
            up = upstream[:, cols]
            for k in range(SLOTS // 8):
                rows = pl.ds(64 * k, 64)
                value = dsum[rows, cols].reshape(8, 8, 256) * up[None]
                dsum[rows, cols] = value.reshape(64, 256)

    parts = width // 256
    scale_slope(0, parts // 4)
    next(third)
    scale_slope(parts // 4, parts * 5 // 8)
    next(third)
    scale_slope(parts * 5 // 8, parts)
    loads["normed"].wait()
    loads["we"].wait()
    loads["act2"].wait()
    next(third, None)
    share = 1.0 / stats[pl.ds(6, 1), :]
    plane[0, pl.ds(0, 1), :] = grad_norm_expand[pl.ds(0, 1), :] * share
    plane[0, pl.ds(1, 1), :] = grad_norm_expand[pl.ds(1, 1), :] * share
    plane[1, pl.ds(0, 1), :] = norm_expand[pl.ds(0, 1), :] * stats[pl.ds(5, 1), :]
    first_row = grad_norm_expand[pl.ds(0, 1), :]
    grad_norm_expand[pl.ds(0, 1), :] = grad_norm_expand[pl.ds(1, 1), :]
    grad_norm_expand[pl.ds(1, 1), :] = first_row

    @pl.loop(0, width // 256)
    def _(n):
        cols = pl.ds(pl.multiple_of(n * 256, 256), 256)
        total, dot, gain = plane[0, pl.ds(0, 1), cols], plane[0, pl.ds(1, 1), cols], plane[1, pl.ds(0, 1), cols]
        for k in range(SLOTS // 8):
            rows = pl.ds(64 * k, 64)
            value = dsum[rows, cols] - total - normed[rows, cols] * dot
            dexp[rows, cols] = (columns_of(mask[rows, :], 256) * (value * gain)).astype(bf16)


    small_share = share[:, 0:1]
    loads["spatial"].wait()

    def slope_pass(values, source, norm, at, buf):
        centre, scale = stats[pl.ds(at, 1), pl.ds(0, inner)], stats[pl.ds(at + 1, 1), pl.ds(0, inner)]

        def block(k, carry):
            s1, s2 = carry
            rows = pl.ds(pl.multiple_of(k * 32, 32), 32)
            normal = (source[rows, :] - centre) * scale
            point = norm[pl.ds(0, 1), :] * normal + norm[pl.ds(1, 1), :]
            sig = sigmoid(point)
            value = columns_of(mask[rows, :], inner) * values[rows, :] * (sig * (1.0 + point * (1.0 - sig)))
            values[rows, :] = value
            return s1 + fold8(value), s2 + fold8(value * normal)

        zero = jnp.zeros((8, inner), f32)
        s1, s2 = lax.fori_loop(0, ROWS // 32, block, (zero, zero))
        buf[me, pl.ds(0, 1), :] = jnp.sum(s1, axis=0, keepdims=True)
        buf[me, pl.ds(1, 1), :] = jnp.sum(s2, axis=0, keepdims=True)

    def norm_pass(values, source, norm, at, total, grad_norm, store):
        centre, scale = stats[pl.ds(at, 1), pl.ds(0, inner)], stats[pl.ds(at + 1, 1), pl.ds(0, inner)]
        grad_norm[pl.ds(0, 1), :] = total[1:2]
        grad_norm[pl.ds(1, 1), :] = total[0:1]
        gain = norm[pl.ds(0, 1), :] * scale
        mean, dot = total[0:1] * small_share, total[1:2] * small_share

        @pl.loop(0, ROWS // 32)
        def _(k):
            rows = pl.ds(pl.multiple_of(k * 32, 32), 32)
            normal = (source[rows, :] - centre) * scale
            value = values[rows, :] - mean - normal * dot
            store(k, columns_of(mask[rows, :], inner) * (value * gain))

    @pl.loop(0, inner // 256)
    def _(n):
        cols = pl.ds(pl.multiple_of(n * 256, 256), 256)
        level[:, cols] = mm_nt(dexp[...], we[cols, :])

    slope_pass(level, spatial, norm_spatial, 2, buf5)
    direct_start(buf5, send.at[3], recv.at[3])

    @pl.loop(0, width // 256)
    def _(n):
        cols = pl.ds(pl.multiple_of(n * 256, 256), 256)
        big[:, cols] = mm_tn(act2[...], dexp[:, cols])

    grads = (gs, gr, big)
    outs = (grad_spatial, grad_reduce, grad_expand)
    lands = (land_s, land_r, land_e)

    def make_job(j):
        k, r0, rows, c0, cols, ring_first = JOBS[j]
        half = grads[k].shape[0] // 2

        def cut(ref, base):
            return ref.at[pl.ds(pl.multiple_of(base + r0, 8), rows), pl.ds(c0, cols)]

        return Job(
            ring_first,
            rows,
            cut(grads[k], sub * half),
            cut(grads[k], (1 - sub) * half),
            cut(outs[k], sub * half),
            cut(outs[k], (1 - sub) * half),
            cut(lands[k], 0),
            scratches[j],
            jsend.at[j],
            jrecv.at[j],
            jloc.at[j],
        ).run()

    live = {}

    def begin(*which):
        for j in which:
            live[j] = make_job(j)
            next(live[j])

    def turn():
        for j in sorted(live):
            try:
                next(live[j])
            except StopIteration:
                live.pop(j)

    begin(0, 1)
    total = direct_finish(buf5, send.at[3], recv.at[3])
    turn()

    def store_spatial(k, value):
        wide[pl.ds(pl.multiple_of(k * 32 + 8, 8), 32), :] = value
        shifted[1, pl.ds(pl.multiple_of(k * 32 + 64, 32), 32), :] = value.astype(bf16)

    norm_pass(level, spatial, norm_spatial, 2, total, grad_norm_spatial, store_spatial)

    @pl.loop(0, ROWS // 32)
    def _(k):
        for b in (0, 2):
            rows = wide[pl.ds(pl.multiple_of(k * 32 + 16 - 8 * b, 8), 32), :]
            shifted[b, pl.ds(pl.multiple_of(k * 32 + 64, 32), 32), :] = rows.astype(bf16)

    turn()
    loads["ws"].wait()
    loads["reduced"].wait()
    loads["act1"].wait()

    @pl.loop(0, inner // 256)
    def _(n):
        cols = pl.ds(pl.multiple_of(n * 256, 256), 256)

        def taps(a, total):
            for b in range(3):
                left = shifted[b, pl.ds(128 - 64 * a, ROWS), :]
                right = ws[pl.ds(pl.multiple_of((a * 3 + b) * inner + n * 256, 256), 256), :]
                total = total + mm_nt(left, right)
            return total

        level[:, cols] = taps(0, jnp.zeros((ROWS, 256), f32))
        level[:, cols] = taps(1, level[:, cols])
        level[:, cols] = taps(2, level[:, cols])

    turn()
    slope_pass(level, reduced, norm_reduce, 0, buf6)
    direct_start(buf6, send.at[4], recv.at[4])

    @pl.loop(0, 9)
    def _(tap):
        right = shifted[lax.rem(tap, 3), pl.ds(pl.multiple_of(128 - 64 * (tap // 3), 64), ROWS), :]
        gs[pl.ds(pl.multiple_of(tap * inner, inner), inner), :] = mm_tn(act1[...], right)

    begin(2, 3, 4, 5)
    total = direct_finish(buf6, send.at[4], recv.at[4])

    def store_reduce(k, value):
        dred[pl.ds(pl.multiple_of(k * 32, 32), 32), :] = value.astype(bf16)

    norm_pass(level, reduced, norm_reduce, 0, total, grad_norm_reduce, store_reduce)
    turn()
    loads["masked"].wait()

    @pl.loop(0, width // 256)
    def _(n):
        cols = pl.ds(pl.multiple_of(n * 256, 256), 256)
        gr[cols, :] = mm_tn(masked[:, cols], dred[...])

    begin(6, 7)
    turn()
    loads["wr"].wait()

    @pl.loop(0, width // 256)
    def _(n):
        cols = pl.ds(pl.multiple_of(n * 256, 256), 256)
        value = dsum[:, cols] + mm_nt(dred[...], wr[cols, :])
        dsum[:, cols] = value * columns_of(mask[...], 256)

    images_out = [
        pltpu.make_async_copy(dsum.at[pl.ds(64 * r, 56)], grad_images.at[pl.ds(56 * r, 56)], osem.at[r])
        for r in range(SIDE)
    ]
    for copy in images_out:
        copy.start()
    while live:
        turn()
    for copy in images_out:
        copy.wait()


def backward(
    upstream, masked, reduced, act1, spatial, act2, normed, slope, mask, stats, sums,
    w_reduce, w_spatial, w_expand, norm_reduce, norm_spatial, norm_expand,
):
    width, inner = w_reduce.shape
    hbm = pl.BlockSpec(memory_space=pl.ANY)
    vmem = pl.BlockSpec(memory_space=pltpu.VMEM)
    shape = jax.ShapeDtypeStruct
    landings = [
        pltpu.VMEM((landing_rows(ring_first, rows), cols), f32) for _, _, rows, _, cols, ring_first in JOBS
    ]
    return pl.pallas_call(
        back_kernel,
        out_shape=[
            shape((392, width), f32),
            shape((9 * inner, inner), f32),
            shape((width, inner), f32),
            shape((inner, width), f32),
            shape((2, inner), f32),
            shape((2, inner), f32),
            shape((2, width), f32),
        ],
        in_specs=[vmem] + [hbm] * 7 + [vmem] * 3 + [hbm] * 3 + [vmem] * 3,
        out_specs=[hbm] * 4 + [vmem] * 3,
        scratch_shapes=[
            pltpu.VMEM((width, inner), bf16),
            pltpu.VMEM((9 * inner, inner), bf16),
            pltpu.VMEM((inner, width), bf16),
            pltpu.VMEM((ROWS, width), bf16),
            pltpu.VMEM((ROWS, inner), f32),
            pltpu.VMEM((ROWS, inner), bf16),
            pltpu.VMEM((ROWS, inner), f32),
            pltpu.VMEM((ROWS, inner), bf16),
            pltpu.VMEM((inner, width), f32),
            pltpu.VMEM((ROWS, width), f32),
            pltpu.VMEM((ROWS, width), bf16),
            pltpu.VMEM((ROWS, inner), f32),
            pltpu.VMEM((ROWS + 16, inner), f32),
            pltpu.VMEM((3, ROWS + 128, inner), bf16),
            pltpu.VMEM((ROWS, inner), bf16),
            pltpu.VMEM((9 * inner, inner), f32),
            pltpu.VMEM((width, inner), f32),
            pltpu.VMEM((9 * inner // 2, inner), f32),
            pltpu.VMEM((width // 2, inner), f32),
            pltpu.VMEM((inner // 2, width), f32),
            *landings,
            pltpu.VMEM((32, 2, inner), f32),
            pltpu.VMEM((32, 2, inner), f32),
            pltpu.VMEM((2, 2, width), f32),
            pltpu.VMEM((4, 2, width), f32),
            pltpu.VMEM((4, 2, width), f32),
            pltpu.SemaphoreType.DMA((10,)),
            pltpu.SemaphoreType.DMA((5,)),
            pltpu.SemaphoreType.DMA((5,)),
            pltpu.SemaphoreType.DMA((len(JOBS), JOB_SEMS)),
            pltpu.SemaphoreType.DMA((len(JOBS), JOB_SEMS)),
            pltpu.SemaphoreType.DMA((len(JOBS),)),
            pltpu.SemaphoreType.DMA((SIDE,)),
        ],
        compiler_params=pltpu.CompilerParams(
            collective_id=21, has_side_effects=True, vmem_limit_bytes=63 << 20
        ),
    )(
        upstream, masked, reduced, act1, spatial, act2, normed, slope, mask, stats, sums,
        w_reduce, w_spatial, w_expand, norm_reduce, norm_spatial, norm_expand,
    )


def whiten(codes, pairing):
    highest = lax.Precision.HIGHEST
    total = codes.shape[0]
    centre = jnp.sum(codes, axis=0) / total
    moved = codes - centre
    covariance = jnp.dot(moved.T, moved, precision=highest) / total
    covariance = covariance + whiten_floor * jnp.eye(codes.shape[1], dtype=jnp.float32)
    factor = jnp.linalg.cholesky(covariance)
    inverse = lax.linalg.triangular_solve(factor, jnp.eye(codes.shape[1], dtype=jnp.float32), left_side=True, lower=True)
    white = jnp.dot(moved, inverse.T, precision=highest)
    scale = lax.rsqrt(jnp.sum(white * white, axis=1, keepdims=True) + epsilon)
    unit = white * scale
    same = (pairing[:, None] == pairing[None, :]).astype(jnp.float32)
    gap = 2.0 * unit - jnp.dot(same, unit, precision=highest)
    loss_value = jnp.sum(gap * gap) / total
    grad_unit = 0.5 * (2.0 * gap - jnp.dot(same, gap, precision=highest))
    grad_white = scale * grad_unit - white * scale * scale * scale * jnp.sum(white * grad_unit, axis=1, keepdims=True)
    gram = jnp.dot(grad_white.T, white, precision=highest)
    row = lax.broadcasted_iota(jnp.int32, gram.shape, 0)
    column = lax.broadcasted_iota(jnp.int32, gram.shape, 1)
    lower = jnp.where(row > column, gram, jnp.where(row == column, 0.5 * gram, 0.0))
    both = lower + lower.T
    grad_moved = jnp.dot(grad_white - jnp.dot(white, both, precision=highest) / total, inverse, precision=highest)
    return loss_value, grad_moved - jnp.sum(grad_moved, axis=0) / total


def silu_slope(values):
    sigmoid_value = jax.nn.sigmoid(values)
    return sigmoid_value * (1.0 + values * (1.0 - sigmoid_value))


def moments(sum_value, sum_square, total_count):
    centre = sum_value / total_count
    return (centre, lax.rsqrt(sum_square / total_count - centre * centre + epsilon))


def make_columns(activation):
    images_here, pixel_count, inner_width = activation.shape
    grid_map = activation.reshape(images_here, SIDE, SIDE, inner_width)
    padded = jnp.pad(grid_map, ((0, 0), (1, 1), (1, 1), (0, 0)))
    pieces = [
        padded[:, tap_row : tap_row + SIDE, tap_col : tap_col + SIDE, :]
        for tap_row in range(3)
        for tap_col in range(3)
    ]
    return jnp.concatenate(pieces, axis=3).reshape(images_here * pixel_count, 9 * inner_width)


def fold_columns(columns, images_here, inner_width):
    tap_grads = columns.reshape(images_here, SIDE, SIDE, 9, inner_width)
    padded = jnp.zeros((images_here, SIDE + 2, SIDE + 2, inner_width), jnp.float32)
    for tap_row in range(3):
        for tap_col in range(3):
            padded = padded.at[:, tap_row : tap_row + SIDE, tap_col : tap_col + SIDE, :].add(
                tap_grads[:, :, :, 3 * tap_row + tap_col, :]
            )
    return padded[:, 1 : SIDE + 1, 1 : SIDE + 1, :].reshape(images_here, SIDE * SIDE, inner_width)


def pixel_sums(values, weight):
    return (jnp.sum(values * weight, axis=(0, 1)), jnp.sum(values * values * weight, axis=(0, 1)))


def front(
    masked_low,
    weight,
    counts,
    w_reduce,
    w_spatial,
    w_expand,
    norm_reduce,
    norm_spatial,
    norm_expand,
):
    images_here, pixel_count, width = masked_low.shape
    inner_width = w_reduce.shape[1]
    rows_here = images_here * pixel_count
    reduced = jnp.dot(
        masked_low.reshape(rows_here, width), w_reduce, preferred_element_type=jnp.float32
    ).reshape(images_here, pixel_count, inner_width)
    sum_reduce, square_reduce = pixel_sums(reduced, weight)
    sum_reduce, square_reduce, valid_total = lax.psum((sum_reduce, square_reduce, jnp.sum(counts)), ("dp", "sub"))
    centre_reduce, scale_reduce = moments(sum_reduce, square_reduce, valid_total)
    normed_reduce = (reduced - centre_reduce) * scale_reduce
    level_reduce = norm_reduce[0] * normed_reduce + norm_reduce[1]
    act_reduce = (weight * jax.nn.silu(level_reduce)).astype(jnp.bfloat16)
    columns = make_columns(act_reduce)
    spatial = jnp.dot(
        columns, w_spatial.reshape(9 * inner_width, inner_width), preferred_element_type=jnp.float32
    ).reshape(images_here, pixel_count, inner_width)
    sum_spatial, square_spatial = pixel_sums(spatial, weight)
    sum_spatial, square_spatial = lax.psum((sum_spatial, square_spatial), ("dp", "sub"))
    centre_spatial, scale_spatial = moments(sum_spatial, square_spatial, valid_total)
    normed_spatial = (spatial - centre_spatial) * scale_spatial
    level_spatial = norm_spatial[0] * normed_spatial + norm_spatial[1]
    act_spatial = (weight * jax.nn.silu(level_spatial)).astype(jnp.bfloat16)
    expanded = jnp.dot(
        act_spatial.reshape(rows_here, inner_width), w_expand, preferred_element_type=jnp.float32
    ).reshape(images_here, pixel_count, width)
    sum_expand, square_expand = pixel_sums(expanded, weight)
    sum_expand, square_expand = lax.psum((sum_expand, square_expand), ("dp", "sub"))
    centre_expand, scale_expand = moments(sum_expand, square_expand, valid_total)
    normed_expand = (expanded - centre_expand) * scale_expand
    summed = masked_low.astype(jnp.float32) + norm_expand[0] * normed_expand + norm_expand[1]
    stats = (
        valid_total,
        centre_reduce,
        scale_reduce,
        centre_spatial,
        scale_spatial,
        centre_expand,
        scale_expand,
    )
    return (
        (
            normed_reduce,
            level_reduce,
            columns,
            normed_spatial,
            level_spatial,
            act_spatial,
            normed_expand,
            summed,
        ),
        stats,
    )


def norm_back(upstream, normed, gain, scale_value, sum_grad, dot_grad, total_count):
    return gain * scale_value * (upstream - (sum_grad + normed * dot_grad) / total_count)


def plain_shards(
    images,
    pixel_mask,
    pairing,
    w_reduce,
    w_spatial,
    w_expand,
    w_project,
    w_code,
    norm_reduce,
    norm_spatial,
    norm_expand,
    norm_project,
):
    images_here, pixel_count, width = images.shape
    inner_width = w_reduce.shape[1]
    images_total = pairing.shape[0]
    rows_here = images_here * pixel_count
    highest = lax.Precision.HIGHEST
    weight = pixel_mask.astype(jnp.float32)[:, :, None]
    counts = jnp.sum(weight, axis=1)
    masked_low = images * weight.astype(jnp.bfloat16)
    project_full = w_project.astype(jnp.float32)
    code_full = w_code.astype(jnp.float32)
    saved, stats = front(
        masked_low,
        weight,
        counts,
        w_reduce,
        w_spatial,
        w_expand,
        norm_reduce,
        norm_spatial,
        norm_expand,
    )
    (
        normed_reduce,
        level_reduce,
        columns,
        normed_spatial,
        level_spatial,
        act_spatial,
        normed_expand,
        summed,
    ) = saved
    (
        valid_total,
        centre_reduce,
        scale_reduce,
        centre_spatial,
        scale_spatial,
        centre_expand,
        scale_expand,
    ) = stats
    output = weight * jax.nn.silu(summed)
    own_pooled = jnp.sum(output, axis=1) / counts
    pooled = lax.all_gather(own_pooled, ("dp", "sub"), axis=0, tiled=True)
    projected = jnp.dot(pooled, project_full, precision=highest)
    centre_project, scale_project = moments(
        jnp.sum(projected, axis=0), jnp.sum(projected * projected, axis=0), float(images_total)
    )
    normed_project = (projected - centre_project) * scale_project
    level_project = norm_project[0] * normed_project + norm_project[1]
    hidden = jax.nn.silu(level_project)
    codes = jnp.dot(hidden, code_full, precision=highest)
    loss_value, grad_codes = whiten(codes, pairing)
    grad_w_code = jnp.dot(hidden.T, grad_codes, precision=highest)
    grad_hidden = jnp.dot(grad_codes, code_full.T, precision=highest)
    grad_level_project = grad_hidden * silu_slope(level_project)
    sum_project_grad = jnp.sum(grad_level_project, axis=0)
    dot_project_grad = jnp.sum(grad_level_project * normed_project, axis=0)
    grad_norm_project = jnp.stack([dot_project_grad, sum_project_grad])
    grad_projected = norm_back(
        grad_level_project,
        normed_project,
        norm_project[0],
        scale_project,
        sum_project_grad,
        dot_project_grad,
        float(images_total),
    )
    grad_w_project = jnp.dot(pooled.T, grad_projected, precision=highest)
    own_start = lax.axis_index(("dp", "sub")) * images_here
    own_projected = lax.dynamic_slice_in_dim(grad_projected, own_start, images_here, 0)
    grad_pooled = jnp.dot(own_projected, project_full.T, precision=highest)
    grad_summed = weight * (grad_pooled / counts)[:, None, :] * silu_slope(summed)
    sum_expand_grad, dot_expand_grad = lax.psum(
        (jnp.sum(grad_summed, axis=(0, 1)), jnp.sum(grad_summed * normed_expand, axis=(0, 1))), ("dp", "sub")
    )
    grad_norm_expand = jnp.stack([dot_expand_grad, sum_expand_grad])
    grad_expanded = (
        (
            weight
            * norm_back(
                grad_summed,
                normed_expand,
                norm_expand[0],
                scale_expand,
                sum_expand_grad,
                dot_expand_grad,
                valid_total,
            )
        )
        .astype(jnp.bfloat16)
        .reshape(rows_here, width)
    )
    grad_w_expand = jnp.einsum(
        "rm,rc->mc",
        act_spatial.reshape(rows_here, inner_width),
        grad_expanded,
        preferred_element_type=jnp.float32,
    )
    grad_act_spatial = jnp.einsum(
        "rc,mc->rm", grad_expanded, w_expand, preferred_element_type=jnp.float32
    ).reshape(images_here, pixel_count, inner_width)
    grad_level_spatial = grad_act_spatial * weight * silu_slope(level_spatial)
    sum_spatial_grad, dot_spatial_grad = lax.psum(
        (
            jnp.sum(grad_level_spatial, axis=(0, 1)),
            jnp.sum(grad_level_spatial * normed_spatial, axis=(0, 1)),
        ),
        ("dp", "sub"),
    )
    grad_norm_spatial = jnp.stack([dot_spatial_grad, sum_spatial_grad])
    grad_spatial_out = (
        (
            weight
            * norm_back(
                grad_level_spatial,
                normed_spatial,
                norm_spatial[0],
                scale_spatial,
                sum_spatial_grad,
                dot_spatial_grad,
                valid_total,
            )
        )
        .astype(jnp.bfloat16)
        .reshape(rows_here, inner_width)
    )
    grad_w_spatial = jnp.einsum(
        "rk,rm->km", columns, grad_spatial_out, preferred_element_type=jnp.float32
    ).reshape(3, 3, inner_width, inner_width)
    grad_columns = jnp.einsum(
        "rm,km->rk",
        grad_spatial_out,
        w_spatial.reshape(9 * inner_width, inner_width),
        preferred_element_type=jnp.float32,
    )
    grad_act_reduce = fold_columns(grad_columns, images_here, inner_width)
    grad_level_reduce = grad_act_reduce * weight * silu_slope(level_reduce)
    sum_reduce_grad, dot_reduce_grad = lax.psum(
        (
            jnp.sum(grad_level_reduce, axis=(0, 1)),
            jnp.sum(grad_level_reduce * normed_reduce, axis=(0, 1)),
        ),
        ("dp", "sub"),
    )
    grad_norm_reduce = jnp.stack([dot_reduce_grad, sum_reduce_grad])
    grad_reduced = (
        (
            weight
            * norm_back(
                grad_level_reduce,
                normed_reduce,
                norm_reduce[0],
                scale_reduce,
                sum_reduce_grad,
                dot_reduce_grad,
                valid_total,
            )
        )
        .astype(jnp.bfloat16)
        .reshape(rows_here, inner_width)
    )
    grad_w_reduce = jnp.einsum(
        "rc,rm->cm",
        masked_low.reshape(rows_here, width),
        grad_reduced,
        preferred_element_type=jnp.float32,
    )
    grad_input = jnp.einsum(
        "rm,cm->rc", grad_reduced, w_reduce, preferred_element_type=jnp.float32
    ).reshape(images_here, pixel_count, width)
    grad_images = weight * (grad_summed + grad_input)
    grad_w_spatial, grad_w_reduce, grad_w_expand = lax.psum(
        (grad_w_spatial, grad_w_reduce, grad_w_expand), ("dp", "sub")
    )
    return (
        loss_value,
        grad_images,
        grad_w_reduce,
        grad_w_spatial.reshape(3, 3, inner_width, inner_width),
        grad_w_expand,
        grad_w_project,
        grad_w_code,
        grad_norm_reduce,
        grad_norm_spatial,
        grad_norm_expand,
        grad_norm_project,
    )


def shards(
    images,
    pixel_mask,
    pairing,
    w_reduce,
    w_spatial,
    w_expand,
    w_project,
    w_code,
    norm_reduce,
    norm_spatial,
    norm_expand,
    norm_project,
):
    width, inner = w_reduce.shape
    highest = lax.Precision.HIGHEST
    taps = w_spatial.reshape(9 * inner, inner)
    (
        pooled, hidden, dprojected, dcodes, loss, grad_norm_project, upstream,
        masked, reduced, act1, spatial, act2, normed, slope, mask, stats, sums,
    ) = forward(
        jnp.transpose(images, (1, 0, 2)),
        pixel_mask,
        pairing.reshape(256, 1),
        pairing.reshape(1, 256),
        w_reduce,
        taps,
        w_expand,
        w_project,
        w_code,
        norm_reduce,
        norm_spatial,
        norm_expand,
        norm_project,
    )
    (
        grad_images, grad_spatial, grad_reduce, grad_expand,
        grad_norm_reduce, grad_norm_spatial, grad_norm_expand,
    ) = backward(
        upstream, masked, reduced, act1, spatial, act2, normed, slope, mask, stats, sums,
        w_reduce, taps, w_expand, norm_reduce, norm_spatial, norm_expand,
    )
    grad_project = jnp.dot(pooled.reshape(256, width).T, dprojected, precision=highest)
    grad_code = jnp.dot(hidden.T, dcodes, precision=highest)
    return (
        loss[0, 0],
        jnp.transpose(grad_images.reshape(49, 8, width), (1, 0, 2)),
        grad_reduce,
        grad_spatial.reshape(w_spatial.shape),
        grad_expand,
        grad_project,
        grad_code,
        grad_norm_reduce,
        grad_norm_spatial,
        grad_norm_expand,
        grad_norm_project,
    )


def solution(mesh):
    fits = mesh.shape["dp"] == 16 and mesh.shape["sub"] == 2
    placed = (P(("dp", "sub"), None, None), P(("dp", "sub"), None)) + (P(),) * 10
    return jax.shard_map(
        shards if fits else plain_shards,
        mesh=mesh,
        in_specs=placed,
        out_specs=(P(), P(("dp", "sub"), None, None)) + (P(),) * 9,
        check_vma=False,
    )
```

```python
import jax
import jax.numpy as jnp
from jax import lax
from jax.experimental import pallas as pl
from jax.experimental.pallas import tpu as pltpu
from jax.sharding import PartitionSpec as P

MESH = pl.DeviceIdType.MESH
SIDE = 7
SLOTS = 56
ROWS = 448
epsilon = 1e-05
whiten_floor = 0.001
f32 = jnp.float32
bf16 = jnp.bfloat16


def place():
    dp = lax.axis_index("dp")
    sub = lax.axis_index("sub")
    z = dp // 4
    y = lax.rem(dp // 2, 2)
    x = lax.rem(dp, 2)
    ring = 3 * y + x - 2 * x * y
    return dp, sub, z, ring


def plane_of(ring):
    ring = lax.rem(ring + 4, 4)
    y = ring // 2
    odd = lax.rem(ring, 2)
    return y * 2 + odd + y - 2 * odd * y


def ring_dp(z, ring):
    return z * 4 + plane_of(ring)


def dev(dp, sub):
    return {"dp": dp, "sub": sub}


def greet_start():
    dp, sub, _, _ = place()
    me = dp * 2 + sub
    barrier = pltpu.get_barrier_semaphore()

    @pl.loop(1, 32)
    def _(step):
        other = lax.rem(me + step, 32)
        pl.semaphore_signal(
            barrier, inc=1, device_id=dev(other // 2, lax.rem(other, 2)), device_id_type=MESH
        )


def greet_wait():
    pl.semaphore_wait(pltpu.get_barrier_semaphore(), 31)


def remote(src, dst, send, recv, where):
    return pltpu.make_async_remote_copy(
        src_ref=src,
        dst_ref=dst,
        send_sem=send,
        recv_sem=recv,
        device_id=dev(*where),
        device_id_type=MESH,
    )


def arrived(ref, sem):
    pltpu.make_async_copy(ref, ref, sem).wait()


def direct_start(buf, send, recv):
    dp, sub, _, _ = place()
    me = dp * 2 + sub

    @pl.loop(1, 32)
    def _(step):
        other = lax.rem(me + step, 32)
        remote(buf.at[me], buf.at[me], send, recv, (other // 2, lax.rem(other, 2))).start()


def direct_finish(buf, send, recv):
    many = buf.at[pl.ds(0, 31)]
    arrived(many, recv)
    total = jnp.sum(buf[...], axis=0)
    arrived(many, send)
    return total


def tree_gen(pair, plane, line, send, recv, result):
    dp, sub, z, _ = place()
    w = lax.rem(dp, 4)
    remote(pair.at[sub], pair.at[sub], send.at[0], recv.at[0], (dp, 1 - sub)).start()
    yield
    arrived(pair.at[0], recv.at[0])
    plane[w] = pair[0] + pair[1]
    for k in range(1, 4):
        where = (z * 4 + lax.rem(w + k, 4), sub)
        remote(plane.at[w], plane.at[w], send.at[1], recv.at[1], where).start()
    yield
    arrived(plane.at[pl.ds(0, 3)], recv.at[1])
    line[z] = (plane[0] + plane[1]) + (plane[2] + plane[3])
    for k in range(1, 4):
        where = (lax.rem(z + k, 4) * 4 + w, sub)
        remote(line.at[z], line.at[z], send.at[2], recv.at[2], where).start()
    yield
    arrived(line.at[pl.ds(0, 3)], recv.at[2])
    result[...] = (line[0] + line[1]) + (line[2] + line[3])
    arrived(pair.at[0], send.at[0])
    arrived(plane.at[pl.ds(0, 3)], send.at[1])
    arrived(line.at[pl.ds(0, 3)], send.at[2])


class Mover:
    def __init__(self, send, recv):
        self.send, self.recv, self.pending = send, recv, []

    def go(self, cond, src, dst, s, r, where):
        def body():
            remote(src, dst, self.send.at[s], self.recv.at[r], where).start()

        if cond is None:
            body()
        else:
            pl.when(cond)(body)
        self.pending.append((cond, src, s))

    def got(self, cond, ref, r, then=None):
        def body():
            arrived(ref, self.recv.at[r])
            if then is not None:
                then()

        if cond is None:
            body()
        else:
            pl.when(cond)(body)

    def drain(self):
        for cond, ref, s in self.pending:

            def body(ref=ref, s=s):
                arrived(ref, self.send.at[s])

            if cond is None:
                body()
            else:
                pl.when(cond)(body)
        self.pending = []

    def settle(self, s):
        for cond, ref, other in self.pending:
            if other == s:
                arrived(ref, self.send.at[s])
        self.pending = [item for item in self.pending if item[2] != s]

    def line_gather(self, at, first, base):
        dp, sub, z, _ = place()
        up, down = (dp + 4, sub), (dp - 4, sub)
        hold = lambda j: at(jnp.clip(j, 0, 3))
        for t in range(3):
            from_up = first if t == 0 and first is not None else hold(z - t)
            from_down = first if t == 0 and first is not None else hold(z + t)
            self.go(jnp.logical_and(z <= 2, z >= t), from_up, hold(z - t), base + t, base + t, up)
            self.go(
                jnp.logical_and(z >= 1, z <= 3 - t),
                from_down,
                hold(z + t),
                base + 3 + t,
                base + 3 + t,
                down,
            )
            yield
            self.got(z >= t + 1, hold(z - 1 - t), base + t)
            self.got(z <= 2 - t, hold(z + 1 + t), base + 3 + t)

    def line_direct(self, at, first, base):
        dp, sub, z, _ = place()
        w = lax.rem(dp, 4)
        for k in range(1, 4):
            where = (lax.rem(z + k, 4) * 4 + w, sub)
            self.go(None, first, at(z), base + k - 1, base + k - 1, where)
        yield
        for k in range(1, 4):
            self.got(None, at(lax.rem(z + 4 - k, 4)), base + k - 1)

    def ring_direct(self, blk, first, base, after):
        dp, sub, z, q = place()
        src = first if first is not None else blk(0, None)
        for k in range(1, 4):
            self.go(None, src, blk(0, None), base + k - 1, base + k - 1, (ring_dp(z, q + k), sub))
        yield
        for k in range(1, 4):
            self.got(None, blk(4 - k, None), base + k - 1)
            after(blk(4 - k, None), 3 - k)

    def ring_gather(self, blk, first, base, after):
        dp, sub, z, q = place()
        after_me, before_me = (ring_dp(z, q + 1), sub), (ring_dp(z, q + 3), sub)
        src = first if first is not None else blk(0, None)
        self.go(None, src, blk(0, None), base, base, after_me)
        self.go(None, src, blk(0, None), base + 1, base + 1, before_me)
        yield
        self.got(None, blk(3, None), base)
        self.go(None, blk(3, 0), blk(3, 0), base + 2, base + 2, after_me)
        after(blk(3, None), 0)
        self.got(None, blk(1, None), base + 1)
        self.go(None, blk(1, 1), blk(1, 1), base + 3, base + 3, before_me)
        after(blk(1, None), 1)
        yield
        self.got(None, blk(2, 0), base + 2)
        self.got(None, blk(2, 1), base + 3)
        after(blk(2, None), 2)


def run_all(gens, starts=None):
    live = dict(enumerate(gens))
    tick = 0
    while live:
        for j in sorted(live):
            if starts is None or tick >= starts[j]:
                try:
                    next(live[j])
                except StopIteration:
                    live.pop(j)
        tick += 1


def gather_rows(own, out, send, recv, split, direct=(1, 0, 1, 1)):
    dp, sub, z, q = place()
    width = out.shape[-1]
    sib = (dp, 1 - sub)

    def first_line():
        cols = pl.ds(0, split)
        mid = split // 2
        mover = Mover(send.at[0], recv.at[0])
        at = lambda j: out.at[j, plane_of(q), sub, :, cols]

        def blk(k, h):
            ring = plane_of(q + k)
            if h is None:
                return out.at[:, ring, sub, :, cols]
            return out.at[pl.ds(2 * h, 2), ring, sub, :, cols]

        def share(ref, s):
            mover.go(None, ref, ref, 10 + s, 10, sib)

        line = mover.line_direct if direct[0] else mover.line_gather
        yield from line(at, own.at[:, cols], 0)
        share(blk(0, None), 3)
        ring = mover.ring_direct if direct[1] else mover.ring_gather
        yield from ring(blk, None, 6, share)
        yield
        arrived(out.at[:, :, 1 - sub, :, cols], recv.at[0, 10])
        mover.drain()

    def first_ring():
        cols = pl.ds(split, width - split)
        mid = (width - split) // 2
        mover = Mover(send.at[1], recv.at[1])

        def blk(k, h):
            ring = plane_of(q + k)
            if h is None:
                return out.at[z, ring, sub, :, cols]
            return out.at[z, ring, sub, :, pl.ds(split + h * mid, mid)]

        at = lambda j: out.at[j, :, sub, :, cols]

        def share(ref, s):
            mover.go(None, ref, ref, 10 + s, 10, sib)

        ring = mover.ring_direct if direct[2] else mover.ring_gather
        yield from ring(blk, own.at[:, cols], 0, lambda ref, s: None)
        share(at(z), 3)
        line = mover.line_direct if direct[3] else mover.line_gather
        yield from line(at, at(z), 4)
        for k in range(1, 4):
            share(at(lax.rem(z + k, 4)), k - 1)
        yield
        arrived(out.at[:, :, 1 - sub, :, cols], recv.at[1, 10])
        mover.drain()

    return [first_line(), first_ring()]


def mm(a, b):
    return jnp.dot(a, b, preferred_element_type=f32)


def mm_nt(a, b):
    return lax.dot_general(a, b, (((1,), (1,)), ((), ())), preferred_element_type=f32)


def mm_tn(a, b):
    return lax.dot_general(a, b, (((0,), (0,)), ((), ())), preferred_element_type=f32)


def sigmoid(v):
    return 0.5 + 0.5 * jnp.tanh(0.5 * v)


def split(v):
    high = v.astype(bf16)
    return high, (v - high.astype(f32)).astype(bf16)


def exact(a, b, dims):
    return lax.dot_general(
        a, b, (dims, ((), ())), precision=lax.Precision.HIGHEST, preferred_element_type=f32
    )


def factor_inverse(cov, block=8):
    size = cov.shape[0]
    tiles = size // 8
    row = lax.broadcasted_iota(jnp.int32, (8, size), 0)
    column = lax.broadcasted_iota(jnp.int32, (8, size), 1)
    left = [cov[8 * t : 8 * t + 8, :] for t in range(tiles)]
    right = [jnp.where(row + 8 * t == column, 1.0, 0.0) for t in range(tiles)]
    wide = lambda v: jnp.broadcast_to(v, (8, size))
    for j in range(0, size, block):
        t0, s = j // 8, j % 8
        columns = [[wide(left[t][:, j + k : j + k + 1]) for k in range(block)] for t in range(t0, tiles)]
        lefts = [wide(left[t0][s + k : s + k + 1, :]) for k in range(block)]
        rights = [wide(right[t0][s + k : s + k + 1, :]) for k in range(block)]
        entry = [[wide(columns[0][k][s + m : s + m + 1, :]) for k in range(m + 1)] for m in range(block)]
        lower = [[None] * block for _ in range(block)]
        inverses = []
        for k in range(block):
            inverse = 1.0 / entry[k][k]
            inverses.append(inverse)
            for m in range(k + 1, block):
                lower[m][k] = entry[m][k] * inverse
            for m in range(k + 1, block):
                for n in range(k + 1, m + 1):
                    entry[m][n] = entry[m][n] - lower[m][k] * entry[n][k]
        for m in range(block):
            for k in range(m):
                lefts[m] = lefts[m] - lower[m][k] * lefts[k]
                rights[m] = rights[m] - lower[m][k] * rights[k]
        scaled_left = [a * b for a, b in zip(lefts, inverses)]
        scaled_right = [a * b for a, b in zip(rights, inverses)]
        for t in range(t0, tiles):
            if t == t0 and s + block == 8 and block == 1:
                continue
            own = columns[t - t0]
            for m in range(block):
                for k in range(m):
                    own[m] = own[m] - lower[m][k] * own[k]
            for m in range(block):
                factor = own[m]
                if t == t0:
                    factor = jnp.where(row > s + m, factor, 0.0)
                left[t] = left[t] - factor * scaled_left[m]
                right[t] = right[t] - factor * scaled_right[m]
    out = []
    for t in range(tiles):
        pivots = jnp.sum(jnp.where(row + 8 * t == column, left[t], 0.0), axis=1, keepdims=True)
        out.append(right[t] * lax.rsqrt(pivots))
    return jnp.concatenate(out, axis=0)


def fold8(v):
    rows, cols = v.shape
    return jnp.sum(v.reshape(rows // 8, 8, cols), axis=0)


def columns_of(mask, cols):
    return jnp.concatenate([mask] * (cols // 128), axis=1)


def fwd_kernel(
    images, pixel_mask, pair_row, w_reduce, w_spatial, w_expand, w_project, w_code,
    norm_reduce, norm_spatial, norm_expand, norm_project,
    pooled_out, hidden_out, dprojected_out, dcodes_out, loss_out, grad_norm_out, upstream,
    masked_out, reduced_out, act1_out, spatial_out, act2_out, normed_out, slope_out, mask, stats, sums_out,
    img, masked, wr, ws, we, wp, wc, reduced, wide, shifted, spatial, act2, normed, slope, own,
    own_proj, proj_all, same, totals, act1_turned, act2_turned, level, normal, hidden, dproj, counts,
    counts_buf, buf1, buf2, pair, plane, line,
    load, save, send, recv, gsend, grecv, hsend, hrecv,
):
    dp, sub, z, q = place()
    me = dp * 2 + sub
    inner = wr.shape[1]
    width = wr.shape[0]
    loads = [pltpu.make_async_copy(a, b, load.at[k]) for k, (a, b) in enumerate(
        [(images, img), (w_reduce, wr), (w_spatial, ws), (w_expand, we), (w_project, wp), (w_code, wc)])]
    loads[0].start()
    loads[1].start()
    greet_start()
    here = pixel_mask[...].astype(f32)
    counts[...] = jnp.broadcast_to(jnp.sum(here, axis=1, keepdims=True), (8, 128))
    for slot in range(SLOTS):
        r, c = slot // 8, slot % 8
        if c == SIDE:
            value = jnp.zeros((8, 128), f32)
        else:
            value = jnp.broadcast_to(here[:, SIDE * r + c : SIDE * r + c + 1], (8, 128))
        mask[pl.ds(8 * slot, 8), :] = value
    wide[pl.ds(0, 8), :] = jnp.zeros((8, inner), f32)
    wide[pl.ds(ROWS + 8, 8), :] = jnp.zeros((8, inner), f32)
    shifted[pl.ds(0, 64), :] = jnp.zeros((64, 3 * inner), bf16)
    shifted[pl.ds(512, 64), :] = jnp.zeros((64, 3 * inner), bf16)
    greet_wait()
    counts_buf[me] = counts[...]
    direct_start(counts_buf, send.at[0], recv.at[0])
    loads[0].wait()
    for copy in loads[2:]:
        copy.start()
    gap = jnp.zeros((8, 256), f32)

    @pl.loop(0, width // 256)
    def _(n):
        cols = pl.ds(pl.multiple_of(n * 256, 256), 256)
        for r in range(SIDE):
            rows = img[pl.ds(SIDE * r, SIDE), :, cols].astype(f32).reshape(SIDE * 8, 256)
            rows = rows * columns_of(mask[pl.ds(64 * r, 56), :], 256)
            masked[pl.ds(64 * r, 64), cols] = jnp.concatenate([rows, gap], axis=0).astype(bf16)

    saves = []

    def keep(a, b):
        copy = pltpu.make_async_copy(a, b, save.at[len(saves)])
        copy.start()
        saves.append(copy)

    keep(masked, masked_out)
    loads[1].wait()

    @pl.loop(0, inner // 256)
    def _(n):
        cols = pl.ds(pl.multiple_of(n * 256, 256), 256)
        got = mm(masked[...], wr[:, cols])
        reduced[:, cols] = got
        buf1[me, pl.ds(0, 1), cols] = jnp.sum(got, axis=0, keepdims=True)
        buf1[me, pl.ds(1, 1), cols] = jnp.sum(got * got, axis=0, keepdims=True)

    direct_start(buf1, send.at[1], recv.at[1])
    keep(reduced, reduced_out)
    pairs = jnp.broadcast_to(pair_row[...].astype(f32), (256, 256))
    same[...] = (pairs == jnp.transpose(pairs)).astype(f32)
    valid = jnp.sum(direct_finish(counts_buf, send.at[0], recv.at[0]), axis=0, keepdims=True)[:, 0:1]
    inverse_valid = 1.0 / valid

    def moments(total):
        centre = total[0:1] * inverse_valid
        return centre, lax.rsqrt(total[1:2] * inverse_valid - centre * centre + epsilon)

    def activate(src, norm, centre, scale, store):
        gain = norm[0:1, :] * scale
        bias = norm[1:2, :] - centre * gain

        @pl.loop(0, ROWS // 32)
        def _(k):
            rows = pl.ds(pl.multiple_of(k * 32, 32), 32)
            level = src[rows, :] * gain + bias
            store(k, columns_of(mask[rows, :], inner) * (level * sigmoid(level)))

    centre1, scale1 = moments(direct_finish(buf1, send.at[1], recv.at[1]))
    stats[pl.ds(0, 1), pl.ds(0, inner)] = centre1
    stats[pl.ds(1, 1), pl.ds(0, inner)] = scale1

    def store_wide(k, value):
        wide[pl.ds(pl.multiple_of(k * 32 + 8, 8), 32), :] = value
        shifted[pl.ds(pl.multiple_of(k * 32 + 64, 32), 32), pl.ds(inner, inner)] = value.astype(bf16)

    activate(reduced, norm_reduce, centre1, scale1, store_wide)

    @pl.loop(0, ROWS // 32)
    def _(k):
        for b in (0, 2):
            rows = wide[pl.ds(pl.multiple_of(k * 32 + 8 * b, 8), 32), :]
            shifted[pl.ds(pl.multiple_of(k * 32 + 64, 32), 32), pl.ds(b * inner, inner)] = rows.astype(bf16)

    loads[2].wait()

    @pl.loop(0, inner // 256)
    def _(n):
        cols = pl.ds(pl.multiple_of(n * 256, 256), 256)

        left = jnp.concatenate([shifted[pl.ds(64 * a, ROWS), :] for a in range(3)], axis=1)
        got = mm(left, ws[:, cols]) * columns_of(mask[...], 256)
        spatial[:, cols] = got
        buf2[me, pl.ds(0, 1), cols] = jnp.sum(got, axis=0, keepdims=True)
        buf2[me, pl.ds(1, 1), cols] = jnp.sum(got * got, axis=0, keepdims=True)

    direct_start(buf2, send.at[2], recv.at[2])
    keep(spatial, spatial_out)
    act1_turned[...] = jnp.transpose(wide[pl.ds(8, ROWS), :]).astype(bf16)
    keep(act1_turned, act1_out)
    centre2, scale2 = moments(direct_finish(buf2, send.at[2], recv.at[2]))
    stats[pl.ds(2, 1), pl.ds(0, inner)] = centre2
    stats[pl.ds(3, 1), pl.ds(0, inner)] = scale2

    def store_act2(k, value):
        wide[pl.ds(pl.multiple_of(k * 32 + 8, 8), 32), :] = value
        act2[pl.ds(pl.multiple_of(k * 32, 32), 32), :] = value.astype(bf16)

    activate(spatial, norm_spatial, centre2, scale2, store_act2)
    loads[3].wait()

    @pl.loop(0, width // 256)
    def _(n):
        cols = pl.ds(pl.multiple_of(n * 256, 256), 256)
        got = mm(act2[...], we[:, cols])
        normed[:, cols] = got
        pair[sub, pl.ds(0, 1), cols] = jnp.sum(got, axis=0, keepdims=True)
        pair[sub, pl.ds(1, 1), cols] = jnp.sum(got * got, axis=0, keepdims=True)

    third = tree_gen(pair, plane, line, send.at[pl.ds(3, 3)], recv.at[pl.ds(3, 3)], totals)
    next(third)
    next(third)
    act2_turned[...] = jnp.transpose(wide[pl.ds(8, ROWS), :]).astype(bf16)
    keep(act2_turned, act2_out)
    next(third)
    next(third, None)
    centre3, scale3 = moments(totals[...])
    stats[pl.ds(4, 1), :] = centre3
    stats[pl.ds(5, 1), :] = scale3
    stats[pl.ds(6, 1), :] = jnp.broadcast_to(valid, (1, width))
    stats[pl.ds(7, 1), :] = jnp.zeros((1, width), f32)
    inverse_counts = 1.0 / counts[...]

    def last_norm(cols, rows):
        gain, bias = norm_expand[pl.ds(0, 1), cols], norm_expand[pl.ds(1, 1), cols]
        n3 = (normed[rows, cols] - stats[pl.ds(4, 1), cols]) * stats[pl.ds(5, 1), cols]
        total = masked[rows, cols].astype(f32) + gain * n3 + bias
        sig = sigmoid(total)
        return n3, sig, total * sig

    @pl.loop(0, width // 256)
    def _(n):
        cols = pl.ds(pl.multiple_of(n * 256, 256), 256)
        pool = jnp.zeros((8, 256), f32)
        for k in range(SIDE):
            rows = pl.ds(64 * k, 64)
            _, _, out = last_norm(cols, rows)
            pool = pool + fold8(columns_of(mask[rows, :], 256) * out)
        own[:, cols] = pool * columns_of(inverse_counts, 256)

    def slopes(lo, hi):
        @pl.loop(lo, hi)
        def _(n):
            cols = pl.ds(pl.multiple_of(n * 256, 256), 256)
            s1 = s2 = jnp.zeros((8, 256), f32)
            for k in range(SIDE):
                rows = pl.ds(64 * k, 64)
                n3, sig, out = last_norm(cols, rows)
                slope3 = columns_of(mask[rows, :], 256) * (sig + out * (1.0 - sig))
                normed[rows, cols] = n3
                slope[rows, cols] = slope3
                s1, s2 = s1 + fold8(slope3), s2 + fold8(slope3 * n3)
            sums_out[pl.ds(0, 8), cols] = s1
            sums_out[pl.ds(8, 8), cols] = s2

    rows_all = 256
    loads[4].wait()
    loads[5].wait()
    high = own[...].astype(bf16).astype(f32)
    both_terms = jnp.concatenate([high, own[...] - high], axis=0).astype(bf16)
    proj = hidden.shape[1]

    @pl.loop(0, proj // 256)
    def _(n):
        cols = pl.ds(pl.multiple_of(n * 256, 256), 256)
        value = mm(both_terms, wp[:, cols])
        own_proj[:, cols] = value[0:8] + value[8:16]

    proj_all[z, lax.rem(dp, 4), sub] = own_proj[...]
    proj_movers = gather_rows(own_proj, proj_all, gsend, grecv, proj * 3 // 4, (1, 1, 1, 1))
    pool_movers = gather_rows(own, pooled_out, hsend, hrecv, 1536, (1, 0, 1, 1))

    def move(movers):
        for mover in movers:
            next(mover, None)

    mine = pltpu.make_async_copy(own, pooled_out.at[z, lax.rem(dp, 4), sub], load.at[0])
    mine.start()
    move(proj_movers)
    slopes(0, 3)
    move(proj_movers)
    move(pool_movers)
    slopes(3, 6)
    move(proj_movers)
    slopes(6, 8)
    keep(normed, normed_out)
    keep(slope, slope_out)
    mine.wait()
    move(proj_movers)
    move(proj_movers)
    move(pool_movers)

    share = 1.0 / rows_all

    @pl.loop(0, proj // 256)
    def _(n):
        cols = pl.ds(pl.multiple_of(n * 256, 256), 256)
        value = proj_all[:, :, :, :, cols].reshape(rows_all, 256)
        centre = jnp.sum(value, axis=0, keepdims=True) * share
        square = jnp.sum(value * value, axis=0, keepdims=True) * share
        scale = lax.rsqrt(square - centre * centre + epsilon)
        normal_here = (value - centre) * scale
        level_here = norm_project[pl.ds(0, 1), cols] * normal_here + norm_project[pl.ds(1, 1), cols]
        normal[:, cols] = normal_here
        level[:, cols] = level_here
        hidden[:, cols] = level_here * sigmoid(level_here)
        upstream[pl.ds(0, 1), cols] = scale * norm_project[pl.ds(0, 1), cols]

    keep(hidden, hidden_out)
    high, low = split(hidden[...])
    codes = mm(high, wc[...]) + mm(low, wc[...])

    centre = jnp.sum(codes, axis=0, keepdims=True) * share
    moved = codes - centre
    cov = exact(moved, moved, ((0,), (0,))) * share
    size = cov.shape[0]
    row = lax.broadcasted_iota(jnp.int32, (size, size), 0)
    column = lax.broadcasted_iota(jnp.int32, (size, size), 1)
    inverse = factor_inverse(cov + jnp.where(row == column, whiten_floor, 0.0))
    move(pool_movers)
    white = exact(moved, inverse, ((1,), (1,)))
    unit_scale = lax.rsqrt(jnp.sum(white * white, axis=1, keepdims=True) + epsilon)
    unit = white * unit_scale
    gap = 2.0 * unit - exact(same[...], unit, ((1,), (0,)))
    loss_out[...] = jnp.broadcast_to(jnp.sum(jnp.sum(gap * gap, axis=1, keepdims=True), axis=0, keepdims=True) * share, (8, 128))
    grad_white = unit_scale * (gap - unit * jnp.sum(unit * gap, axis=1, keepdims=True))
    gram = exact(grad_white, white, ((0,), (0,)))
    half = jnp.where(row > column, gram, jnp.where(row == column, 0.5 * gram, 0.0))
    both = half + jnp.transpose(half)
    grad_moved = exact(grad_white - exact(white, both, ((1,), (0,))) * share, inverse, ((1,), (0,)))
    dcodes = grad_moved - jnp.sum(grad_moved, axis=0, keepdims=True) * share
    dcodes_out[...] = dcodes

    move(pool_movers)
    high, low = split(dcodes)

    @pl.loop(0, proj // 256)
    def _(n):
        cols = pl.ds(pl.multiple_of(n * 256, 256), 256)
        right = wc[cols, :]
        grad = mm_nt(high, right) + mm_nt(low, right)
        level_here = level[:, cols]
        sig = sigmoid(level_here)
        grad = grad * (sig * (1.0 + level_here * (1.0 - sig)))
        normal_here = normal[:, cols]
        total = jnp.sum(grad, axis=0, keepdims=True)
        dot = jnp.sum(grad * normal_here, axis=0, keepdims=True)
        grad_norm_out[pl.ds(0, 1), cols] = dot
        grad_norm_out[pl.ds(1, 1), cols] = total
        dproj[:, cols] = upstream[pl.ds(0, 1), cols] * (grad - (total + normal_here * dot) * share)

    keep(dproj, dprojected_out)
    for mover in pool_movers:
        for _ in mover:
            pass
    mine = dproj[pl.ds(pl.multiple_of(me * 8, 8), 8), :]
    high = mine.astype(bf16).astype(f32)
    both_terms = jnp.concatenate([high, mine - high], axis=0).astype(bf16)

    @pl.loop(0, width // 256)
    def _(n):
        cols = pl.ds(pl.multiple_of(n * 256, 256), 256)
        value = mm_nt(both_terms, wp[cols, :])
        upstream[:, cols] = (value[0:8] + value[8:16]) * columns_of(inverse_counts, 256)

    for copy in saves:
        copy.wait()


def forward(
    images, pixel_mask, pair_row, w_reduce, w_spatial, w_expand, w_project, w_code,
    norm_reduce, norm_spatial, norm_expand, norm_project,
):
    width, inner = w_reduce.shape
    proj, code = w_code.shape
    hbm = pl.BlockSpec(memory_space=pl.ANY)
    vmem = pl.BlockSpec(memory_space=pltpu.VMEM)
    shape = jax.ShapeDtypeStruct
    return pl.pallas_call(
        fwd_kernel,
        out_shape=[
            shape((4, 4, 2, 8, width), f32),
            shape((256, proj), f32),
            shape((256, proj), f32),
            shape((256, code), f32),
            shape((8, 128), f32),
            shape((2, proj), f32),
            shape((8, width), f32),
            shape((ROWS, width), bf16),
            shape((ROWS, inner), f32),
            shape((inner, ROWS), bf16),
            shape((ROWS, inner), f32),
            shape((inner, ROWS), bf16),
            shape((ROWS, width), f32),
            shape((ROWS, width), f32),
            shape((ROWS, 128), f32),
            shape((8, width), f32),
            shape((16, width), f32),
        ],
        in_specs=[hbm, vmem, vmem, hbm, hbm, hbm, hbm, hbm, vmem, vmem, vmem, vmem],
        out_specs=[hbm, hbm, hbm, vmem, vmem, vmem, vmem] + [hbm] * 7 + [vmem] * 3,
        scratch_shapes=[
            pltpu.VMEM((49, 8, width), bf16),
            pltpu.VMEM((ROWS, width), bf16),
            pltpu.VMEM((width, inner), bf16),
            pltpu.VMEM((9 * inner, inner), bf16),
            pltpu.VMEM((inner, width), bf16),
            pltpu.VMEM((width, proj), bf16),
            pltpu.VMEM((proj, code), bf16),
            pltpu.VMEM((ROWS, inner), f32),
            pltpu.VMEM((ROWS + 16, inner), f32),
            pltpu.VMEM((ROWS + 128, 3 * inner), bf16),
            pltpu.VMEM((ROWS, inner), f32),
            pltpu.VMEM((ROWS, inner), bf16),
            pltpu.VMEM((ROWS, width), f32),
            pltpu.VMEM((ROWS, width), f32),
            pltpu.VMEM((8, width), f32),
            pltpu.VMEM((8, proj), f32),
            pltpu.VMEM((4, 4, 2, 8, proj), f32),
            pltpu.VMEM((256, 256), f32),
            pltpu.VMEM((2, width), f32),
            pltpu.VMEM((inner, ROWS), bf16),
            pltpu.VMEM((inner, ROWS), bf16),
            pltpu.VMEM((256, proj), f32),
            pltpu.VMEM((256, proj), f32),
            pltpu.VMEM((256, proj), f32),
            pltpu.VMEM((256, proj), f32),
            pltpu.VMEM((8, 128), f32),
            pltpu.VMEM((32, 8, 128), f32),
            pltpu.VMEM((32, 2, inner), f32),
            pltpu.VMEM((32, 2, inner), f32),
            pltpu.VMEM((2, 2, width), f32),
            pltpu.VMEM((4, 2, width), f32),
            pltpu.VMEM((4, 2, width), f32),
            pltpu.SemaphoreType.DMA((6,)),
            pltpu.SemaphoreType.DMA((10,)),
            pltpu.SemaphoreType.DMA((6,)),
            pltpu.SemaphoreType.DMA((6,)),
            pltpu.SemaphoreType.DMA((2, 14)),
            pltpu.SemaphoreType.DMA((2, 14)),
            pltpu.SemaphoreType.DMA((2, 14)),
            pltpu.SemaphoreType.DMA((2, 14)),
        ],
        compiler_params=pltpu.CompilerParams(
            collective_id=20, has_side_effects=True, vmem_limit_bytes=58 << 20
        ),
    )(
        images, pixel_mask, pair_row, w_reduce, w_spatial, w_expand, w_project, w_code,
        norm_reduce, norm_spatial, norm_expand, norm_project,
    )


def halves(ref, h):
    cols = ref.shape[1] // 2
    return ref.at[:, pl.ds(h * cols, cols)]


class Job:
    def __init__(self, ring_first, rows, acc, other, land, scratch, send, recv, free):
        self.ring_first, self.rows, self.acc, self.other = ring_first, rows, acc, other
        self.land, self.scratch, self.free = land, scratch, free
        self.mover = Mover(send, recv)
        self.taken = 0

    def take(self, rows):
        ref = rows_at(self.scratch, self.taken, rows)
        self.taken += rows
        return ref

    def ring_reduce(self, base, block):
        dp, sub, z, q = place()
        go, got = self.mover.go, self.mover.got
        after_me, before_me = (ring_dp(z, q + 1), sub), (ring_dp(z, q + 3), sub)
        r0 = self.take(block)
        r1a, r1b = self.take(block), self.take(block)

        def blk(k):
            return rows_at(self.land, base + lax.rem(q + k, 4) * block, block)

        go(None, halves(blk(2), 0), halves(r0, 0), 1, 1, after_me)
        go(None, halves(blk(2), 1), halves(r0, 1), 2, 2, before_me)
        yield
        got(None, halves(r0, 0), 1)
        add_into(halves(blk(1), 0), halves(r0, 0), block)
        go(None, blk(1), r1a, 3, 3, after_me)
        got(None, halves(r0, 1), 2)
        add_into(halves(blk(3), 1), halves(r0, 1), block)
        go(None, blk(3), r1b, 4, 4, before_me)
        yield
        got(None, r1a, 3)
        got(None, r1b, 4)
        add_into(blk(0), r1a, block, r1b)

    def line_reduce(self, base, chunk):
        dp, sub, z, _ = place()
        go, got = self.mover.go, self.mover.got
        up, down = (dp + 4, sub), (dp - 4, sub)
        low = [self.take(chunk) for _ in range(3)]
        high = [self.take(chunk) for _ in range(3)]

        def at(j):
            return rows_at(self.land, base + jnp.clip(j, 0, 3) * chunk, chunk)

        for t in range(3):
            go(z <= t, at(3 + z - t), low[t], 5 + t, 5 + t, up)
            go(z >= 3 - t, at(z - 3 + t), high[t], 8 + t, 8 + t, down)
            yield
            got(
                jnp.logical_and(z >= 1, z <= t + 1),
                low[t],
                5 + t,
                lambda: add_into(at(2 + z - t), low[t], chunk),
            )
            got(
                jnp.logical_and(z <= 2, z >= 2 - t),
                high[t],
                8 + t,
                lambda: add_into(at(z - 2 + t), high[t], chunk),
            )

    def run(self):
        dp, sub, z, q = place()
        sib = (dp, 1 - sub)
        mover, acc, rows = self.mover, self.acc, self.rows
        mover.go(None, self.other, self.land, 0, 0, sib)
        yield
        mover.got(None, self.land, 0)
        add_into(self.land, acc, rows)
        big, small = rows // 4, rows // 16

        def hand_over():
            mover.settle(0)
            pl.semaphore_signal(self.free, inc=1, device_id=dev(*sib), device_id_type=MESH)

        def total(start):
            copy_into(rows_at(acc, start, small), rows_at(self.land, start, small), small)

        def share(ref, k):
            mover.go(None, ref, ref, 21 + k, 21, sib)

        if self.ring_first:
            yield from self.ring_reduce(0, big)
            hand_over()
            yield from self.line_reduce(q * big, small)
            total(q * big + z * small)
            at = lambda j: rows_at(acc, q * big + j * small, small)
            yield from mover.line_gather(at, None, 11)
            pl.semaphore_wait(self.free, 1)
            share(rows_at(acc, q * big, big), 3)

            def blk(k, h):
                ref = rows_at(acc, lax.rem(q + k, 4) * big, big)
                return ref if h is None else halves(ref, h)

            yield from mover.ring_gather(blk, None, 17, share)
        else:
            yield from self.line_reduce(0, big)
            hand_over()
            yield from self.ring_reduce(z * big, small)
            total(z * big + q * small)

            def blk(k, h):
                ref = rows_at(acc, z * big + lax.rem(q + k, 4) * small, small)
                return ref if h is None else halves(ref, h)

            yield from mover.ring_gather(blk, None, 17, lambda ref, k: None)
            pl.semaphore_wait(self.free, 1)
            share(rows_at(acc, z * big, big), 3)
            at = lambda j: rows_at(acc, j * big, big)
            yield from mover.line_gather(at, None, 11)
            for k in range(1, 4):
                share(rows_at(acc, lax.rem(z + k, 4) * big, big), k - 1)
        yield
        arrived(self.other, mover.recv.at[21])
        mover.drain()


JOB_SEMS = 25


def add_into(dst, src, rows, more=None):
    step = 16 if rows % 16 == 0 else 8

    @pl.loop(0, rows // step)
    def _(k):
        at = pl.ds(pl.multiple_of(k * step, 8), step)
        value = dst[at, :] + src[at, :]
        dst[at, :] = value if more is None else value + more[at, :]


def copy_into(dst, src, rows):
    @pl.loop(0, rows // 8)
    def _(k):
        at = pl.ds(pl.multiple_of(k * 8, 8), 8)
        dst[at, :] = src[at, :]


def rows_at(ref, start, size):
    return ref.at[pl.ds(pl.multiple_of(start, 8), size)]


def landing_rows(ring_first, rows):
    big, small = rows // 4, rows // 16
    return 3 * big + 6 * small if ring_first else 3 * small + 6 * big


JOBS = (
    (2, 0, 256, 0, 768, True),
    (2, 0, 256, 768, 256, False),
    (2, 0, 256, 1024, 768, True),
    (2, 0, 256, 1792, 256, False),
    (0, 0, 512, 0, 512, True),
    (0, 512, 256, 0, 512, False),
    (0, 768, 512, 0, 512, True),
    (0, 1280, 256, 0, 512, False),
    (0, 1536, 512, 0, 512, True),
    (0, 2048, 256, 0, 512, False),
    (1, 0, 384, 0, 512, True),
    (1, 384, 128, 0, 512, False),
    (1, 512, 384, 0, 512, True),
    (1, 896, 128, 0, 512, False),
)

ORDER = (
    -1, -2, 1, 0, -3, 1, 3, 2, 0, 3, 1, 2, 3, 0, -4, 1, 3, -5, 9, 0, 1, 8, 2, 0,
    5, 9, 4, 8, 7, 3, 5, 1, 0, 4, 9, -6, 1, 8, 5, 2, 6, 3, 9, 2, 1, 0, 4, 5,
    -7, -8, 2, 13, 0, 6, 12, 1, 10, 4, 5, 2, 3, 12, 7, 0, 1, 4, 5, 2, 10, 13, 11, 7,
    5, 12, 3, 1, 2, 9, 13, 5, 4, 7, 0, 10, 9, 4, 12, 6, 5, 4, 13, 0, 12, 11, 3, 8,
    7, 5, 13, 4, 12, 3, 5, 11, 6, 2, 12, 3, 10, 8, 13, 4, 11, 12, 7, 6, 10, 2, 8, 12,
    1, 6, 10, 9, 11, 8, 13, 6, 7, 4, 10, 9, 8, 7, 6, 13, 11, 12, 10, 8, 11, 6, 5, 7,
    9, 8, 11, 6, 12, 9, 10, 7, 10, 13, 8, 11, 9, 9, 2, 0, 11, 11, 6, 1, 13, 4, 7, 9,
    -9, 10, 13, 3, 12, 8, 6, 8, 7, 11, 6, 10, 2, 13, 12, 0, 10, 4, 13, 11, 7, 3, 5,
)


VM = 42


def back_kernel(
    upstream, masked_in, reduced_in, act1_in, spatial_in, act2_in, normed_in, slope_in, mask, stats, sums_in,
    w_reduce, w_spatial, w_expand, norm_reduce, norm_spatial, norm_expand,
    dsum, gs, gr, big, grad_norm_reduce, grad_norm_spatial, grad_norm_expand,
    wr, ws, we, masked, reduced, act1, spatial, act2, dexp, level, wide, shifted, dred,
    land_s, land_r, land_e, *rest,
):
    scratches = rest[: len(JOBS)]
    buf5, buf6, pair, plane, line, load, send, recv, jsend, jrecv, jfree = rest[len(JOBS) :]
    dp, sub, z, q = place()
    me = dp * 2 + sub
    width, inner = wr.shape
    normed = big.at[pl.ds(0, ROWS)]
    loads = {}
    for k, (name, a, b) in enumerate(
        [
            ("slope", slope_in, dsum),
            ("normed", normed_in, normed),
            ("we", w_expand, we),
            ("act2", act2_in, act2),
            ("spatial", spatial_in, spatial),
            ("ws", w_spatial, ws),
            ("act1", act1_in, act1),
            ("reduced", reduced_in, reduced),
            ("masked", masked_in, masked),
            ("wr", w_reduce, wr),
        ]
    ):
        loads[name] = pltpu.make_async_copy(a, b, load.at[k])
        loads[name].start()
    greet_start()

    def third_norm():
        @pl.loop(0, width // 512)
        def _(n):
            cols = pl.ds(pl.multiple_of(n * 512, 512), 512)
            up = upstream[:, cols]
            pair[sub, pl.ds(0, 1), cols] = jnp.sum(up * sums_in[pl.ds(0, 8), cols], axis=0, keepdims=True)
            pair[sub, pl.ds(1, 1), cols] = jnp.sum(up * sums_in[pl.ds(8, 8), cols], axis=0, keepdims=True)

        wide[pl.ds(0, 8), :] = jnp.zeros((8, inner), f32)
        wide[pl.ds(ROWS + 8, 8), :] = jnp.zeros((8, inner), f32)
        shifted[pl.ds(0, 64), :] = jnp.zeros((64, 3 * inner), bf16)
        shifted[pl.ds(512, 64), :] = jnp.zeros((64, 3 * inner), bf16)
        greet_wait()
        third = tree_gen(pair, plane, line, send, recv, grad_norm_expand)
        next(third)
        loads["slope"].wait()

        def scale_slope(lo, hi):
            @pl.loop(lo, hi)
            def _(n):
                cols = pl.ds(pl.multiple_of(n * 256, 256), 256)
                up = upstream[:, cols]
                for k in range(SLOTS // 8):
                    rows = pl.ds(64 * k, 64)
                    value = dsum[rows, cols].reshape(8, 8, 256) * up[None]
                    dsum[rows, cols] = value.reshape(64, 256)

        parts = width // 256
        scale_slope(0, parts // 4)
        next(third)
        scale_slope(parts // 4, parts * 5 // 8)
        next(third)
        scale_slope(parts * 5 // 8, parts)
        loads["normed"].wait()
        loads["we"].wait()
        loads["act2"].wait()
        next(third, None)
        share = 1.0 / stats[pl.ds(6, 1), :]
        plane[0, pl.ds(0, 1), :] = grad_norm_expand[pl.ds(0, 1), :] * share
        plane[0, pl.ds(1, 1), :] = grad_norm_expand[pl.ds(1, 1), :] * share
        plane[1, pl.ds(0, 1), :] = norm_expand[pl.ds(0, 1), :] * stats[pl.ds(5, 1), :]
        first_row = grad_norm_expand[pl.ds(0, 1), :]
        grad_norm_expand[pl.ds(0, 1), :] = grad_norm_expand[pl.ds(1, 1), :]
        grad_norm_expand[pl.ds(1, 1), :] = first_row

        @pl.loop(0, width // 256)
        def _(n):
            cols = pl.ds(pl.multiple_of(n * 256, 256), 256)
            total, dot = plane[0, pl.ds(0, 1), cols], plane[0, pl.ds(1, 1), cols]
            gain = plane[1, pl.ds(0, 1), cols]
            for k in range(SLOTS // 8):
                rows = pl.ds(64 * k, 64)
                value = dsum[rows, cols] - total - normed[rows, cols] * dot
                dexp[rows, cols] = (columns_of(mask[rows, :], 256) * (value * gain)).astype(bf16)

    def slope_pass(values, source, norm, at, buf):
        centre, scale = stats[pl.ds(at, 1), pl.ds(0, inner)], stats[pl.ds(at + 1, 1), pl.ds(0, inner)]

        def block(k, carry):
            s1, s2 = carry
            rows = pl.ds(pl.multiple_of(k * 32, 32), 32)
            normal = (source[rows, :] - centre) * scale
            point = norm[pl.ds(0, 1), :] * normal + norm[pl.ds(1, 1), :]
            sig = sigmoid(point)
            value = columns_of(mask[rows, :], inner) * values[rows, :] * (sig * (1.0 + point * (1.0 - sig)))
            values[rows, :] = value
            return s1 + fold8(value), s2 + fold8(value * normal)

        zero = jnp.zeros((8, inner), f32)
        s1, s2 = lax.fori_loop(0, ROWS // 32, block, (zero, zero))
        buf[me, pl.ds(0, 1), :] = jnp.sum(s1, axis=0, keepdims=True)
        buf[me, pl.ds(1, 1), :] = jnp.sum(s2, axis=0, keepdims=True)

    def norm_pass(values, source, norm, at, total, grad_norm, store):
        centre, scale = stats[pl.ds(at, 1), pl.ds(0, inner)], stats[pl.ds(at + 1, 1), pl.ds(0, inner)]
        share = 1.0 / stats[pl.ds(6, 1), pl.ds(0, inner)]
        grad_norm[pl.ds(0, 1), :] = total[1:2]
        grad_norm[pl.ds(1, 1), :] = total[0:1]
        gain = norm[pl.ds(0, 1), :] * scale
        mean, dot = total[0:1] * share, total[1:2] * share

        @pl.loop(0, ROWS // 32)
        def _(k):
            rows = pl.ds(pl.multiple_of(k * 32, 32), 32)
            normal = (source[rows, :] - centre) * scale
            value = values[rows, :] - mean - normal * dot
            store(k, columns_of(mask[rows, :], inner) * (value * gain))

    def expand_weights():
        @pl.loop(0, width // 256)
        def _(n):
            cols = pl.ds(pl.multiple_of(n * 256, 256), 256)
            big[:, cols] = mm(act2[...], dexp[:, cols])

    def spatial_level():
        loads["spatial"].wait()

        @pl.loop(0, inner // 256)
        def _(n):
            cols = pl.ds(pl.multiple_of(n * 256, 256), 256)
            level[:, cols] = mm_nt(dexp[...], we[cols, :])

        slope_pass(level, spatial, norm_spatial, 2, buf5)
        direct_start(buf5, send.at[3], recv.at[3])

    def spatial_norm():
        total = direct_finish(buf5, send.at[3], recv.at[3])

        def store(k, value):
            wide[pl.ds(pl.multiple_of(k * 32 + 8, 8), 32), :] = value
            shifted[pl.ds(pl.multiple_of(k * 32 + 64, 32), 32), pl.ds(inner, inner)] = value.astype(bf16)

        norm_pass(level, spatial, norm_spatial, 2, total, grad_norm_spatial, store)

        @pl.loop(0, ROWS // 32)
        def _(k):
            for b in (0, 2):
                rows = wide[pl.ds(pl.multiple_of(k * 32 + 16 - 8 * b, 8), 32), :]
                shifted[pl.ds(pl.multiple_of(k * 32 + 64, 32), 32), pl.ds(b * inner, inner)] = rows.astype(bf16)

    def spatial_weights():
        loads["act1"].wait()

        @pl.loop(0, 9)
        def _(tap):
            rows = pl.ds(pl.multiple_of(128 - 64 * (tap // 3), 64), ROWS)
            right = shifted[rows, pl.ds(pl.multiple_of(lax.rem(tap, 3) * inner, inner), inner)]
            gs[pl.ds(pl.multiple_of(tap * inner, inner), inner), :] = mm(act1[...], right)

    def reduce_level():
        loads["ws"].wait()
        loads["reduced"].wait()

        @pl.loop(0, inner // 256)
        def _(n):
            cols = pl.ds(pl.multiple_of(n * 256, 256), 256)

            left = jnp.concatenate([shifted[pl.ds(128 - 64 * a, ROWS), :] for a in range(3)], axis=1)
            right = [ws[pl.ds(pl.multiple_of(tap * inner + n * 256, 256), 256), :] for tap in range(9)]
            level[:, cols] = mm_nt(left, jnp.concatenate(right, axis=1))

        slope_pass(level, reduced, norm_reduce, 0, buf6)
        direct_start(buf6, send.at[4], recv.at[4])

    def reduce_norm():
        total = direct_finish(buf6, send.at[4], recv.at[4])

        def store(k, value):
            dred[pl.ds(pl.multiple_of(k * 32, 32), 32), :] = value.astype(bf16)

        norm_pass(level, reduced, norm_reduce, 0, total, grad_norm_reduce, store)

    def reduce_weights():
        loads["masked"].wait()

        @pl.loop(0, width // 256)
        def _(n):
            cols = pl.ds(pl.multiple_of(n * 256, 256), 256)
            gr[cols, :] = mm_tn(masked[:, cols], dred[...])

    def image_values():
        loads["wr"].wait()

        @pl.loop(0, width // 256)
        def _(n):
            cols = pl.ds(pl.multiple_of(n * 256, 256), 256)
            value = dsum[:, cols] + mm_nt(dred[...], wr[cols, :])
            dsum[:, cols] = value * columns_of(mask[...], 256)


    grads = (gs, gr, big)
    lands = (land_s, land_r, land_e)

    def make_job(j):
        k, r0, rows, c0, cols, ring_first = JOBS[j]
        half = grads[k].shape[0] // 2

        def cut(ref, base):
            return ref.at[pl.ds(pl.multiple_of(base + r0, 8), rows), pl.ds(c0, cols)]

        return Job(
            ring_first,
            rows,
            cut(grads[k], sub * half),
            cut(grads[k], (1 - sub) * half),
            cut(lands[k], 0),
            scratches[j],
            jsend.at[j],
            jrecv.at[j],
            jfree.at[j],
        ).run()

    steps = (
        third_norm, expand_weights, spatial_level, spatial_norm, spatial_weights,
        reduce_level, reduce_norm, reduce_weights, image_values,
    )
    jobs = [make_job(j) for j in range(len(JOBS))]
    for item in ORDER:
        if item < 0:
            steps[-1 - item]()
        else:
            next(jobs[item], None)
    for job in jobs:
        for _ in job:
            pass


def backward(
    upstream, masked, reduced, act1, spatial, act2, normed, slope, mask, stats, sums,
    w_reduce, w_spatial, w_expand, norm_reduce, norm_spatial, norm_expand,
):
    width, inner = w_reduce.shape
    hbm = pl.BlockSpec(memory_space=pl.ANY)
    vmem = pl.BlockSpec(memory_space=pltpu.VMEM)
    shape = jax.ShapeDtypeStruct
    landings = [
        pltpu.VMEM((landing_rows(ring_first, rows), cols), f32) for _, _, rows, _, cols, ring_first in JOBS
    ]
    return pl.pallas_call(
        back_kernel,
        out_shape=[
            pltpu.VMEM((ROWS, width), f32),
            pltpu.VMEM((9 * inner, inner), f32),
            pltpu.VMEM((width, inner), f32),
            pltpu.VMEM((inner, width), f32),
            pltpu.VMEM((2, inner), f32),
            pltpu.VMEM((2, inner), f32),
            pltpu.VMEM((2, width), f32),
        ],
        in_specs=[vmem] + [hbm] * 7 + [vmem] * 3 + [hbm] * 3 + [vmem] * 3,
        out_specs=[vmem] * 7,
        scratch_shapes=[
            pltpu.VMEM((width, inner), bf16),
            pltpu.VMEM((9 * inner, inner), bf16),
            pltpu.VMEM((inner, width), bf16),
            pltpu.VMEM((ROWS, width), bf16),
            pltpu.VMEM((ROWS, inner), f32),
            pltpu.VMEM((inner, ROWS), bf16),
            pltpu.VMEM((ROWS, inner), f32),
            pltpu.VMEM((inner, ROWS), bf16),
            pltpu.VMEM((ROWS, width), bf16),
            pltpu.VMEM((ROWS, inner), f32),
            pltpu.VMEM((ROWS + 16, inner), f32),
            pltpu.VMEM((ROWS + 128, 3 * inner), bf16),
            pltpu.VMEM((ROWS, inner), bf16),
            pltpu.VMEM((9 * inner // 2, inner), f32),
            pltpu.VMEM((width // 2, inner), f32),
            pltpu.VMEM((inner // 2, width), f32),
            *landings,
            pltpu.VMEM((32, 2, inner), f32),
            pltpu.VMEM((32, 2, inner), f32),
            pltpu.VMEM((2, 2, width), f32),
            pltpu.VMEM((4, 2, width), f32),
            pltpu.VMEM((4, 2, width), f32),
            pltpu.SemaphoreType.DMA((10,)),
            pltpu.SemaphoreType.DMA((5,)),
            pltpu.SemaphoreType.DMA((5,)),
            pltpu.SemaphoreType.DMA((len(JOBS), JOB_SEMS)),
            pltpu.SemaphoreType.DMA((len(JOBS), JOB_SEMS)),
            pltpu.SemaphoreType.REGULAR((len(JOBS),)),
        ],
        compiler_params=pltpu.CompilerParams(
            collective_id=21, has_side_effects=True, vmem_limit_bytes=VM << 20
        ),
    )(
        upstream, masked, reduced, act1, spatial, act2, normed, slope, mask, stats, sums,
        w_reduce, w_spatial, w_expand, norm_reduce, norm_spatial, norm_expand,
    )


def finish_kernel(
    loss, n1, n2, n3, n4, g1, g2, g3, g4, loss_out, o1, o2, o3, o4, h1, h2, h3, h4, sems
):
    copies = [
        pltpu.make_async_copy(g1.at[pl.ds(64 * r, 56)], h1.at[pl.ds(56 * r, 56)], sems.at[r]) for r in range(SIDE)
    ]
    for k, (a, b) in enumerate([(g2, h2), (g3, h3), (g4, h4)]):
        part = a.shape[0] // 4
        for i in range(4):
            at = pl.ds(part * i, part)
            copies.append(pltpu.make_async_copy(a.at[at], b.at[at], sems.at[SIDE + 4 * k + i]))
    for copy in copies:
        copy.start()
    loss_out[...] = loss[pl.ds(0, 1), pl.ds(0, 1)]
    o1[...] = n1[...]
    o2[...] = n2[...]
    o3[...] = n3[...]
    o4[...] = n4[...]
    for copy in copies:
        copy.wait()


def finish(loss, norms, grads):
    width = grads[0].shape[1]
    hbm = pl.BlockSpec(memory_space=pl.ANY)
    vmem = pl.BlockSpec(memory_space=pltpu.VMEM)
    shape = jax.ShapeDtypeStruct
    return pl.pallas_call(
        finish_kernel,
        out_shape=[shape((1, 1), f32)]
        + [shape(x.shape, f32) for x in norms]
        + [shape((392, width), f32)]
        + [shape(x.shape, f32) for x in grads[1:]],
        in_specs=[vmem] * 9,
        out_specs=[vmem] * 5 + [hbm] * 4,
        scratch_shapes=[pltpu.SemaphoreType.DMA((SIDE + 12,))],
        compiler_params=pltpu.CompilerParams(vmem_limit_bytes=4 << 20),
    )(loss, *norms, *grads)


def project_kernel(
    pooled_in, dproj, hidden, dcodes, grad_project, grad_code, pooled, terms, result, load, save
):
    rows, proj = dproj.shape
    loads = pltpu.make_async_copy(pooled_in, pooled, load)
    loads.start()
    a, b = split(dproj[...])
    terms[pl.ds(0, rows), :] = a
    terms[pl.ds(rows, rows), :] = a
    terms[pl.ds(2 * rows, rows), :] = b
    loads.wait()

    def block(m):
        at = pl.ds(pl.multiple_of(m * 256, 256), 256)
        return pltpu.make_async_copy(result.at[at], grad_project.at[at], save.at[m])

    @pl.loop(0, result.shape[0] // 256)
    def _(m):
        at = pl.ds(pl.multiple_of(m * 256, 256), 256)
        a, b = split(pooled[:, at])
        left = jnp.concatenate([a, b, a], axis=0)
        for n in range(proj // 256):
            cols = pl.ds(256 * n, 256)
            result[at, cols] = mm_tn(left, terms[:, cols])
        block(m).start()

    a, b = split(hidden[...])
    c, d = split(dcodes[...])
    grad_code[...] = mm_tn(jnp.concatenate([a, b, a], axis=0), jnp.concatenate([c, c, d], axis=0))
    for m in range(result.shape[0] // 256):
        block(m).wait()


def project_weights(pooled, dproj, hidden, dcodes):
    rows, width = pooled.shape
    proj, code = hidden.shape[1], dcodes.shape[1]
    hbm = pl.BlockSpec(memory_space=pl.ANY)
    vmem = pl.BlockSpec(memory_space=pltpu.VMEM)
    shape = jax.ShapeDtypeStruct
    return pl.pallas_call(
        project_kernel,
        out_shape=[shape((width, proj), f32), shape((proj, code), f32)],
        in_specs=[hbm] + [vmem] * 3,
        out_specs=[hbm, vmem],
        scratch_shapes=[
            pltpu.VMEM((rows, width), f32),
            pltpu.VMEM((3 * rows, proj), bf16),
            pltpu.VMEM((width, proj), f32),
            pltpu.SemaphoreType.DMA,
            pltpu.SemaphoreType.DMA((width // 256,)),
        ],
        compiler_params=pltpu.CompilerParams(vmem_limit_bytes=60 << 20),
    )(pooled, dproj, hidden, dcodes)


def whiten(codes, pairing):
    highest = lax.Precision.HIGHEST
    total = codes.shape[0]
    centre = jnp.sum(codes, axis=0) / total
    moved = codes - centre
    covariance = jnp.dot(moved.T, moved, precision=highest) / total
    covariance = covariance + whiten_floor * jnp.eye(codes.shape[1], dtype=jnp.float32)
    factor = jnp.linalg.cholesky(covariance)
    inverse = lax.linalg.triangular_solve(factor, jnp.eye(codes.shape[1], dtype=jnp.float32), left_side=True, lower=True)
    white = jnp.dot(moved, inverse.T, precision=highest)
    scale = lax.rsqrt(jnp.sum(white * white, axis=1, keepdims=True) + epsilon)
    unit = white * scale
    same = (pairing[:, None] == pairing[None, :]).astype(jnp.float32)
    gap = 2.0 * unit - jnp.dot(same, unit, precision=highest)
    loss_value = jnp.sum(gap * gap) / total
    grad_unit = 0.5 * (2.0 * gap - jnp.dot(same, gap, precision=highest))
    grad_white = scale * grad_unit - white * scale * scale * scale * jnp.sum(white * grad_unit, axis=1, keepdims=True)
    gram = jnp.dot(grad_white.T, white, precision=highest)
    row = lax.broadcasted_iota(jnp.int32, gram.shape, 0)
    column = lax.broadcasted_iota(jnp.int32, gram.shape, 1)
    lower = jnp.where(row > column, gram, jnp.where(row == column, 0.5 * gram, 0.0))
    both = lower + lower.T
    grad_moved = jnp.dot(grad_white - jnp.dot(white, both, precision=highest) / total, inverse, precision=highest)
    return loss_value, grad_moved - jnp.sum(grad_moved, axis=0) / total


def silu_slope(values):
    sigmoid_value = jax.nn.sigmoid(values)
    return sigmoid_value * (1.0 + values * (1.0 - sigmoid_value))


def moments(sum_value, sum_square, total_count):
    centre = sum_value / total_count
    return (centre, lax.rsqrt(sum_square / total_count - centre * centre + epsilon))


def make_columns(activation):
    images_here, pixel_count, inner_width = activation.shape
    grid_map = activation.reshape(images_here, SIDE, SIDE, inner_width)
    padded = jnp.pad(grid_map, ((0, 0), (1, 1), (1, 1), (0, 0)))
    pieces = [
        padded[:, tap_row : tap_row + SIDE, tap_col : tap_col + SIDE, :]
        for tap_row in range(3)
        for tap_col in range(3)
    ]
    return jnp.concatenate(pieces, axis=3).reshape(images_here * pixel_count, 9 * inner_width)


def fold_columns(columns, images_here, inner_width):
    tap_grads = columns.reshape(images_here, SIDE, SIDE, 9, inner_width)
    padded = jnp.zeros((images_here, SIDE + 2, SIDE + 2, inner_width), jnp.float32)
    for tap_row in range(3):
        for tap_col in range(3):
            padded = padded.at[:, tap_row : tap_row + SIDE, tap_col : tap_col + SIDE, :].add(
                tap_grads[:, :, :, 3 * tap_row + tap_col, :]
            )
    return padded[:, 1 : SIDE + 1, 1 : SIDE + 1, :].reshape(images_here, SIDE * SIDE, inner_width)


def pixel_sums(values, weight):
    return (jnp.sum(values * weight, axis=(0, 1)), jnp.sum(values * values * weight, axis=(0, 1)))


def front(
    masked_low,
    weight,
    counts,
    w_reduce,
    w_spatial,
    w_expand,
    norm_reduce,
    norm_spatial,
    norm_expand,
):
    images_here, pixel_count, width = masked_low.shape
    inner_width = w_reduce.shape[1]
    rows_here = images_here * pixel_count
    reduced = jnp.dot(
        masked_low.reshape(rows_here, width), w_reduce, preferred_element_type=jnp.float32
    ).reshape(images_here, pixel_count, inner_width)
    sum_reduce, square_reduce = pixel_sums(reduced, weight)
    sum_reduce, square_reduce, valid_total = lax.psum((sum_reduce, square_reduce, jnp.sum(counts)), ("dp", "sub"))
    centre_reduce, scale_reduce = moments(sum_reduce, square_reduce, valid_total)
    normed_reduce = (reduced - centre_reduce) * scale_reduce
    level_reduce = norm_reduce[0] * normed_reduce + norm_reduce[1]
    act_reduce = (weight * jax.nn.silu(level_reduce)).astype(jnp.bfloat16)
    columns = make_columns(act_reduce)
    spatial = jnp.dot(
        columns, w_spatial.reshape(9 * inner_width, inner_width), preferred_element_type=jnp.float32
    ).reshape(images_here, pixel_count, inner_width)
    sum_spatial, square_spatial = pixel_sums(spatial, weight)
    sum_spatial, square_spatial = lax.psum((sum_spatial, square_spatial), ("dp", "sub"))
    centre_spatial, scale_spatial = moments(sum_spatial, square_spatial, valid_total)
    normed_spatial = (spatial - centre_spatial) * scale_spatial
    level_spatial = norm_spatial[0] * normed_spatial + norm_spatial[1]
    act_spatial = (weight * jax.nn.silu(level_spatial)).astype(jnp.bfloat16)
    expanded = jnp.dot(
        act_spatial.reshape(rows_here, inner_width), w_expand, preferred_element_type=jnp.float32
    ).reshape(images_here, pixel_count, width)
    sum_expand, square_expand = pixel_sums(expanded, weight)
    sum_expand, square_expand = lax.psum((sum_expand, square_expand), ("dp", "sub"))
    centre_expand, scale_expand = moments(sum_expand, square_expand, valid_total)
    normed_expand = (expanded - centre_expand) * scale_expand
    summed = masked_low.astype(jnp.float32) + norm_expand[0] * normed_expand + norm_expand[1]
    stats = (
        valid_total,
        centre_reduce,
        scale_reduce,
        centre_spatial,
        scale_spatial,
        centre_expand,
        scale_expand,
    )
    return (
        (
            normed_reduce,
            level_reduce,
            columns,
            normed_spatial,
            level_spatial,
            act_spatial,
            normed_expand,
            summed,
        ),
        stats,
    )


def norm_back(upstream, normed, gain, scale_value, sum_grad, dot_grad, total_count):
    return gain * scale_value * (upstream - (sum_grad + normed * dot_grad) / total_count)


def plain_shards(
    images,
    pixel_mask,
    pairing,
    w_reduce,
    w_spatial,
    w_expand,
    w_project,
    w_code,
    norm_reduce,
    norm_spatial,
    norm_expand,
    norm_project,
):
    images_here, pixel_count, width = images.shape
    inner_width = w_reduce.shape[1]
    images_total = pairing.shape[0]
    rows_here = images_here * pixel_count
    highest = lax.Precision.HIGHEST
    weight = pixel_mask.astype(jnp.float32)[:, :, None]
    counts = jnp.sum(weight, axis=1)
    masked_low = images * weight.astype(jnp.bfloat16)
    project_full = w_project.astype(jnp.float32)
    code_full = w_code.astype(jnp.float32)
    saved, stats = front(
        masked_low,
        weight,
        counts,
        w_reduce,
        w_spatial,
        w_expand,
        norm_reduce,
        norm_spatial,
        norm_expand,
    )
    (
        normed_reduce,
        level_reduce,
        columns,
        normed_spatial,
        level_spatial,
        act_spatial,
        normed_expand,
        summed,
    ) = saved
    (
        valid_total,
        centre_reduce,
        scale_reduce,
        centre_spatial,
        scale_spatial,
        centre_expand,
        scale_expand,
    ) = stats
    output = weight * jax.nn.silu(summed)
    own_pooled = jnp.sum(output, axis=1) / counts
    pooled = lax.all_gather(own_pooled, ("dp", "sub"), axis=0, tiled=True)
    projected = jnp.dot(pooled, project_full, precision=highest)
    centre_project, scale_project = moments(
        jnp.sum(projected, axis=0), jnp.sum(projected * projected, axis=0), float(images_total)
    )
    normed_project = (projected - centre_project) * scale_project
    level_project = norm_project[0] * normed_project + norm_project[1]
    hidden = jax.nn.silu(level_project)
    codes = jnp.dot(hidden, code_full, precision=highest)
    loss_value, grad_codes = whiten(codes, pairing)
    grad_w_code = jnp.dot(hidden.T, grad_codes, precision=highest)
    grad_hidden = jnp.dot(grad_codes, code_full.T, precision=highest)
    grad_level_project = grad_hidden * silu_slope(level_project)
    sum_project_grad = jnp.sum(grad_level_project, axis=0)
    dot_project_grad = jnp.sum(grad_level_project * normed_project, axis=0)
    grad_norm_project = jnp.stack([dot_project_grad, sum_project_grad])
    grad_projected = norm_back(
        grad_level_project,
        normed_project,
        norm_project[0],
        scale_project,
        sum_project_grad,
        dot_project_grad,
        float(images_total),
    )
    grad_w_project = jnp.dot(pooled.T, grad_projected, precision=highest)
    own_start = lax.axis_index(("dp", "sub")) * images_here
    own_projected = lax.dynamic_slice_in_dim(grad_projected, own_start, images_here, 0)
    grad_pooled = jnp.dot(own_projected, project_full.T, precision=highest)
    grad_summed = weight * (grad_pooled / counts)[:, None, :] * silu_slope(summed)
    sum_expand_grad, dot_expand_grad = lax.psum(
        (jnp.sum(grad_summed, axis=(0, 1)), jnp.sum(grad_summed * normed_expand, axis=(0, 1))), ("dp", "sub")
    )
    grad_norm_expand = jnp.stack([dot_expand_grad, sum_expand_grad])
    grad_expanded = (
        (
            weight
            * norm_back(
                grad_summed,
                normed_expand,
                norm_expand[0],
                scale_expand,
                sum_expand_grad,
                dot_expand_grad,
                valid_total,
            )
        )
        .astype(jnp.bfloat16)
        .reshape(rows_here, width)
    )
    grad_w_expand = jnp.einsum(
        "rm,rc->mc",
        act_spatial.reshape(rows_here, inner_width),
        grad_expanded,
        preferred_element_type=jnp.float32,
    )
    grad_act_spatial = jnp.einsum(
        "rc,mc->rm", grad_expanded, w_expand, preferred_element_type=jnp.float32
    ).reshape(images_here, pixel_count, inner_width)
    grad_level_spatial = grad_act_spatial * weight * silu_slope(level_spatial)
    sum_spatial_grad, dot_spatial_grad = lax.psum(
        (
            jnp.sum(grad_level_spatial, axis=(0, 1)),
            jnp.sum(grad_level_spatial * normed_spatial, axis=(0, 1)),
        ),
        ("dp", "sub"),
    )
    grad_norm_spatial = jnp.stack([dot_spatial_grad, sum_spatial_grad])
    grad_spatial_out = (
        (
            weight
            * norm_back(
                grad_level_spatial,
                normed_spatial,
                norm_spatial[0],
                scale_spatial,
                sum_spatial_grad,
                dot_spatial_grad,
                valid_total,
            )
        )
        .astype(jnp.bfloat16)
        .reshape(rows_here, inner_width)
    )
    grad_w_spatial = jnp.einsum(
        "rk,rm->km", columns, grad_spatial_out, preferred_element_type=jnp.float32
    ).reshape(3, 3, inner_width, inner_width)
    grad_columns = jnp.einsum(
        "rm,km->rk",
        grad_spatial_out,
        w_spatial.reshape(9 * inner_width, inner_width),
        preferred_element_type=jnp.float32,
    )
    grad_act_reduce = fold_columns(grad_columns, images_here, inner_width)
    grad_level_reduce = grad_act_reduce * weight * silu_slope(level_reduce)
    sum_reduce_grad, dot_reduce_grad = lax.psum(
        (
            jnp.sum(grad_level_reduce, axis=(0, 1)),
            jnp.sum(grad_level_reduce * normed_reduce, axis=(0, 1)),
        ),
        ("dp", "sub"),
    )
    grad_norm_reduce = jnp.stack([dot_reduce_grad, sum_reduce_grad])
    grad_reduced = (
        (
            weight
            * norm_back(
                grad_level_reduce,
                normed_reduce,
                norm_reduce[0],
                scale_reduce,
                sum_reduce_grad,
                dot_reduce_grad,
                valid_total,
            )
        )
        .astype(jnp.bfloat16)
        .reshape(rows_here, inner_width)
    )
    grad_w_reduce = jnp.einsum(
        "rc,rm->cm",
        masked_low.reshape(rows_here, width),
        grad_reduced,
        preferred_element_type=jnp.float32,
    )
    grad_input = jnp.einsum(
        "rm,cm->rc", grad_reduced, w_reduce, preferred_element_type=jnp.float32
    ).reshape(images_here, pixel_count, width)
    grad_images = weight * (grad_summed + grad_input)
    grad_w_spatial, grad_w_reduce, grad_w_expand = lax.psum(
        (grad_w_spatial, grad_w_reduce, grad_w_expand), ("dp", "sub")
    )
    return (
        loss_value,
        grad_images,
        grad_w_reduce,
        grad_w_spatial.reshape(3, 3, inner_width, inner_width),
        grad_w_expand,
        grad_w_project,
        grad_w_code,
        grad_norm_reduce,
        grad_norm_spatial,
        grad_norm_expand,
        grad_norm_project,
    )


def shards(
    images,
    pixel_mask,
    pairing,
    w_reduce,
    w_spatial,
    w_expand,
    w_project,
    w_code,
    norm_reduce,
    norm_spatial,
    norm_expand,
    norm_project,
):
    width, inner = w_reduce.shape
    taps = w_spatial.reshape(9 * inner, inner)
    (
        pooled, hidden, dprojected, dcodes, loss, grad_norm_project, upstream,
        masked, reduced, act1, spatial, act2, normed, slope, mask, stats, sums,
    ) = forward(
        jnp.transpose(images, (1, 0, 2)),
        pixel_mask,
        pairing.reshape(1, 256),
        w_reduce,
        taps,
        w_expand,
        w_project,
        w_code,
        norm_reduce,
        norm_spatial,
        norm_expand,
        norm_project,
    )
    (
        grad_images, grad_spatial, grad_reduce, grad_expand,
        grad_norm_reduce, grad_norm_spatial, grad_norm_expand,
    ) = backward(
        upstream, masked, reduced, act1, spatial, act2, normed, slope, mask, stats, sums,
        w_reduce, taps, w_expand, norm_reduce, norm_spatial, norm_expand,
    )
    grad_project, grad_code = project_weights(pooled.reshape(256, width), dprojected, hidden, dcodes)
    (
        loss, grad_norm_reduce, grad_norm_spatial, grad_norm_expand, grad_norm_project,
        grad_images, grad_spatial, grad_reduce, grad_expand,
    ) = finish(
        loss,
        (grad_norm_reduce, grad_norm_spatial, grad_norm_expand, grad_norm_project),
        (grad_images, grad_spatial, grad_reduce, grad_expand),
    )
    return (
        loss[0, 0],
        jnp.transpose(grad_images.reshape(49, 8, width), (1, 0, 2)),
        grad_reduce,
        grad_spatial.reshape(w_spatial.shape),
        grad_expand,
        grad_project,
        grad_code,
        grad_norm_reduce,
        grad_norm_spatial,
        grad_norm_expand,
        grad_norm_project,
    )


def solution(mesh):
    fits = mesh.shape["dp"] == 16 and mesh.shape["sub"] == 2
    placed = (P(("dp", "sub"), None, None), P(("dp", "sub"), None)) + (P(),) * 10
    return jax.shard_map(
        shards if fits else plain_shards,
        mesh=mesh,
        in_specs=placed,
        out_specs=(P(), P(("dp", "sub"), None, None)) + (P(),) * 9,
        check_vma=False,
    )
```

```python
import functools
import jax
import jax.numpy as jnp
from jax import lax
from jax.experimental import pallas as pl
from jax.experimental.pallas import tpu as pltpu
from jax.sharding import PartitionSpec as P

MESH = pl.DeviceIdType.MESH
SIDE = 7
SLOTS = 56
ROWS = 448
epsilon = 1e-05
whiten_floor = 0.001
f32 = jnp.float32
bf16 = jnp.bfloat16


def place():
    dp = lax.axis_index("dp")
    sub = lax.axis_index("sub")
    z = dp // 4
    y = lax.rem(dp // 2, 2)
    x = lax.rem(dp, 2)
    ring = 3 * y + x - 2 * x * y
    return dp, sub, z, ring


def plane_of(ring):
    ring = lax.rem(ring + 4, 4)
    y = ring // 2
    odd = lax.rem(ring, 2)
    return y * 2 + odd + y - 2 * odd * y


def ring_dp(z, ring):
    return z * 4 + plane_of(ring)


def dev(dp, sub):
    return {"dp": dp, "sub": sub}


def greet_start():
    dp, sub, _, _ = place()
    me = dp * 2 + sub
    barrier = pltpu.get_barrier_semaphore()

    @pl.loop(1, 32)
    def _(step):
        other = lax.rem(me + step, 32)
        pl.semaphore_signal(
            barrier, inc=1, device_id=dev(other // 2, lax.rem(other, 2)), device_id_type=MESH
        )


def greet_wait():
    pl.semaphore_wait(pltpu.get_barrier_semaphore(), 31)


def remote(src, dst, send, recv, where):
    return pltpu.make_async_remote_copy(
        src_ref=src,
        dst_ref=dst,
        send_sem=send,
        recv_sem=recv,
        device_id=dev(*where),
        device_id_type=MESH,
    )


def arrived(ref, sem):
    pltpu.make_async_copy(ref, ref, sem).wait()


def direct_start(buf, send, recv):
    dp, sub, _, _ = place()
    me = dp * 2 + sub

    @pl.loop(1, 32)
    def _(step):
        other = lax.rem(me + step, 32)
        remote(buf.at[me], buf.at[me], send, recv, (other // 2, lax.rem(other, 2))).start()


def direct_finish(buf, send, recv):
    many = buf.at[pl.ds(0, 31)]
    arrived(many, recv)
    total = jnp.sum(buf[...], axis=0)
    arrived(many, send)
    return total


def tree_gen(pair, plane, line, send, recv, result):
    dp, sub, z, _ = place()
    w = lax.rem(dp, 4)
    remote(pair.at[sub], pair.at[sub], send.at[0], recv.at[0], (dp, 1 - sub)).start()
    yield
    arrived(pair.at[0], recv.at[0])
    plane[w] = pair[0] + pair[1]
    for k in range(1, 4):
        where = (z * 4 + lax.rem(w + k, 4), sub)
        remote(plane.at[w], plane.at[w], send.at[1], recv.at[1], where).start()
    yield
    arrived(plane.at[pl.ds(0, 3)], recv.at[1])
    line[z] = (plane[0] + plane[1]) + (plane[2] + plane[3])
    for k in range(1, 4):
        where = (lax.rem(z + k, 4) * 4 + w, sub)
        remote(line.at[z], line.at[z], send.at[2], recv.at[2], where).start()
    yield
    arrived(line.at[pl.ds(0, 3)], recv.at[2])
    result[...] = (line[0] + line[1]) + (line[2] + line[3])
    arrived(pair.at[0], send.at[0])
    arrived(plane.at[pl.ds(0, 3)], send.at[1])
    arrived(line.at[pl.ds(0, 3)], send.at[2])


class Mover:
    def __init__(self, send, recv):
        self.send, self.recv, self.pending = send, recv, []

    def go(self, cond, src, dst, s, r, where):
        def body():
            remote(src, dst, self.send.at[s], self.recv.at[r], where).start()

        if cond is None:
            body()
        else:
            pl.when(cond)(body)
        self.pending.append((cond, src, s))

    def got(self, cond, ref, r, then=None):
        def body():
            arrived(ref, self.recv.at[r])
            if then is not None:
                then()

        if cond is None:
            body()
        else:
            pl.when(cond)(body)

    def drain(self):
        for cond, ref, s in self.pending:

            def body(ref=ref, s=s):
                arrived(ref, self.send.at[s])

            if cond is None:
                body()
            else:
                pl.when(cond)(body)
        self.pending = []

    def settle(self, s):
        for cond, ref, other in self.pending:
            if other == s:
                arrived(ref, self.send.at[s])
        self.pending = [item for item in self.pending if item[2] != s]

    def line_gather(self, at, first, base):
        dp, sub, z, _ = place()
        up, down = (dp + 4, sub), (dp - 4, sub)
        hold = lambda j: at(jnp.clip(j, 0, 3))
        for t in range(3):
            from_up = first if t == 0 and first is not None else hold(z - t)
            from_down = first if t == 0 and first is not None else hold(z + t)
            self.go(jnp.logical_and(z <= 2, z >= t), from_up, hold(z - t), base + t, base + t, up)
            self.go(
                jnp.logical_and(z >= 1, z <= 3 - t),
                from_down,
                hold(z + t),
                base + 3 + t,
                base + 3 + t,
                down,
            )
            yield
            self.got(z >= t + 1, hold(z - 1 - t), base + t)
            self.got(z <= 2 - t, hold(z + 1 + t), base + 3 + t)

    def line_direct(self, at, first, base):
        dp, sub, z, _ = place()
        w = lax.rem(dp, 4)
        for k in range(1, 4):
            where = (lax.rem(z + k, 4) * 4 + w, sub)
            self.go(None, first, at(z), base + k - 1, base + k - 1, where)
        yield
        for k in range(1, 4):
            self.got(None, at(lax.rem(z + 4 - k, 4)), base + k - 1)

    def ring_direct(self, blk, first, base, after):
        dp, sub, z, q = place()
        src = first if first is not None else blk(0, None)
        for k in range(1, 4):
            self.go(None, src, blk(0, None), base + k - 1, base + k - 1, (ring_dp(z, q + k), sub))
        yield
        for k in range(1, 4):
            self.got(None, blk(4 - k, None), base + k - 1)
            after(blk(4 - k, None), 3 - k)

    def ring_gather(self, blk, first, base, after):
        dp, sub, z, q = place()
        after_me, before_me = (ring_dp(z, q + 1), sub), (ring_dp(z, q + 3), sub)
        src = first if first is not None else blk(0, None)
        self.go(None, src, blk(0, None), base, base, after_me)
        self.go(None, src, blk(0, None), base + 1, base + 1, before_me)
        yield
        self.got(None, blk(3, None), base)
        self.go(None, blk(3, 0), blk(3, 0), base + 2, base + 2, after_me)
        after(blk(3, None), 0)
        self.got(None, blk(1, None), base + 1)
        self.go(None, blk(1, 1), blk(1, 1), base + 3, base + 3, before_me)
        after(blk(1, None), 1)
        yield
        self.got(None, blk(2, 0), base + 2)
        self.got(None, blk(2, 1), base + 3)
        after(blk(2, None), 2)


def run_all(gens, starts=None):
    live = dict(enumerate(gens))
    tick = 0
    while live:
        for j in sorted(live):
            if starts is None or tick >= starts[j]:
                try:
                    next(live[j])
                except StopIteration:
                    live.pop(j)
        tick += 1


def gather_rows(own, out, send, recv, split, direct=(1, 0, 1, 1)):
    dp, sub, z, q = place()
    width = out.shape[-1]
    sib = (dp, 1 - sub)

    def first_line():
        cols = pl.ds(0, split)
        mid = split // 2
        mover = Mover(send.at[0], recv.at[0])
        at = lambda j: out.at[j, plane_of(q), sub, :, cols]

        def blk(k, h):
            ring = plane_of(q + k)
            if h is None:
                return out.at[:, ring, sub, :, cols]
            return out.at[pl.ds(2 * h, 2), ring, sub, :, cols]

        def share(ref, s):
            mover.go(None, ref, ref, 10 + s, 10, sib)

        line = mover.line_direct if direct[0] else mover.line_gather
        yield from line(at, own.at[:, cols], 0)
        share(blk(0, None), 3)
        ring = mover.ring_direct if direct[1] else mover.ring_gather
        yield from ring(blk, None, 6, share)
        yield
        arrived(out.at[:, :, 1 - sub, :, cols], recv.at[0, 10])
        mover.drain()

    def first_ring():
        cols = pl.ds(split, width - split)
        mid = (width - split) // 2
        mover = Mover(send.at[1], recv.at[1])

        def blk(k, h):
            ring = plane_of(q + k)
            if h is None:
                return out.at[z, ring, sub, :, cols]
            return out.at[z, ring, sub, :, pl.ds(split + h * mid, mid)]

        at = lambda j: out.at[j, :, sub, :, cols]

        def share(ref, s):
            mover.go(None, ref, ref, 10 + s, 10, sib)

        ring = mover.ring_direct if direct[2] else mover.ring_gather
        yield from ring(blk, own.at[:, cols], 0, lambda ref, s: None)
        share(at(z), 3)
        line = mover.line_direct if direct[3] else mover.line_gather
        yield from line(at, at(z), 4)
        for k in range(1, 4):
            share(at(lax.rem(z + k, 4)), k - 1)
        yield
        arrived(out.at[:, :, 1 - sub, :, cols], recv.at[1, 10])
        mover.drain()

    return [first_line(), first_ring()]


def mm(a, b):
    return jnp.dot(a, b, preferred_element_type=f32)


def mm_nt(a, b):
    return lax.dot_general(a, b, (((1,), (1,)), ((), ())), preferred_element_type=f32)


def mm_tn(a, b):
    return lax.dot_general(a, b, (((0,), (0,)), ((), ())), preferred_element_type=f32)


def sigmoid(v):
    return 0.5 + 0.5 * jnp.tanh(0.5 * v)


def split(v):
    high = v.astype(bf16)
    return high, (v - high.astype(f32)).astype(bf16)


def exact(a, b, dims):
    return lax.dot_general(
        a, b, (dims, ((), ())), precision=lax.Precision.HIGHEST, preferred_element_type=f32
    )


def factor_inverse(cov, block=8):
    size = cov.shape[0]
    tiles = size // 8
    row = lax.broadcasted_iota(jnp.int32, (8, size), 0)
    column = lax.broadcasted_iota(jnp.int32, (8, size), 1)
    left = [cov[8 * t : 8 * t + 8, :] for t in range(tiles)]
    right = [jnp.where(row + 8 * t == column, 1.0, 0.0) for t in range(tiles)]
    wide = lambda v: jnp.broadcast_to(v, (8, size))
    for j in range(0, size, block):
        t0, s = j // 8, j % 8
        columns = [[wide(left[t][:, j + k : j + k + 1]) for k in range(block)] for t in range(t0, tiles)]
        lefts = [wide(left[t0][s + k : s + k + 1, :]) for k in range(block)]
        rights = [wide(right[t0][s + k : s + k + 1, :]) for k in range(block)]
        entry = [[wide(columns[0][k][s + m : s + m + 1, :]) for k in range(m + 1)] for m in range(block)]
        lower = [[None] * block for _ in range(block)]
        inverses = []
        for k in range(block):
            inverse = 1.0 / entry[k][k]
            inverses.append(inverse)
            for m in range(k + 1, block):
                lower[m][k] = entry[m][k] * inverse
            for m in range(k + 1, block):
                for n in range(k + 1, m + 1):
                    entry[m][n] = entry[m][n] - lower[m][k] * entry[n][k]
        for m in range(block):
            for k in range(m):
                lefts[m] = lefts[m] - lower[m][k] * lefts[k]
                rights[m] = rights[m] - lower[m][k] * rights[k]
        scaled_left = [a * b for a, b in zip(lefts, inverses)]
        scaled_right = [a * b for a, b in zip(rights, inverses)]
        for t in range(t0, tiles):
            if t == t0 and s + block == 8 and block == 1:
                continue
            own = columns[t - t0]
            for m in range(block):
                for k in range(m):
                    own[m] = own[m] - lower[m][k] * own[k]
            for m in range(block):
                factor = own[m]
                if t == t0:
                    factor = jnp.where(row > s + m, factor, 0.0)
                left[t] = left[t] - factor * scaled_left[m]
                right[t] = right[t] - factor * scaled_right[m]
    out = []
    for t in range(tiles):
        pivots = jnp.sum(jnp.where(row + 8 * t == column, left[t], 0.0), axis=1, keepdims=True)
        out.append(right[t] * lax.rsqrt(pivots))
    return jnp.concatenate(out, axis=0)


def fold8(v):
    rows, cols = v.shape
    return jnp.sum(v.reshape(rows // 8, 8, cols), axis=0)


def columns_of(mask, cols):
    return jnp.concatenate([mask] * (cols // 128), axis=1)


def halves(ref, h):
    cols = ref.shape[1] // 2
    return ref.at[:, pl.ds(h * cols, cols)]


class Job:
    def __init__(self, ring_first, rows, acc, other, land, scratch, send, recv, free):
        self.ring_first, self.rows, self.acc, self.other = ring_first, rows, acc, other
        self.land, self.scratch, self.free = land, scratch, free
        self.mover = Mover(send, recv)
        self.taken = 0

    def take(self, rows):
        ref = rows_at(self.scratch, self.taken, rows)
        self.taken += rows
        return ref

    def ring_reduce(self, base, block):
        dp, sub, z, q = place()
        go, got = self.mover.go, self.mover.got
        after_me, before_me = (ring_dp(z, q + 1), sub), (ring_dp(z, q + 3), sub)
        r0 = self.take(block)
        r1a, r1b = self.take(block), self.take(block)

        def blk(k):
            return rows_at(self.land, base + lax.rem(q + k, 4) * block, block)

        go(None, halves(blk(2), 0), halves(r0, 0), 1, 1, after_me)
        go(None, halves(blk(2), 1), halves(r0, 1), 2, 2, before_me)
        yield
        got(None, halves(r0, 0), 1)
        add_into(halves(blk(1), 0), halves(r0, 0), block)
        go(None, blk(1), r1a, 3, 3, after_me)
        got(None, halves(r0, 1), 2)
        add_into(halves(blk(3), 1), halves(r0, 1), block)
        go(None, blk(3), r1b, 4, 4, before_me)
        yield
        got(None, r1a, 3)
        got(None, r1b, 4)
        add_into(blk(0), r1a, block, r1b)

    def line_reduce(self, base, chunk):
        dp, sub, z, _ = place()
        go, got = self.mover.go, self.mover.got
        up, down = (dp + 4, sub), (dp - 4, sub)
        low = [self.take(chunk) for _ in range(3)]
        high = [low[0], self.take(chunk), self.take(chunk)]

        def at(j):
            return rows_at(self.land, base + jnp.clip(j, 0, 3) * chunk, chunk)

        for t in range(3):
            go(z <= t, at(3 + z - t), low[t], 5 + t, 5 + t, up)
            go(z >= 3 - t, at(z - 3 + t), high[t], 8 + t, 8 + t, down)
            yield
            got(
                jnp.logical_and(z >= 1, z <= t + 1),
                low[t],
                5 + t,
                lambda: add_into(at(2 + z - t), low[t], chunk),
            )
            got(
                jnp.logical_and(z <= 2, z >= 2 - t),
                high[t],
                8 + t,
                lambda: add_into(at(z - 2 + t), high[t], chunk),
            )

    def run(self):
        dp, sub, z, q = place()
        sib = (dp, 1 - sub)
        mover, acc, rows = self.mover, self.acc, self.rows
        mover.go(None, self.other, self.land, 0, 0, sib)
        yield
        mover.got(None, self.land, 0)
        add_into(self.land, acc, rows)
        big, small = rows // 4, rows // 16

        def hand_over():
            mover.settle(0)
            pl.semaphore_signal(self.free, inc=1, device_id=dev(*sib), device_id_type=MESH)

        def total(start):
            copy_into(rows_at(acc, start, small), rows_at(self.land, start, small), small)

        def share(ref, k):
            mover.go(None, ref, ref, 21 + k, 21, sib)

        if self.ring_first:
            yield from self.ring_reduce(0, big)
            hand_over()
            yield from self.line_reduce(q * big, small)
            total(q * big + z * small)
            at = lambda j: rows_at(acc, q * big + j * small, small)
            yield from mover.line_gather(at, None, 11)
            pl.semaphore_wait(self.free, 1)
            share(rows_at(acc, q * big, big), 3)

            def blk(k, h):
                ref = rows_at(acc, lax.rem(q + k, 4) * big, big)
                return ref if h is None else halves(ref, h)

            yield from mover.ring_gather(blk, None, 17, share)
        else:
            yield from self.line_reduce(0, big)
            hand_over()
            yield from self.ring_reduce(z * big, small)
            total(z * big + q * small)

            def blk(k, h):
                ref = rows_at(acc, z * big + lax.rem(q + k, 4) * small, small)
                return ref if h is None else halves(ref, h)

            yield from mover.ring_gather(blk, None, 17, lambda ref, k: None)
            pl.semaphore_wait(self.free, 1)
            share(rows_at(acc, z * big, big), 3)
            at = lambda j: rows_at(acc, j * big, big)
            yield from mover.line_gather(at, None, 11)
            for k in range(1, 4):
                share(rows_at(acc, lax.rem(z + k, 4) * big, big), k - 1)
        yield
        arrived(self.other, mover.recv.at[21])
        mover.drain()


JOB_SEMS = 25


def add_into(dst, src, rows, more=None):
    step = 16 if rows % 16 == 0 else 8

    @pl.loop(0, rows // step)
    def _(k):
        at = pl.ds(pl.multiple_of(k * step, 8), step)
        value = dst[at, :] + src[at, :]
        dst[at, :] = value if more is None else value + more[at, :]


def copy_into(dst, src, rows):
    @pl.loop(0, rows // 8)
    def _(k):
        at = pl.ds(pl.multiple_of(k * 8, 8), 8)
        dst[at, :] = src[at, :]


def rows_at(ref, start, size):
    return ref.at[pl.ds(pl.multiple_of(start, 8), size)]


def landing_rows(ring_first, rows):
    big, small = rows // 4, rows // 16
    return 3 * big + 5 * small if ring_first else 3 * small + 5 * big


JOBS = (
    (2, 0, 256, 0, 768, True),
    (2, 0, 256, 768, 256, False),
    (2, 0, 256, 1024, 768, True),
    (2, 0, 256, 1792, 256, False),
    (0, 0, 384, 0, 512, True),
    (0, 384, 256, 0, 512, False),
    (0, 640, 384, 0, 512, True),
    (0, 1024, 128, 0, 512, False),
    (0, 1152, 384, 0, 512, True),
    (0, 1536, 256, 0, 512, False),
    (0, 1792, 384, 0, 512, True),
    (0, 2176, 128, 0, 512, False),
    (1, 0, 384, 0, 512, True),
    (1, 384, 128, 0, 512, False),
    (1, 512, 384, 0, 512, True),
    (1, 896, 128, 0, 512, False),
)

ORDER = (
    -1, 1, -2, 1, 2, -3, 2, 1, 0, 3, 0, 3, 1, 2, -4, 3, -5, 7, 5, 10, 8, 3, 0, 7,
    2, 5, -6, 10, 2, 7, 6, 1, 8, 3, 9, 5, 6, 0, 2, 7, 4, 1, 8, 3, 9, -7, 1, 10,
    -10, 2, 0, 5, -8, 14, 1, 8, 6, 12, 2, 9, -9, 3, 1, 2, 7, 8, 4, 0, 12, 9, 7, 1,
    3, 5, 14, 13, 10, -11, 0, 8, 7, 12, 3, -12, 6, 10, 1, 7, 4, 8, 3, 15, -13, 0, 13, 10,
    8, 6, 9, 2, 7, 5, 10, -14, 3, 12, 15, 13, 6, 9, 0, 14, 7, 10, 2, 4, 12, 5, -15, 15,
    8, 7, 6, 12, 9, 8, 10, 4, 13, 11, 12, 5, 4, 15, 14, 10, 6, 9, 12, 4, 11, 13, 5, 0,
    15, 14, 3, -16, 6, 11, 4, 9, 13, 12, 10, 15, 0, 11, 13, 14, 2, 8, 4, 2, 9, 13, 6, 0,
    13, 11, 14, 15, 5, 4, 9, 11, 1, -17, 8, 14, 15, 13, 1, 12, 0, 11, 15, 6, 14, 3, 5, 11,
    12, 14, 7, 10, 11, 15, 6, -18, 13, 12, 8, 5, 4, 11, 15, 6, 14, 5, 11, 12, 9, 13, 7, 4,
    9, 15, 10, 14, 4, 11, 15, 13, 14, 11,
)

VM = 43

PROJECTOR_ROWS = 12288


def step_kernel(
    images, pixel_mask, pair_row, w_reduce, w_spatial, w_expand, w_project, w_code,
    norm_reduce, norm_spatial, norm_expand, norm_project,
    pooled_out, projector, masked_out, loss_out,
    grad_norm_out, third_grad, grad_norm_reduce, grad_norm_spatial, dsum, gs, gr, big,
    img, wr, ws, we, wc, masked, reduced, spatial, act1, act2, dred, level, wide, shifted, mask, stats,
    own, own_proj, proj_all, same, codes_buf, counts, sums, totals, third_sums, upstream,
    buf1, buf2, buf5, buf6, pair, plane, line, pair4, plane4, line4, land_s, land_r, land_e, *rest,
):
    scratches = rest[: len(JOBS)]
    load, save, send, recv, gsend, grecv, hsend, hrecv, jsend, jrecv, jfree, wsem = rest[len(JOBS) :]
    dp, sub, z, q = place()
    me = dp * 2 + sub
    width, inner = wr.shape
    proj = wc.shape[0]
    normed = big.at[pl.ds(0, ROWS)]
    slope, dexp, act2_rows = dsum, masked, dred
    half_proj = proj // 2
    loads = [
        pltpu.make_async_copy(a, b, load.at[k])
        for k, (a, b) in enumerate(
            [(images, img), (w_reduce, wr), (w_spatial, ws), (w_expand, we), (w_code, wc)]
            + [
                (w_project.at[:, pl.ds(h * half_proj, half_proj)], ws.at[pl.ds(h * width, width)])
                for h in range(2)
            ]
            + [(w_spatial, ws), (masked_out, masked)]
        )
    ]

    def block(k, n):
        start = pl.multiple_of(512 * k + 256 * (n // 2), 256)
        return gr.at[pl.ds(start, 256), pl.ds(pl.multiple_of(lax.rem(n, 2) * 256, 256), 256)]

    loads[0].start()
    loads[1].start()
    greet_start()
    here = pixel_mask[...].astype(f32)
    counts[...] = jnp.broadcast_to(jnp.sum(here, axis=1, keepdims=True), (8, 128))
    for slot in range(SLOTS):
        r, c = slot // 8, slot % 8
        if c == SIDE:
            value = jnp.zeros((8, 128), f32)
        else:
            value = jnp.broadcast_to(here[:, SIDE * r + c : SIDE * r + c + 1], (8, 128))
        mask[pl.ds(8 * slot, 8), :] = value
    wide[pl.ds(0, 8), :] = jnp.zeros((8, inner), f32)
    wide[pl.ds(ROWS + 8, 8), :] = jnp.zeros((8, inner), f32)
    shifted[pl.ds(0, 64), :] = jnp.zeros((64, 3 * inner), bf16)
    shifted[pl.ds(512, 64), :] = jnp.zeros((64, 3 * inner), bf16)
    loads[0].wait()
    for copy in loads[2:5]:
        copy.start()
    gap = jnp.zeros((8, 256), f32)

    @pl.loop(0, width // 256)
    def _(n):
        cols = pl.ds(pl.multiple_of(n * 256, 256), 256)
        for r in range(SIDE):
            rows = img[pl.ds(SIDE * r, SIDE), :, cols].astype(f32).reshape(SIDE * 8, 256)
            rows = rows * columns_of(mask[pl.ds(64 * r, 56), :], 256)
            masked[pl.ds(64 * r, 64), cols] = jnp.concatenate([rows, gap], axis=0).astype(bf16)

    saves = []

    def keep(a, b):
        copy = pltpu.make_async_copy(a, b, save.at[len(saves)])
        copy.start()
        saves.append(copy)

    keep(masked, masked_out)
    loads[1].wait()

    @pl.loop(0, inner // 256)
    def _(n):
        cols = pl.ds(pl.multiple_of(n * 256, 256), 256)
        got = mm(masked[...], wr[:, cols])
        reduced[:, cols] = got
        buf1[me, pl.ds(0, 1), cols] = jnp.sum(got, axis=0, keepdims=True)
        buf1[me, pl.ds(1, 1), cols] = jnp.sum(got * got, axis=0, keepdims=True)

    extra = pl.ds(inner, 128)
    buf1[me, pl.ds(0, 1), extra] = jnp.sum(counts[...], axis=0, keepdims=True)
    buf1[me, pl.ds(1, 1), extra] = jnp.zeros((1, 128), f32)
    greet_wait()
    direct_start(buf1, send.at[1], recv.at[1])
    pairs = jnp.broadcast_to(pair_row[...].astype(f32), (256, 256))
    same[...] = (pairs == jnp.transpose(pairs)).astype(f32)
    first = direct_finish(buf1, send.at[1], recv.at[1])
    valid = first[0:1, inner : inner + 1]
    inverse_valid = 1.0 / valid

    def moments(total):
        centre = total[0:1] * inverse_valid
        return centre, lax.rsqrt(total[1:2] * inverse_valid - centre * centre + epsilon)

    def activate(src, norm, centre, scale, store):
        gain = norm[0:1, :] * scale
        bias = norm[1:2, :] - centre * gain

        @pl.loop(0, ROWS // 32)
        def _(k):
            rows = pl.ds(pl.multiple_of(k * 32, 32), 32)
            level = src[rows, :] * gain + bias
            store(k, columns_of(mask[rows, :], inner) * (level * sigmoid(level)))

    centre1, scale1 = moments(first[:, :inner])
    stats[pl.ds(0, 1), pl.ds(0, inner)] = centre1
    stats[pl.ds(1, 1), pl.ds(0, inner)] = scale1

    def store_wide(k, value):
        wide[pl.ds(pl.multiple_of(k * 32 + 8, 8), 32), :] = value
        shifted[pl.ds(pl.multiple_of(k * 32 + 64, 32), 32), pl.ds(inner, inner)] = value.astype(bf16)

    activate(reduced, norm_reduce, centre1, scale1, store_wide)

    @pl.loop(0, ROWS // 32)
    def _(k):
        for b in (0, 2):
            rows = wide[pl.ds(pl.multiple_of(k * 32 + 8 * b, 8), 32), :]
            shifted[pl.ds(pl.multiple_of(k * 32 + 64, 32), 32), pl.ds(b * inner, inner)] = rows.astype(bf16)

    loads[2].wait()

    @pl.loop(0, inner // 256)
    def _(n):
        cols = pl.ds(pl.multiple_of(n * 256, 256), 256)

        left = jnp.concatenate([shifted[pl.ds(64 * a, ROWS), :] for a in range(3)], axis=1)
        got = mm(left, ws[:, cols]) * columns_of(mask[...], 256)
        spatial[:, cols] = got
        buf2[me, pl.ds(0, 1), cols] = jnp.sum(got, axis=0, keepdims=True)
        buf2[me, pl.ds(1, 1), cols] = jnp.sum(got * got, axis=0, keepdims=True)

    direct_start(buf2, send.at[2], recv.at[2])
    loads[5].start()
    loads[6].start()
    act1[...] = jnp.transpose(wide[pl.ds(8, ROWS), :]).astype(bf16)
    centre2, scale2 = moments(direct_finish(buf2, send.at[2], recv.at[2]))
    stats[pl.ds(2, 1), pl.ds(0, inner)] = centre2
    stats[pl.ds(3, 1), pl.ds(0, inner)] = scale2

    def store_act2(k, value):
        wide[pl.ds(pl.multiple_of(k * 32 + 8, 8), 32), :] = value
        act2_rows[pl.ds(pl.multiple_of(k * 32, 32), 32), :] = value.astype(bf16)

    activate(spatial, norm_spatial, centre2, scale2, store_act2)
    loads[3].wait()

    @pl.loop(0, width // 256)
    def _(n):
        cols = pl.ds(pl.multiple_of(n * 256, 256), 256)
        got = mm(act2_rows[...], we[:, cols])
        normed[:, cols] = got
        pair[sub, pl.ds(0, 1), cols] = jnp.sum(got, axis=0, keepdims=True)
        pair[sub, pl.ds(1, 1), cols] = jnp.sum(got * got, axis=0, keepdims=True)

    third = tree_gen(pair, plane, line, send.at[pl.ds(3, 3)], recv.at[pl.ds(3, 3)], totals)
    next(third)
    next(third)
    act2[...] = jnp.transpose(wide[pl.ds(8, ROWS), :]).astype(bf16)
    next(third)
    next(third, None)
    centre3, scale3 = moments(totals[...])
    stats[pl.ds(4, 1), :] = centre3
    stats[pl.ds(5, 1), :] = scale3
    stats[pl.ds(6, 1), :] = jnp.broadcast_to(valid, (1, width))
    stats[pl.ds(7, 1), :] = jnp.zeros((1, width), f32)
    inverse_counts = 1.0 / counts[...]

    def last_norm(cols, rows):
        gain, bias = norm_expand[pl.ds(0, 1), cols], norm_expand[pl.ds(1, 1), cols]
        n3 = (normed[rows, cols] - stats[pl.ds(4, 1), cols]) * stats[pl.ds(5, 1), cols]
        total = masked[rows, cols].astype(f32) + gain * n3 + bias
        sig = sigmoid(total)
        return n3, sig, total * sig

    @pl.loop(0, width // 256)
    def _(n):
        cols = pl.ds(pl.multiple_of(n * 256, 256), 256)
        pool = jnp.zeros((8, 256), f32)
        for k in range(SIDE):
            rows = pl.ds(64 * k, 64)
            _, _, out = last_norm(cols, rows)
            pool = pool + fold8(columns_of(mask[rows, :], 256) * out)
        own[:, cols] = pool * columns_of(inverse_counts, 256)

    def slopes(lo, hi):
        @pl.loop(lo, hi)
        def _(n):
            cols = pl.ds(pl.multiple_of(n * 256, 256), 256)
            s1 = s2 = jnp.zeros((8, 256), f32)
            for k in range(SIDE):
                rows = pl.ds(64 * k, 64)
                n3, sig, out = last_norm(cols, rows)
                slope3 = columns_of(mask[rows, :], 256) * (sig + out * (1.0 - sig))
                normed[rows, cols] = n3
                slope[rows, cols] = slope3
                s1, s2 = s1 + fold8(slope3), s2 + fold8(slope3 * n3)
            sums[pl.ds(0, 8), cols] = s1
            sums[pl.ds(8, 8), cols] = s2

    rows_all = 256
    for k in (4, 5, 6):
        loads[k].wait()
    high = own[...].astype(bf16).astype(f32)
    both_terms = jnp.concatenate([high, own[...] - high], axis=0).astype(bf16)

    @pl.loop(0, proj // 256)
    def _(n):
        cols = pl.ds(pl.multiple_of(n * 256, 256), 256)
        rows = pl.ds(pl.multiple_of((n // 2) * width, 256), width)
        value = mm(both_terms, ws[rows, pl.ds(pl.multiple_of(lax.rem(n, 2) * 256, 256), 256)])
        own_proj[:, cols] = value[0:8] + value[8:16]

    proj_all[z, lax.rem(dp, 4), sub] = own_proj[...]
    proj_movers = gather_rows(own_proj, proj_all, gsend, grecv, proj * 3 // 4, (1, 1, 1, 1))
    pool_movers = gather_rows(own, pooled_out, hsend, hrecv, 1536, (1, 0, 1, 1))

    def move(movers):
        for mover in movers:
            next(mover, None)

    mine = pltpu.make_async_copy(own, pooled_out.at[z, lax.rem(dp, 4), sub], load.at[0])
    mine.start()
    move(proj_movers)
    slopes(0, 3)
    move(proj_movers)
    move(pool_movers)
    slopes(3, 6)
    move(proj_movers)
    slopes(6, 8)
    mine.wait()
    move(proj_movers)
    move(proj_movers)
    move(pool_movers)

    share = 1.0 / rows_all
    codes_buf[...] = jnp.zeros_like(codes_buf)

    @pl.loop(0, proj // 256)
    def _(n):
        cols = pl.ds(pl.multiple_of(n * 256, 256), 256)
        value = proj_all[:, :, :, :, cols].reshape(rows_all, 256)
        centre = jnp.sum(value, axis=0, keepdims=True) * share
        square = jnp.sum(value * value, axis=0, keepdims=True) * share
        scale = lax.rsqrt(square - centre * centre + epsilon)
        normal_here = (value - centre) * scale
        level_here = norm_project[pl.ds(0, 1), cols] * normal_here + norm_project[pl.ds(1, 1), cols]
        block(1, n)[...] = normal_here
        block(0, n)[...] = level_here
        value = level_here * sigmoid(level_here)
        block(2, n)[...] = value
        high, low = split(value)
        codes_buf[...] += mm(high, wc[cols, :]) + mm(low, wc[cols, :])
        upstream[pl.ds(0, 1), cols] = scale * norm_project[pl.ds(0, 1), cols]

    codes = codes_buf[...]

    centre = jnp.sum(codes, axis=0, keepdims=True) * share
    moved = codes - centre
    cov = exact(moved, moved, ((0,), (0,))) * share
    size = cov.shape[0]
    row = lax.broadcasted_iota(jnp.int32, (size, size), 0)
    column = lax.broadcasted_iota(jnp.int32, (size, size), 1)
    inverse = factor_inverse(cov + jnp.where(row == column, whiten_floor, 0.0))
    move(pool_movers)
    white = exact(moved, inverse, ((1,), (1,)))
    unit_scale = lax.rsqrt(jnp.sum(white * white, axis=1, keepdims=True) + epsilon)
    unit = white * unit_scale
    gap = 2.0 * unit - exact(same[...], unit, ((1,), (0,)))
    loss_out[...] = jnp.broadcast_to(jnp.sum(jnp.sum(gap * gap, axis=1, keepdims=True), axis=0, keepdims=True) * share, (8, 128))
    grad_white = unit_scale * (gap - unit * jnp.sum(unit * gap, axis=1, keepdims=True))
    gram = exact(grad_white, white, ((0,), (0,)))
    half = jnp.where(row > column, gram, jnp.where(row == column, 0.5 * gram, 0.0))
    both = half + jnp.transpose(half)
    grad_moved = exact(grad_white - exact(white, both, ((1,), (0,))) * share, inverse, ((1,), (0,)))
    dcodes = grad_moved - jnp.sum(grad_moved, axis=0, keepdims=True) * share

    move(pool_movers)
    high, low = split(dcodes)

    @pl.loop(0, proj // 256)
    def _(n):
        cols = pl.ds(pl.multiple_of(n * 256, 256), 256)
        right = wc[cols, :]
        grad = mm_nt(high, right) + mm_nt(low, right)
        level_here = block(0, n)[...]
        sig = sigmoid(level_here)
        grad = grad * (sig * (1.0 + level_here * (1.0 - sig)))
        normal_here = block(1, n)[...]
        total = jnp.sum(grad, axis=0, keepdims=True)
        dot = jnp.sum(grad * normal_here, axis=0, keepdims=True)
        grad_norm_out[pl.ds(0, 1), cols] = dot
        grad_norm_out[pl.ds(1, 1), cols] = total
        block(3, n)[...] = upstream[pl.ds(0, 1), cols] * (grad - (total + normal_here * dot) * share)

    move(pool_movers)
    own_rows = [gr[pl.ds(pl.multiple_of(1536 + 256 * h + me * 8, 8), 8), :] for h in range(2)]
    mine = jnp.concatenate(own_rows, axis=1)
    high = mine.astype(bf16).astype(f32)
    both_terms = jnp.concatenate([high, mine - high], axis=0).astype(bf16)

    @pl.loop(0, width // 256)
    def _(n):
        cols = pl.ds(pl.multiple_of(n * 256, 256), 256)
        value = mm_nt(both_terms[:, :half_proj], ws[cols, :])
        value = value + mm_nt(both_terms[:, half_proj:], ws[pl.ds(pl.multiple_of(width + n * 256, 256), 256), :])
        up = (value[0:8] + value[8:16]) * columns_of(inverse_counts, 256)
        upstream[:, cols] = up
        pair4[sub, pl.ds(0, 1), cols] = jnp.sum(up * sums[pl.ds(0, 8), cols], axis=0, keepdims=True)
        pair4[sub, pl.ds(1, 1), cols] = jnp.sum(up * sums[pl.ds(8, 8), cols], axis=0, keepdims=True)

    loads[7].start()
    fourth = tree_gen(pair4, plane4, line4, send.at[pl.ds(6, 3)], recv.at[pl.ds(6, 3)], third_sums)
    next(fourth)
    code_out = []
    code_high, code_low = split(dcodes)
    code_terms = jnp.concatenate([code_high, code_high, code_low], axis=0)
    for n in range(proj // 256):
        high, low = split(block(2, n)[...])
        place_at = codes_buf if n == 2 else same.at[:, pl.ds(128 * (n % 2), 128)]
        if n == 3:
            code_out[1].wait()
        place_at[...] = mm_tn(jnp.concatenate([high, low, high], axis=0), code_terms)
        code_out.append(pltpu.make_async_copy(place_at, projector.at[pl.ds(width + 256 * n, 256), pl.ds(0, codes_buf.shape[1])], save.at[1 + n]))
        code_out[n].start()
    next(fourth)
    saves.extend(code_out[k] for k in (0, 2, 3))
    for mover in pool_movers:
        for _ in mover:
            pass
    next(fourth)
    next(fourth, None)
    third_grad[pl.ds(0, 1), :] = third_sums[pl.ds(1, 1), :]
    third_grad[pl.ds(1, 1), :] = third_sums[pl.ds(0, 1), :]


    def third_part(lo, hi):
        @pl.loop(lo, hi)
        def _(n):
            cols = pl.ds(pl.multiple_of(n * 256, 256), 256)
            share = 1.0 / stats[pl.ds(6, 1), cols]
            total, dot = third_sums[pl.ds(0, 1), cols] * share, third_sums[pl.ds(1, 1), cols] * share
            gain = norm_expand[pl.ds(0, 1), cols] * stats[pl.ds(5, 1), cols]
            up = upstream[:, cols]
            for k in range(SIDE):
                rows = pl.ds(64 * k, 64)
                value = (dsum[rows, cols].reshape(8, 8, 256) * up[None]).reshape(64, 256)
                dsum[rows, cols] = value
                value = (value - total - normed[rows, cols] * dot) * gain
                dexp[rows, cols] = (columns_of(mask[rows, :], 256) * value).astype(bf16)

        @pl.loop(lo, hi)
        def _(n):
            cols = pl.ds(pl.multiple_of(n * 256, 256), 256)
            big[:, cols] = mm(act2[...], dexp[:, cols])

    def third_norm():
        for copy in saves:
            copy.wait()
        third_part(0, width // 512)

    def third_rest():
        third_part(width // 512, width // 256)

    def slope_pass(values, source, norm, at, buf):
        centre, scale = stats[pl.ds(at, 1), pl.ds(0, inner)], stats[pl.ds(at + 1, 1), pl.ds(0, inner)]

        def block(k, carry):
            s1, s2 = carry
            rows = pl.ds(pl.multiple_of(k * 32, 32), 32)
            normal = (source[rows, :] - centre) * scale
            point = norm[pl.ds(0, 1), :] * normal + norm[pl.ds(1, 1), :]
            sig = sigmoid(point)
            value = columns_of(mask[rows, :], inner) * values[rows, :] * (sig * (1.0 + point * (1.0 - sig)))
            values[rows, :] = value
            return s1 + fold8(value), s2 + fold8(value * normal)

        zero = jnp.zeros((8, inner), f32)
        s1, s2 = lax.fori_loop(0, ROWS // 32, block, (zero, zero))
        buf[me, pl.ds(0, 1), :] = jnp.sum(s1, axis=0, keepdims=True)
        buf[me, pl.ds(1, 1), :] = jnp.sum(s2, axis=0, keepdims=True)

    def norm_pass(values, source, norm, at, total, grad_norm, store):
        centre, scale = stats[pl.ds(at, 1), pl.ds(0, inner)], stats[pl.ds(at + 1, 1), pl.ds(0, inner)]
        share = 1.0 / stats[pl.ds(6, 1), pl.ds(0, inner)]
        grad_norm[pl.ds(0, 1), :] = total[1:2]
        grad_norm[pl.ds(1, 1), :] = total[0:1]
        gain = norm[pl.ds(0, 1), :] * scale
        mean, dot = total[0:1] * share, total[1:2] * share

        @pl.loop(0, ROWS // 32)
        def _(k):
            rows = pl.ds(pl.multiple_of(k * 32, 32), 32)
            normal = (source[rows, :] - centre) * scale
            value = values[rows, :] - mean - normal * dot
            store(k, columns_of(mask[rows, :], inner) * (value * gain))

    def spatial_level():

        @pl.loop(0, inner // 256)
        def _(n):
            cols = pl.ds(pl.multiple_of(n * 256, 256), 256)
            level[:, cols] = mm_nt(dexp[...], we[cols, :])

        loads[8].start()
        slope_pass(level, spatial, norm_spatial, 2, buf5)
        direct_start(buf5, send.at[9], recv.at[9])

    def spatial_norm():
        total = direct_finish(buf5, send.at[9], recv.at[9])

        def store(k, value):
            wide[pl.ds(pl.multiple_of(k * 32 + 8, 8), 32), :] = value
            shifted[pl.ds(pl.multiple_of(k * 32 + 64, 32), 32), pl.ds(inner, inner)] = value.astype(bf16)

        norm_pass(level, spatial, norm_spatial, 2, total, grad_norm_spatial, store)

        @pl.loop(0, ROWS // 32)
        def _(k):
            for b in (0, 2):
                rows = wide[pl.ds(pl.multiple_of(k * 32 + 16 - 8 * b, 8), 32), :]
                shifted[pl.ds(pl.multiple_of(k * 32 + 64, 32), 32), pl.ds(b * inner, inner)] = rows.astype(bf16)

    def spatial_weights():
        @pl.loop(0, 9)
        def _(tap):
            rows = pl.ds(pl.multiple_of(128 - 64 * (tap // 3), 64), ROWS)
            right = shifted[rows, pl.ds(pl.multiple_of(lax.rem(tap, 3) * inner, inner), inner)]
            gs[pl.ds(pl.multiple_of(tap * inner, inner), inner), :] = mm(act1[...], right)

    def reduce_level():
        loads[7].wait()

        @pl.loop(0, inner // 256)
        def _(n):
            cols = pl.ds(pl.multiple_of(n * 256, 256), 256)

            left = jnp.concatenate([shifted[pl.ds(128 - 64 * a, ROWS), :] for a in range(3)], axis=1)
            right = [ws[pl.ds(pl.multiple_of(tap * inner + n * 256, 256), 256), :] for tap in range(9)]
            level[:, cols] = mm_nt(left, jnp.concatenate(right, axis=1))

        slope_pass(level, reduced, norm_reduce, 0, buf6)
        direct_start(buf6, send.at[10], recv.at[10])

    def reduce_norm():
        total = direct_finish(buf6, send.at[10], recv.at[10])

        def store(k, value):
            dred[pl.ds(pl.multiple_of(k * 32, 32), 32), :] = value.astype(bf16)

        norm_pass(level, reduced, norm_reduce, 0, total, grad_norm_reduce, store)

    def reduce_weights():
        loads[8].wait()

        @pl.loop(0, width // 256)
        def _(n):
            cols = pl.ds(pl.multiple_of(n * 256, 256), 256)
            gr[cols, :] = mm_tn(masked[:, cols], dred[...])

    def image_values():
        @pl.loop(0, width // 256)
        def _(n):
            cols = pl.ds(pl.multiple_of(n * 256, 256), 256)
            value = dsum[:, cols] + mm_nt(dred[...], wr[cols, :])
            dsum[:, cols] = value * columns_of(mask[...], 256)


    def pooled_part(h):
        cols = pl.ds(h * half_proj * 2, half_proj * 2)
        return pltpu.make_async_copy(pooled_out.at[:, :, :, :, cols], proj_all, load.at[9 + h])

    def project_terms():
        pooled_part(0).start()
        for h in range(2):
            high, low = split(gr[pl.ds(1536 + 256 * h, 256), :])
            for k, part in enumerate((high, high, low)):
                ws[pl.ds(768 * h + 256 * k, 256), :] = part

    project_out = []

    def project_block(m):
        spare = ((level, 0), (reduced, 0)) if m % 2 == 0 else ((spatial, 0), (wide, 8))
        if m == 0:
            pooled_part(0).wait()
        if m == 4:
            pooled_part(1).start()
            pooled_part(1).wait()
        for copy in project_out[2 * m - 4 : 2 * m - 2] if m >= 2 else []:
            copy.wait()
        block_rows = proj_all[:, :, :, :, pl.ds(256 * (m % 4), 256)].reshape(256, 256)
        high, low = split(jnp.transpose(block_rows))
        left = jnp.concatenate([high, low, high], axis=1)
        for h, (ref, start) in enumerate(spare):
            ref[pl.ds(start, 256), :] = mm(left, ws[pl.ds(768 * h, 768), :])
            copy = pltpu.make_async_copy(
                ref.at[pl.ds(start, 256)],
                projector.at[pl.ds(256 * m, 256), pl.ds(512 * h, 512)],
                wsem.at[m, h],
            )
            copy.start()
            project_out.append(copy)

    grads = (gs, gr, big)
    lands = (land_s, land_r, land_e)

    def make_job(j):
        k, r0, rows, c0, cols, ring_first = JOBS[j]
        half = grads[k].shape[0] // 2

        def cut(ref, base):
            return ref.at[pl.ds(pl.multiple_of(base + r0, 8), rows), pl.ds(c0, cols)]

        return Job(
            ring_first,
            rows,
            cut(grads[k], sub * half),
            cut(grads[k], (1 - sub) * half),
            cut(lands[k], 0),
            scratches[j],
            jsend.at[j],
            jrecv.at[j],
            jfree.at[j],
        ).run()

    steps = (
        third_norm, third_rest, spatial_level, spatial_norm, spatial_weights,
        reduce_level, reduce_norm, reduce_weights, image_values, project_terms,
        *[functools.partial(project_block, m) for m in range(8)],
    )
    jobs = [make_job(j) for j in range(len(JOBS))]
    for item in ORDER:
        if item < 0:
            steps[-1 - item]()
        else:
            next(jobs[item], None)
    for job in jobs:
        for _ in job:
            pass
    for copy in project_out[-4:]:
        copy.wait()


def training_step(
    images, pixel_mask, pair_row, w_reduce, w_spatial, w_expand, w_project, w_code,
    norm_reduce, norm_spatial, norm_expand, norm_project,
):
    width, inner = w_reduce.shape
    proj, code = w_code.shape
    hbm = pl.BlockSpec(memory_space=pl.ANY)
    vmem = pl.BlockSpec(memory_space=pltpu.VMEM)
    shape = jax.ShapeDtypeStruct
    landings = [
        pltpu.VMEM((landing_rows(ring_first, rows), cols), f32) for _, _, rows, _, cols, ring_first in JOBS
    ]
    return pl.pallas_call(
        step_kernel,
        out_shape=[
            shape((4, 4, 2, 8, width), f32),
            shape((PROJECTOR_ROWS, proj), f32),
            shape((ROWS, width), bf16),
            pltpu.VMEM((8, 128), f32),
            pltpu.VMEM((2, proj), f32),
            pltpu.VMEM((2, width), f32),
            pltpu.VMEM((2, inner), f32),
            pltpu.VMEM((2, inner), f32),
            pltpu.VMEM((ROWS, width), f32),
            pltpu.VMEM((9 * inner, inner), f32),
            pltpu.VMEM((width, inner), f32),
            pltpu.VMEM((inner, width), f32),
        ],
        in_specs=[hbm, vmem, vmem] + [hbm] * 5 + [vmem] * 4,
        out_specs=[hbm] * 3 + [vmem] * 9,
        scratch_shapes=[
            pltpu.VMEM((49, 8, width), bf16),
            pltpu.VMEM((width, inner), bf16),
            pltpu.VMEM((9 * inner, inner), bf16),
            pltpu.VMEM((inner, width), bf16),
            pltpu.VMEM((proj, code), bf16),
            pltpu.VMEM((ROWS, width), bf16),
            pltpu.VMEM((ROWS, inner), f32),
            pltpu.VMEM((ROWS, inner), f32),
            pltpu.VMEM((inner, ROWS), bf16),
            pltpu.VMEM((inner, ROWS), bf16),
            pltpu.VMEM((ROWS, inner), bf16),
            pltpu.VMEM((ROWS, inner), f32),
            pltpu.VMEM((ROWS + 16, inner), f32),
            pltpu.VMEM((ROWS + 128, 3 * inner), bf16),
            pltpu.VMEM((ROWS, 128), f32),
            pltpu.VMEM((8, width), f32),
            pltpu.VMEM((8, width), f32),
            pltpu.VMEM((8, proj), f32),
            pltpu.VMEM((4, 4, 2, 8, proj), f32),
            pltpu.VMEM((256, 256), f32),
            pltpu.VMEM((256, code), f32),
            pltpu.VMEM((8, 128), f32),
            pltpu.VMEM((16, width), f32),
            pltpu.VMEM((2, width), f32),
            pltpu.VMEM((2, width), f32),
            pltpu.VMEM((8, width), f32),
            pltpu.VMEM((32, 2, inner + 128), f32),
            pltpu.VMEM((32, 2, inner), f32),
            pltpu.VMEM((32, 2, inner), f32),
            pltpu.VMEM((32, 2, inner), f32),
            pltpu.VMEM((2, 2, width), f32),
            pltpu.VMEM((4, 2, width), f32),
            pltpu.VMEM((4, 2, width), f32),
            pltpu.VMEM((2, 2, width), f32),
            pltpu.VMEM((4, 2, width), f32),
            pltpu.VMEM((4, 2, width), f32),
            pltpu.VMEM((9 * inner // 2, inner), f32),
            pltpu.VMEM((width // 2, inner), f32),
            pltpu.VMEM((inner // 2, width), f32),
            *landings,
            pltpu.SemaphoreType.DMA((11,)),
            pltpu.SemaphoreType.DMA((6,)),
            pltpu.SemaphoreType.DMA((11,)),
            pltpu.SemaphoreType.DMA((11,)),
            pltpu.SemaphoreType.DMA((2, 14)),
            pltpu.SemaphoreType.DMA((2, 14)),
            pltpu.SemaphoreType.DMA((2, 14)),
            pltpu.SemaphoreType.DMA((2, 14)),
            pltpu.SemaphoreType.DMA((len(JOBS), JOB_SEMS)),
            pltpu.SemaphoreType.DMA((len(JOBS), JOB_SEMS)),
            pltpu.SemaphoreType.REGULAR((len(JOBS),)),
            pltpu.SemaphoreType.DMA((8, 2)),
        ],
        compiler_params=pltpu.CompilerParams(
            collective_id=20, has_side_effects=True, vmem_limit_bytes=VM << 20
        ),
    )(
        images, pixel_mask, pair_row, w_reduce, w_spatial, w_expand, w_project, w_code,
        norm_reduce, norm_spatial, norm_expand, norm_project,
    )


PARTS = 2


def finish_kernel(
    projector, loss, n1, n2, n3, n4, g1, g2, g3, g4,
    project_out, code_out, loss_out, o1, o2, o3, o4, h1, h2, h3, h4,
    held, held_code, sems, load, save,
):
    steps = held.shape[0] // 256

    def through(m):
        at = pl.ds(256 * m, 256)
        return (
            pltpu.make_async_copy(projector.at[at], held.at[at], load.at[m]),
            pltpu.make_async_copy(held.at[at], project_out.at[at], save.at[m]),
        )

    pairs = [through(m) for m in range(steps)]
    pairs.append(
        (
            pltpu.make_async_copy(
                projector.at[pl.ds(held.shape[0], held_code.shape[0]), pl.ds(0, held_code.shape[1])],
                held_code,
                load.at[steps],
            ),
            pltpu.make_async_copy(held_code, code_out, save.at[steps]),
        )
    )
    for read, _ in pairs:
        read.start()
    copies = [
        pltpu.make_async_copy(g1.at[pl.ds(64 * r, 56)], h1.at[pl.ds(56 * r, 56)], sems.at[r]) for r in range(SIDE)
    ]
    for k, (a, b) in enumerate([(g2, h2), (g3, h3), (g4, h4)]):
        part = a.shape[0] // PARTS
        for i in range(PARTS):
            at = pl.ds(part * i, part)
            copies.append(pltpu.make_async_copy(a.at[at], b.at[at], sems.at[SIDE + PARTS * k + i]))
    for copy in copies:
        copy.start()
    loss_out[...] = loss[pl.ds(0, 1), pl.ds(0, 1)]
    o1[...] = n1[...]
    o2[...] = n2[...]
    o3[...] = n3[...]
    o4[...] = n4[...]
    for read, write in pairs:
        read.wait()
        write.start()
    for _, write in pairs:
        write.wait()
    for copy in copies:
        copy.wait()


def finish(projector, project, code, loss, norms, grads):
    width = grads[0].shape[1]
    hbm = pl.BlockSpec(memory_space=pl.ANY)
    vmem = pl.BlockSpec(memory_space=pltpu.VMEM)
    shape = jax.ShapeDtypeStruct
    return pl.pallas_call(
        finish_kernel,
        out_shape=[shape(project, f32), shape(code, f32), shape((1, 1), f32)]
        + [shape(x.shape, f32) for x in norms]
        + [shape((392, width), f32)]
        + [shape(x.shape, f32) for x in grads[1:]],
        in_specs=[hbm] + [vmem] * 9,
        out_specs=[hbm] * 2 + [vmem] * 5 + [hbm] * 4,
        scratch_shapes=[
            pltpu.VMEM(project, f32),
            pltpu.VMEM(code, f32),
            pltpu.SemaphoreType.DMA((SIDE + 3 * PARTS,)),
            pltpu.SemaphoreType.DMA((project[0] // 256 + 1,)),
            pltpu.SemaphoreType.DMA((project[0] // 256 + 1,)),
        ],
        compiler_params=pltpu.CompilerParams(vmem_limit_bytes=14 << 20),
    )(projector, loss, *norms, *grads)


def whiten(codes, pairing):
    highest = lax.Precision.HIGHEST
    total = codes.shape[0]
    centre = jnp.sum(codes, axis=0) / total
    moved = codes - centre
    covariance = jnp.dot(moved.T, moved, precision=highest) / total
    covariance = covariance + whiten_floor * jnp.eye(codes.shape[1], dtype=jnp.float32)
    factor = jnp.linalg.cholesky(covariance)
    inverse = lax.linalg.triangular_solve(factor, jnp.eye(codes.shape[1], dtype=jnp.float32), left_side=True, lower=True)
    white = jnp.dot(moved, inverse.T, precision=highest)
    scale = lax.rsqrt(jnp.sum(white * white, axis=1, keepdims=True) + epsilon)
    unit = white * scale
    same = (pairing[:, None] == pairing[None, :]).astype(jnp.float32)
    gap = 2.0 * unit - jnp.dot(same, unit, precision=highest)
    loss_value = jnp.sum(gap * gap) / total
    grad_unit = 0.5 * (2.0 * gap - jnp.dot(same, gap, precision=highest))
    grad_white = scale * grad_unit - white * scale * scale * scale * jnp.sum(white * grad_unit, axis=1, keepdims=True)
    gram = jnp.dot(grad_white.T, white, precision=highest)
    row = lax.broadcasted_iota(jnp.int32, gram.shape, 0)
    column = lax.broadcasted_iota(jnp.int32, gram.shape, 1)
    lower = jnp.where(row > column, gram, jnp.where(row == column, 0.5 * gram, 0.0))
    both = lower + lower.T
    grad_moved = jnp.dot(grad_white - jnp.dot(white, both, precision=highest) / total, inverse, precision=highest)
    return loss_value, grad_moved - jnp.sum(grad_moved, axis=0) / total


def silu_slope(values):
    sigmoid_value = jax.nn.sigmoid(values)
    return sigmoid_value * (1.0 + values * (1.0 - sigmoid_value))


def moments(sum_value, sum_square, total_count):
    centre = sum_value / total_count
    return (centre, lax.rsqrt(sum_square / total_count - centre * centre + epsilon))


def make_columns(activation):
    images_here, pixel_count, inner_width = activation.shape
    grid_map = activation.reshape(images_here, SIDE, SIDE, inner_width)
    padded = jnp.pad(grid_map, ((0, 0), (1, 1), (1, 1), (0, 0)))
    pieces = [
        padded[:, tap_row : tap_row + SIDE, tap_col : tap_col + SIDE, :]
        for tap_row in range(3)
        for tap_col in range(3)
    ]
    return jnp.concatenate(pieces, axis=3).reshape(images_here * pixel_count, 9 * inner_width)


def fold_columns(columns, images_here, inner_width):
    tap_grads = columns.reshape(images_here, SIDE, SIDE, 9, inner_width)
    padded = jnp.zeros((images_here, SIDE + 2, SIDE + 2, inner_width), jnp.float32)
    for tap_row in range(3):
        for tap_col in range(3):
            padded = padded.at[:, tap_row : tap_row + SIDE, tap_col : tap_col + SIDE, :].add(
                tap_grads[:, :, :, 3 * tap_row + tap_col, :]
            )
    return padded[:, 1 : SIDE + 1, 1 : SIDE + 1, :].reshape(images_here, SIDE * SIDE, inner_width)


def pixel_sums(values, weight):
    return (jnp.sum(values * weight, axis=(0, 1)), jnp.sum(values * values * weight, axis=(0, 1)))


def front(
    masked_low,
    weight,
    counts,
    w_reduce,
    w_spatial,
    w_expand,
    norm_reduce,
    norm_spatial,
    norm_expand,
):
    images_here, pixel_count, width = masked_low.shape
    inner_width = w_reduce.shape[1]
    rows_here = images_here * pixel_count
    reduced = jnp.dot(
        masked_low.reshape(rows_here, width), w_reduce, preferred_element_type=jnp.float32
    ).reshape(images_here, pixel_count, inner_width)
    sum_reduce, square_reduce = pixel_sums(reduced, weight)
    sum_reduce, square_reduce, valid_total = lax.psum((sum_reduce, square_reduce, jnp.sum(counts)), ("dp", "sub"))
    centre_reduce, scale_reduce = moments(sum_reduce, square_reduce, valid_total)
    normed_reduce = (reduced - centre_reduce) * scale_reduce
    level_reduce = norm_reduce[0] * normed_reduce + norm_reduce[1]
    act_reduce = (weight * jax.nn.silu(level_reduce)).astype(jnp.bfloat16)
    columns = make_columns(act_reduce)
    spatial = jnp.dot(
        columns, w_spatial.reshape(9 * inner_width, inner_width), preferred_element_type=jnp.float32
    ).reshape(images_here, pixel_count, inner_width)
    sum_spatial, square_spatial = pixel_sums(spatial, weight)
    sum_spatial, square_spatial = lax.psum((sum_spatial, square_spatial), ("dp", "sub"))
    centre_spatial, scale_spatial = moments(sum_spatial, square_spatial, valid_total)
    normed_spatial = (spatial - centre_spatial) * scale_spatial
    level_spatial = norm_spatial[0] * normed_spatial + norm_spatial[1]
    act_spatial = (weight * jax.nn.silu(level_spatial)).astype(jnp.bfloat16)
    expanded = jnp.dot(
        act_spatial.reshape(rows_here, inner_width), w_expand, preferred_element_type=jnp.float32
    ).reshape(images_here, pixel_count, width)
    sum_expand, square_expand = pixel_sums(expanded, weight)
    sum_expand, square_expand = lax.psum((sum_expand, square_expand), ("dp", "sub"))
    centre_expand, scale_expand = moments(sum_expand, square_expand, valid_total)
    normed_expand = (expanded - centre_expand) * scale_expand
    summed = masked_low.astype(jnp.float32) + norm_expand[0] * normed_expand + norm_expand[1]
    stats = (
        valid_total,
        centre_reduce,
        scale_reduce,
        centre_spatial,
        scale_spatial,
        centre_expand,
        scale_expand,
    )
    return (
        (
            normed_reduce,
            level_reduce,
            columns,
            normed_spatial,
            level_spatial,
            act_spatial,
            normed_expand,
            summed,
        ),
        stats,
    )


def norm_back(upstream, normed, gain, scale_value, sum_grad, dot_grad, total_count):
    return gain * scale_value * (upstream - (sum_grad + normed * dot_grad) / total_count)


def plain_shards(
    images,
    pixel_mask,
    pairing,
    w_reduce,
    w_spatial,
    w_expand,
    w_project,
    w_code,
    norm_reduce,
    norm_spatial,
    norm_expand,
    norm_project,
):
    images_here, pixel_count, width = images.shape
    inner_width = w_reduce.shape[1]
    images_total = pairing.shape[0]
    rows_here = images_here * pixel_count
    highest = lax.Precision.HIGHEST
    weight = pixel_mask.astype(jnp.float32)[:, :, None]
    counts = jnp.sum(weight, axis=1)
    masked_low = images * weight.astype(jnp.bfloat16)
    project_full = w_project.astype(jnp.float32)
    code_full = w_code.astype(jnp.float32)
    saved, stats = front(
        masked_low,
        weight,
        counts,
        w_reduce,
        w_spatial,
        w_expand,
        norm_reduce,
        norm_spatial,
        norm_expand,
    )
    (
        normed_reduce,
        level_reduce,
        columns,
        normed_spatial,
        level_spatial,
        act_spatial,
        normed_expand,
        summed,
    ) = saved
    (
        valid_total,
        centre_reduce,
        scale_reduce,
        centre_spatial,
        scale_spatial,
        centre_expand,
        scale_expand,
    ) = stats
    output = weight * jax.nn.silu(summed)
    own_pooled = jnp.sum(output, axis=1) / counts
    pooled = lax.all_gather(own_pooled, ("dp", "sub"), axis=0, tiled=True)
    projected = jnp.dot(pooled, project_full, precision=highest)
    centre_project, scale_project = moments(
        jnp.sum(projected, axis=0), jnp.sum(projected * projected, axis=0), float(images_total)
    )
    normed_project = (projected - centre_project) * scale_project
    level_project = norm_project[0] * normed_project + norm_project[1]
    hidden = jax.nn.silu(level_project)
    codes = jnp.dot(hidden, code_full, precision=highest)
    loss_value, grad_codes = whiten(codes, pairing)
    grad_w_code = jnp.dot(hidden.T, grad_codes, precision=highest)
    grad_hidden = jnp.dot(grad_codes, code_full.T, precision=highest)
    grad_level_project = grad_hidden * silu_slope(level_project)
    sum_project_grad = jnp.sum(grad_level_project, axis=0)
    dot_project_grad = jnp.sum(grad_level_project * normed_project, axis=0)
    grad_norm_project = jnp.stack([dot_project_grad, sum_project_grad])
    grad_projected = norm_back(
        grad_level_project,
        normed_project,
        norm_project[0],
        scale_project,
        sum_project_grad,
        dot_project_grad,
        float(images_total),
    )
    grad_w_project = jnp.dot(pooled.T, grad_projected, precision=highest)
    own_start = lax.axis_index(("dp", "sub")) * images_here
    own_projected = lax.dynamic_slice_in_dim(grad_projected, own_start, images_here, 0)
    grad_pooled = jnp.dot(own_projected, project_full.T, precision=highest)
    grad_summed = weight * (grad_pooled / counts)[:, None, :] * silu_slope(summed)
    sum_expand_grad, dot_expand_grad = lax.psum(
        (jnp.sum(grad_summed, axis=(0, 1)), jnp.sum(grad_summed * normed_expand, axis=(0, 1))), ("dp", "sub")
    )
    grad_norm_expand = jnp.stack([dot_expand_grad, sum_expand_grad])
    grad_expanded = (
        (
            weight
            * norm_back(
                grad_summed,
                normed_expand,
                norm_expand[0],
                scale_expand,
                sum_expand_grad,
                dot_expand_grad,
                valid_total,
            )
        )
        .astype(jnp.bfloat16)
        .reshape(rows_here, width)
    )
    grad_w_expand = jnp.einsum(
        "rm,rc->mc",
        act_spatial.reshape(rows_here, inner_width),
        grad_expanded,
        preferred_element_type=jnp.float32,
    )
    grad_act_spatial = jnp.einsum(
        "rc,mc->rm", grad_expanded, w_expand, preferred_element_type=jnp.float32
    ).reshape(images_here, pixel_count, inner_width)
    grad_level_spatial = grad_act_spatial * weight * silu_slope(level_spatial)
    sum_spatial_grad, dot_spatial_grad = lax.psum(
        (
            jnp.sum(grad_level_spatial, axis=(0, 1)),
            jnp.sum(grad_level_spatial * normed_spatial, axis=(0, 1)),
        ),
        ("dp", "sub"),
    )
    grad_norm_spatial = jnp.stack([dot_spatial_grad, sum_spatial_grad])
    grad_spatial_out = (
        (
            weight
            * norm_back(
                grad_level_spatial,
                normed_spatial,
                norm_spatial[0],
                scale_spatial,
                sum_spatial_grad,
                dot_spatial_grad,
                valid_total,
            )
        )
        .astype(jnp.bfloat16)
        .reshape(rows_here, inner_width)
    )
    grad_w_spatial = jnp.einsum(
        "rk,rm->km", columns, grad_spatial_out, preferred_element_type=jnp.float32
    ).reshape(3, 3, inner_width, inner_width)
    grad_columns = jnp.einsum(
        "rm,km->rk",
        grad_spatial_out,
        w_spatial.reshape(9 * inner_width, inner_width),
        preferred_element_type=jnp.float32,
    )
    grad_act_reduce = fold_columns(grad_columns, images_here, inner_width)
    grad_level_reduce = grad_act_reduce * weight * silu_slope(level_reduce)
    sum_reduce_grad, dot_reduce_grad = lax.psum(
        (
            jnp.sum(grad_level_reduce, axis=(0, 1)),
            jnp.sum(grad_level_reduce * normed_reduce, axis=(0, 1)),
        ),
        ("dp", "sub"),
    )
    grad_norm_reduce = jnp.stack([dot_reduce_grad, sum_reduce_grad])
    grad_reduced = (
        (
            weight
            * norm_back(
                grad_level_reduce,
                normed_reduce,
                norm_reduce[0],
                scale_reduce,
                sum_reduce_grad,
                dot_reduce_grad,
                valid_total,
            )
        )
        .astype(jnp.bfloat16)
        .reshape(rows_here, inner_width)
    )
    grad_w_reduce = jnp.einsum(
        "rc,rm->cm",
        masked_low.reshape(rows_here, width),
        grad_reduced,
        preferred_element_type=jnp.float32,
    )
    grad_input = jnp.einsum(
        "rm,cm->rc", grad_reduced, w_reduce, preferred_element_type=jnp.float32
    ).reshape(images_here, pixel_count, width)
    grad_images = weight * (grad_summed + grad_input)
    grad_w_spatial, grad_w_reduce, grad_w_expand = lax.psum(
        (grad_w_spatial, grad_w_reduce, grad_w_expand), ("dp", "sub")
    )
    return (
        loss_value,
        grad_images,
        grad_w_reduce,
        grad_w_spatial.reshape(3, 3, inner_width, inner_width),
        grad_w_expand,
        grad_w_project,
        grad_w_code,
        grad_norm_reduce,
        grad_norm_spatial,
        grad_norm_expand,
        grad_norm_project,
    )


def shards(
    images,
    pixel_mask,
    pairing,
    w_reduce,
    w_spatial,
    w_expand,
    w_project,
    w_code,
    norm_reduce,
    norm_spatial,
    norm_expand,
    norm_project,
):
    width, inner = w_reduce.shape
    taps = w_spatial.reshape(9 * inner, inner)
    (
        _, projector, _, loss,
        grad_norm_project, grad_norm_expand, grad_norm_reduce, grad_norm_spatial,
        grad_images, grad_spatial, grad_reduce, grad_expand,
    ) = training_step(
        jnp.transpose(images, (1, 0, 2)),
        pixel_mask,
        pairing.reshape(1, 256),
        w_reduce,
        taps,
        w_expand,
        w_project,
        w_code,
        norm_reduce,
        norm_spatial,
        norm_expand,
        norm_project,
    )
    (
        grad_project, grad_code, loss,
        grad_norm_reduce, grad_norm_spatial, grad_norm_expand, grad_norm_project,
        grad_images, grad_spatial, grad_reduce, grad_expand,
    ) = finish(
        projector,
        w_project.shape,
        w_code.shape,
        loss,
        (grad_norm_reduce, grad_norm_spatial, grad_norm_expand, grad_norm_project),
        (grad_images, grad_spatial, grad_reduce, grad_expand),
    )
    return (
        loss[0, 0],
        jnp.transpose(grad_images.reshape(49, 8, width), (1, 0, 2)),
        grad_reduce,
        grad_spatial.reshape(w_spatial.shape),
        grad_expand,
        grad_project,
        grad_code,
        grad_norm_reduce,
        grad_norm_spatial,
        grad_norm_expand,
        grad_norm_project,
    )


def solution(mesh):
    fits = mesh.shape["dp"] == 16 and mesh.shape["sub"] == 2
    placed = (P(("dp", "sub"), None, None), P(("dp", "sub"), None)) + (P(),) * 10
    return jax.shard_map(
        shards if fits else plain_shards,
        mesh=mesh,
        in_specs=placed,
        out_specs=(P(), P(("dp", "sub"), None, None)) + (P(),) * 9,
        check_vma=False,
    )
```

```python
import functools
import jax
import jax.numpy as jnp
from jax import lax
from jax.experimental import pallas as pl
from jax.experimental.pallas import tpu as pltpu
from jax.sharding import PartitionSpec as P

MESH = pl.DeviceIdType.MESH
SIDE = 7
SLOTS = 56
ROWS = 448
epsilon = 1e-05
whiten_floor = 0.001
f32 = jnp.float32
bf16 = jnp.bfloat16


def place():
    dp = lax.axis_index("dp")
    sub = lax.axis_index("sub")
    z = dp // 4
    y = lax.rem(dp // 2, 2)
    x = lax.rem(dp, 2)
    ring = 3 * y + x - 2 * x * y
    return dp, sub, z, ring


def plane_of(ring):
    ring = lax.rem(ring + 4, 4)
    y = ring // 2
    odd = lax.rem(ring, 2)
    return y * 2 + odd + y - 2 * odd * y


def ring_dp(z, ring):
    return z * 4 + plane_of(ring)


def dev(dp, sub):
    return {"dp": dp, "sub": sub}


def greet_start():
    dp, sub, _, _ = place()
    me = dp * 2 + sub
    barrier = pltpu.get_barrier_semaphore()

    @pl.loop(1, 32)
    def _(step):
        other = lax.rem(me + step, 32)
        pl.semaphore_signal(
            barrier, inc=1, device_id=dev(other // 2, lax.rem(other, 2)), device_id_type=MESH
        )


def greet_wait():
    pl.semaphore_wait(pltpu.get_barrier_semaphore(), 31)


def remote(src, dst, send, recv, where):
    return pltpu.make_async_remote_copy(
        src_ref=src,
        dst_ref=dst,
        send_sem=send,
        recv_sem=recv,
        device_id=dev(*where),
        device_id_type=MESH,
    )


def arrived(ref, sem):
    pltpu.make_async_copy(ref, ref, sem).wait()


def direct_start(buf, send, recv):
    dp, sub, _, _ = place()
    me = dp * 2 + sub

    @pl.loop(1, 32)
    def _(step):
        other = lax.rem(me + step, 32)
        remote(buf.at[me], buf.at[me], send, recv, (other // 2, lax.rem(other, 2))).start()


def direct_finish(buf, send, recv):
    many = buf.at[pl.ds(0, 31)]
    arrived(many, recv)
    total = jnp.sum(buf[...], axis=0)
    arrived(many, send)
    return total


def tree_gen(pair, plane, line, send, recv, result):
    dp, sub, z, _ = place()
    w = lax.rem(dp, 4)
    remote(pair.at[sub], pair.at[sub], send.at[0], recv.at[0], (dp, 1 - sub)).start()
    yield
    arrived(pair.at[0], recv.at[0])
    plane[w] = pair[0] + pair[1]
    for k in range(1, 4):
        where = (z * 4 + lax.rem(w + k, 4), sub)
        remote(plane.at[w], plane.at[w], send.at[1], recv.at[1], where).start()
    yield
    arrived(plane.at[pl.ds(0, 3)], recv.at[1])
    line[z] = (plane[0] + plane[1]) + (plane[2] + plane[3])
    for k in range(1, 4):
        where = (lax.rem(z + k, 4) * 4 + w, sub)
        remote(line.at[z], line.at[z], send.at[2], recv.at[2], where).start()
    yield
    arrived(line.at[pl.ds(0, 3)], recv.at[2])
    result[...] = (line[0] + line[1]) + (line[2] + line[3])
    arrived(pair.at[0], send.at[0])
    arrived(plane.at[pl.ds(0, 3)], send.at[1])
    arrived(line.at[pl.ds(0, 3)], send.at[2])


class Mover:
    def __init__(self, send, recv):
        self.send, self.recv, self.pending = send, recv, []

    def go(self, cond, src, dst, s, r, where):
        def body():
            remote(src, dst, self.send.at[s], self.recv.at[r], where).start()

        if cond is None:
            body()
        else:
            pl.when(cond)(body)
        self.pending.append((cond, src, s))

    def got(self, cond, ref, r, then=None):
        def body():
            arrived(ref, self.recv.at[r])
            if then is not None:
                then()

        if cond is None:
            body()
        else:
            pl.when(cond)(body)

    def drain(self):
        for cond, ref, s in self.pending:

            def body(ref=ref, s=s):
                arrived(ref, self.send.at[s])

            if cond is None:
                body()
            else:
                pl.when(cond)(body)
        self.pending = []

    def settle(self, s):
        for cond, ref, other in self.pending:
            if other == s:
                arrived(ref, self.send.at[s])
        self.pending = [item for item in self.pending if item[2] != s]

    def line_gather(self, at, first, base):
        dp, sub, z, _ = place()
        up, down = (dp + 4, sub), (dp - 4, sub)
        hold = lambda j: at(jnp.clip(j, 0, 3))
        for t in range(3):
            from_up = first if t == 0 and first is not None else hold(z - t)
            from_down = first if t == 0 and first is not None else hold(z + t)
            self.go(jnp.logical_and(z <= 2, z >= t), from_up, hold(z - t), base + t, base + t, up)
            self.go(
                jnp.logical_and(z >= 1, z <= 3 - t),
                from_down,
                hold(z + t),
                base + 3 + t,
                base + 3 + t,
                down,
            )
            yield
            self.got(z >= t + 1, hold(z - 1 - t), base + t)
            self.got(z <= 2 - t, hold(z + 1 + t), base + 3 + t)

    def line_direct(self, at, first, base):
        dp, sub, z, _ = place()
        w = lax.rem(dp, 4)
        for k in range(1, 4):
            where = (lax.rem(z + k, 4) * 4 + w, sub)
            self.go(None, first, at(z), base + k - 1, base + k - 1, where)
        yield
        for k in range(1, 4):
            self.got(None, at(lax.rem(z + 4 - k, 4)), base + k - 1)

    def ring_direct(self, blk, first, base, after):
        dp, sub, z, q = place()
        src = first if first is not None else blk(0, None)
        for k in range(1, 4):
            self.go(None, src, blk(0, None), base + k - 1, base + k - 1, (ring_dp(z, q + k), sub))
        yield
        for k in range(1, 4):
            self.got(None, blk(4 - k, None), base + k - 1)
            after(blk(4 - k, None), 3 - k)

    def ring_gather(self, blk, first, base, after):
        dp, sub, z, q = place()
        after_me, before_me = (ring_dp(z, q + 1), sub), (ring_dp(z, q + 3), sub)
        src = first if first is not None else blk(0, None)
        self.go(None, src, blk(0, None), base, base, after_me)
        self.go(None, src, blk(0, None), base + 1, base + 1, before_me)
        yield
        self.got(None, blk(3, None), base)
        self.go(None, blk(3, 0), blk(3, 0), base + 2, base + 2, after_me)
        after(blk(3, None), 0)
        self.got(None, blk(1, None), base + 1)
        self.go(None, blk(1, 1), blk(1, 1), base + 3, base + 3, before_me)
        after(blk(1, None), 1)
        yield
        self.got(None, blk(2, 0), base + 2)
        self.got(None, blk(2, 1), base + 3)
        after(blk(2, None), 2)


def run_all(gens, starts=None):
    live = dict(enumerate(gens))
    tick = 0
    while live:
        for j in sorted(live):
            if starts is None or tick >= starts[j]:
                try:
                    next(live[j])
                except StopIteration:
                    live.pop(j)
        tick += 1


def gather_rows(own, out, send, recv, split, direct=(1, 0, 1, 1)):
    dp, sub, z, q = place()
    width = out.shape[-1]
    sib = (dp, 1 - sub)

    def first_line():
        cols = pl.ds(0, split)
        mid = split // 2
        mover = Mover(send.at[0], recv.at[0])
        at = lambda j: out.at[j, plane_of(q), sub, :, cols]

        def blk(k, h):
            ring = plane_of(q + k)
            if h is None:
                return out.at[:, ring, sub, :, cols]
            return out.at[pl.ds(2 * h, 2), ring, sub, :, cols]

        def share(ref, s):
            mover.go(None, ref, ref, 10 + s, 10, sib)

        line = mover.line_direct if direct[0] else mover.line_gather
        yield from line(at, own.at[:, cols], 0)
        share(blk(0, None), 3)
        ring = mover.ring_direct if direct[1] else mover.ring_gather
        yield from ring(blk, None, 6, share)
        yield
        arrived(out.at[:, :, 1 - sub, :, cols], recv.at[0, 10])
        mover.drain()

    def first_ring():
        cols = pl.ds(split, width - split)
        mid = (width - split) // 2
        mover = Mover(send.at[1], recv.at[1])

        def blk(k, h):
            ring = plane_of(q + k)
            if h is None:
                return out.at[z, ring, sub, :, cols]
            return out.at[z, ring, sub, :, pl.ds(split + h * mid, mid)]

        at = lambda j: out.at[j, :, sub, :, cols]

        def share(ref, s):
            mover.go(None, ref, ref, 10 + s, 10, sib)

        ring = mover.ring_direct if direct[2] else mover.ring_gather
        yield from ring(blk, own.at[:, cols], 0, lambda ref, s: None)
        share(at(z), 3)
        line = mover.line_direct if direct[3] else mover.line_gather
        yield from line(at, at(z), 4)
        for k in range(1, 4):
            share(at(lax.rem(z + k, 4)), k - 1)
        yield
        arrived(out.at[:, :, 1 - sub, :, cols], recv.at[1, 10])
        mover.drain()

    return [first_line(), first_ring()]


def mm(a, b):
    return jnp.dot(a, b, preferred_element_type=f32)


def mm_nt(a, b):
    return lax.dot_general(a, b, (((1,), (1,)), ((), ())), preferred_element_type=f32)


def mm_tn(a, b):
    return lax.dot_general(a, b, (((0,), (0,)), ((), ())), preferred_element_type=f32)


def sigmoid(v):
    return 0.5 + 0.5 * jnp.tanh(0.5 * v)


def split(v):
    high = v.astype(bf16)
    return high, (v - high.astype(f32)).astype(bf16)


def exact(a, b, dims):
    return lax.dot_general(
        a, b, (dims, ((), ())), precision=lax.Precision.HIGHEST, preferred_element_type=f32
    )


def factor_inverse(cov, block=8):
    size = cov.shape[0]
    tiles = size // 8
    row = lax.broadcasted_iota(jnp.int32, (8, size), 0)
    column = lax.broadcasted_iota(jnp.int32, (8, size), 1)
    left = [cov[8 * t : 8 * t + 8, :] for t in range(tiles)]
    right = [jnp.where(row + 8 * t == column, 1.0, 0.0) for t in range(tiles)]
    wide = lambda v: jnp.broadcast_to(v, (8, size))
    for j in range(0, size, block):
        t0, s = j // 8, j % 8
        columns = [[wide(left[t][:, j + k : j + k + 1]) for k in range(block)] for t in range(t0, tiles)]
        lefts = [wide(left[t0][s + k : s + k + 1, :]) for k in range(block)]
        rights = [wide(right[t0][s + k : s + k + 1, :]) for k in range(block)]
        entry = [[wide(columns[0][k][s + m : s + m + 1, :]) for k in range(m + 1)] for m in range(block)]
        lower = [[None] * block for _ in range(block)]
        inverses = []
        for k in range(block):
            inverse = 1.0 / entry[k][k]
            inverses.append(inverse)
            for m in range(k + 1, block):
                lower[m][k] = entry[m][k] * inverse
            for m in range(k + 1, block):
                for n in range(k + 1, m + 1):
                    entry[m][n] = entry[m][n] - lower[m][k] * entry[n][k]
        for m in range(block):
            for k in range(m):
                lefts[m] = lefts[m] - lower[m][k] * lefts[k]
                rights[m] = rights[m] - lower[m][k] * rights[k]
        scaled_left = [a * b for a, b in zip(lefts, inverses)]
        scaled_right = [a * b for a, b in zip(rights, inverses)]
        for t in range(t0, tiles):
            if t == t0 and s + block == 8 and block == 1:
                continue
            own = columns[t - t0]
            for m in range(block):
                for k in range(m):
                    own[m] = own[m] - lower[m][k] * own[k]
            for m in range(block):
                factor = own[m]
                if t == t0:
                    factor = jnp.where(row > s + m, factor, 0.0)
                left[t] = left[t] - factor * scaled_left[m]
                right[t] = right[t] - factor * scaled_right[m]
    out = []
    for t in range(tiles):
        pivots = jnp.sum(jnp.where(row + 8 * t == column, left[t], 0.0), axis=1, keepdims=True)
        out.append(right[t] * lax.rsqrt(pivots))
    return jnp.concatenate(out, axis=0)


def fold8(v):
    rows, cols = v.shape
    return jnp.sum(v.reshape(rows // 8, 8, cols), axis=0)


def columns_of(mask, cols):
    return jnp.concatenate([mask] * (cols // 128), axis=1)


def halves(ref, h):
    cols = ref.shape[1] // 2
    return ref.at[:, pl.ds(h * cols, cols)]


class Job:
    def __init__(self, ring_first, rows, acc, other, land, scratch, send, recv, free):
        self.ring_first, self.rows, self.acc, self.other = ring_first, rows, acc, other
        self.land, self.scratch, self.free = land, scratch, free
        self.mover = Mover(send, recv)
        self.taken = 0

    def take(self, rows):
        ref = rows_at(self.scratch, self.taken, rows)
        self.taken += rows
        return ref

    def ring_reduce(self, base, block):
        dp, sub, z, q = place()
        go, got = self.mover.go, self.mover.got
        after_me, before_me = (ring_dp(z, q + 1), sub), (ring_dp(z, q + 3), sub)
        r0 = self.take(block)
        r1a, r1b = self.take(block), self.take(block)

        def blk(k):
            return rows_at(self.land, base + lax.rem(q + k, 4) * block, block)

        go(None, halves(blk(2), 0), halves(r0, 0), 1, 1, after_me)
        go(None, halves(blk(2), 1), halves(r0, 1), 2, 2, before_me)
        yield
        got(None, halves(r0, 0), 1)
        add_into(halves(blk(1), 0), halves(r0, 0), block)
        go(None, blk(1), r1a, 3, 3, after_me)
        got(None, halves(r0, 1), 2)
        add_into(halves(blk(3), 1), halves(r0, 1), block)
        go(None, blk(3), r1b, 4, 4, before_me)
        yield
        got(None, r1a, 3)
        got(None, r1b, 4)
        add_into(blk(0), r1a, block, r1b)

    def line_reduce(self, base, chunk):
        dp, sub, z, _ = place()
        go, got = self.mover.go, self.mover.got
        up, down = (dp + 4, sub), (dp - 4, sub)
        low = [self.take(chunk) for _ in range(3)]
        high = [low[0], self.take(chunk), self.take(chunk)]

        def at(j):
            return rows_at(self.land, base + jnp.clip(j, 0, 3) * chunk, chunk)

        for t in range(3):
            go(z <= t, at(3 + z - t), low[t], 5 + t, 5 + t, up)
            go(z >= 3 - t, at(z - 3 + t), high[t], 8 + t, 8 + t, down)
            yield
            got(
                jnp.logical_and(z >= 1, z <= t + 1),
                low[t],
                5 + t,
                lambda: add_into(at(2 + z - t), low[t], chunk),
            )
            got(
                jnp.logical_and(z <= 2, z >= 2 - t),
                high[t],
                8 + t,
                lambda: add_into(at(z - 2 + t), high[t], chunk),
            )

    def run(self):
        dp, sub, z, q = place()
        sib = (dp, 1 - sub)
        mover, acc, rows = self.mover, self.acc, self.rows
        mover.go(None, self.other, self.land, 0, 0, sib)
        yield
        mover.got(None, self.land, 0)
        add_into(self.land, acc, rows)
        big, small = rows // 4, rows // 16

        def hand_over():
            mover.settle(0)
            pl.semaphore_signal(self.free, inc=1, device_id=dev(*sib), device_id_type=MESH)

        def total(start):
            copy_into(rows_at(acc, start, small), rows_at(self.land, start, small), small)

        def share(ref, k):
            mover.go(None, ref, ref, 21 + k, 21, sib)

        if self.ring_first:
            yield from self.ring_reduce(0, big)
            hand_over()
            yield from self.line_reduce(q * big, small)
            total(q * big + z * small)
            at = lambda j: rows_at(acc, q * big + j * small, small)
            yield from mover.line_gather(at, None, 11)
            pl.semaphore_wait(self.free, 1)
            share(rows_at(acc, q * big, big), 3)

            def blk(k, h):
                ref = rows_at(acc, lax.rem(q + k, 4) * big, big)
                return ref if h is None else halves(ref, h)

            yield from mover.ring_gather(blk, None, 17, share)
        else:
            yield from self.line_reduce(0, big)
            hand_over()
            yield from self.ring_reduce(z * big, small)
            total(z * big + q * small)

            def blk(k, h):
                ref = rows_at(acc, z * big + lax.rem(q + k, 4) * small, small)
                return ref if h is None else halves(ref, h)

            yield from mover.ring_gather(blk, None, 17, lambda ref, k: None)
            pl.semaphore_wait(self.free, 1)
            share(rows_at(acc, z * big, big), 3)
            at = lambda j: rows_at(acc, j * big, big)
            yield from mover.line_gather(at, None, 11)
            for k in range(1, 4):
                share(rows_at(acc, lax.rem(z + k, 4) * big, big), k - 1)
        yield
        arrived(self.other, mover.recv.at[21])
        mover.drain()


JOB_SEMS = 25


def add_into(dst, src, rows, more=None):
    step = 16 if rows % 16 == 0 else 8

    @pl.loop(0, rows // step)
    def _(k):
        at = pl.ds(pl.multiple_of(k * step, 8), step)
        value = dst[at, :] + src[at, :]
        dst[at, :] = value if more is None else value + more[at, :]


def copy_into(dst, src, rows):
    @pl.loop(0, rows // 8)
    def _(k):
        at = pl.ds(pl.multiple_of(k * 8, 8), 8)
        dst[at, :] = src[at, :]


def rows_at(ref, start, size):
    return ref.at[pl.ds(pl.multiple_of(start, 8), size)]


def landing_rows(ring_first, rows):
    big, small = rows // 4, rows // 16
    return 3 * big + 5 * small if ring_first else 3 * small + 5 * big


JOBS = (
    (2, 0, 256, 0, 1536, True),
    (2, 0, 256, 1536, 512, False),
    (0, 0, 512, 0, 512, True),
    (0, 512, 256, 0, 512, False),
    (0, 768, 512, 0, 512, True),
    (0, 1280, 256, 0, 512, False),
    (0, 1536, 512, 0, 512, True),
    (0, 2048, 256, 0, 512, False),
    (1, 0, 768, 0, 512, True),
    (1, 768, 256, 0, 512, False),
)

ORDER = (
    -1, -2, 0, -3, 1, 1, 0, -4, 1, -5, 3, 0, 1, 3, 2, 7, 4, -6, 7, 1, 2, 3, 6, 7,
    1, 4, 0, 3, -7, 1, 4, -10, 0, -8, 1, 7, 2, 0, -9, 5, 4, 1, 7, 8, 6, -11, 0, 4,
    3, 2, 7, 8, 1, 4, 9, 0, 7, 5, 6, 2, 1, 3, 4, 9, 0, 7, 5, -12, 8, 2, 6, 4,
    7, -13, 3, 4, 5, 2, 0, 6, 7, -14, 8, 2, 9, 4, -15, 6, 1, 5, 2, 8, 3, 7, 9, 6,
    2, 8, 5, 3, -16, 9, 6, 4, -17, 8, 9, 0, 6, 3, 9, 8, 5, 2, 3, 9, 4, 5, 6, 8,
    5, 0, 2, 7, -18, 9, 3, 8, 6, 5, 3, 7, 4, 9, 5, 8, 5, 9, 1, 6, 6, 5, 9, 2,
    8, 0, 9, 8,
)

VM = 43

PROJECTOR_ROWS = 12288


def step_kernel(
    images, pixel_mask, pair_row, w_reduce, w_spatial, w_expand, w_project, w_code,
    norm_reduce, norm_spatial, norm_expand, norm_project,
    pooled_out, projector, masked_out, loss_out,
    grad_norm_out, third_grad, grad_norm_reduce, grad_norm_spatial, dsum, gs, gr, big,
    img, wr, ws, we, wc, masked, reduced, spatial, act1, act2, dred, level, wide, shifted, mask, stats,
    own, own_proj, proj_all, same, codes_buf, counts, sums, totals, third_sums, upstream,
    buf1, buf2, buf5, buf6, pair, plane, line, pair4, plane4, line4, land_s, land_r, land_e, *rest,
):
    scratches = rest[: len(JOBS)]
    load, save, send, recv, gsend, grecv, hsend, hrecv, jsend, jrecv, jfree, wsem = rest[len(JOBS) :]
    dp, sub, z, q = place()
    me = dp * 2 + sub
    width, inner = wr.shape
    proj = wc.shape[0]
    normed = big.at[pl.ds(0, ROWS)]
    slope, dexp, act2_rows = dsum, masked, dred
    half_proj = proj // 2
    loads = [
        pltpu.make_async_copy(a, b, load.at[k])
        for k, (a, b) in enumerate(
            [(images, img), (w_reduce, wr), (w_spatial, ws), (w_expand, we), (w_code, wc)]
            + [
                (w_project.at[:, pl.ds(h * half_proj, half_proj)], ws.at[pl.ds(h * width, width)])
                for h in range(2)
            ]
            + [(w_spatial, ws), (masked_out, masked)]
        )
    ]

    def block(k, n):
        start = pl.multiple_of(512 * k + 256 * (n // 2), 256)
        return gr.at[pl.ds(start, 256), pl.ds(pl.multiple_of(lax.rem(n, 2) * 256, 256), 256)]

    loads[0].start()
    loads[1].start()
    greet_start()
    here = pixel_mask[...].astype(f32)
    counts[...] = jnp.broadcast_to(jnp.sum(here, axis=1, keepdims=True), (8, 128))
    for slot in range(SLOTS):
        r, c = slot // 8, slot % 8
        if c == SIDE:
            value = jnp.zeros((8, 128), f32)
        else:
            value = jnp.broadcast_to(here[:, SIDE * r + c : SIDE * r + c + 1], (8, 128))
        mask[pl.ds(8 * slot, 8), :] = value
    wide[pl.ds(0, 8), :] = jnp.zeros((8, inner), f32)
    wide[pl.ds(ROWS + 8, 8), :] = jnp.zeros((8, inner), f32)
    shifted[pl.ds(0, 64), :] = jnp.zeros((64, 3 * inner), bf16)
    shifted[pl.ds(512, 64), :] = jnp.zeros((64, 3 * inner), bf16)
    loads[0].wait()
    for copy in loads[2:5]:
        copy.start()
    gap = jnp.zeros((8, 256), f32)

    @pl.loop(0, width // 256)
    def _(n):
        cols = pl.ds(pl.multiple_of(n * 256, 256), 256)
        for r in range(SIDE):
            rows = img[pl.ds(SIDE * r, SIDE), :, cols].astype(f32).reshape(SIDE * 8, 256)
            rows = rows * columns_of(mask[pl.ds(64 * r, 56), :], 256)
            masked[pl.ds(64 * r, 64), cols] = jnp.concatenate([rows, gap], axis=0).astype(bf16)

    saves = []

    def keep(a, b):
        copy = pltpu.make_async_copy(a, b, save.at[len(saves)])
        copy.start()
        saves.append(copy)

    keep(masked, masked_out)
    loads[1].wait()

    @pl.loop(0, inner // 256)
    def _(n):
        cols = pl.ds(pl.multiple_of(n * 256, 256), 256)
        got = mm(masked[...], wr[:, cols])
        reduced[:, cols] = got
        buf1[me, pl.ds(0, 1), cols] = jnp.sum(got, axis=0, keepdims=True)
        buf1[me, pl.ds(1, 1), cols] = jnp.sum(got * got, axis=0, keepdims=True)

    extra = pl.ds(inner, 128)
    buf1[me, pl.ds(0, 1), extra] = jnp.sum(counts[...], axis=0, keepdims=True)
    buf1[me, pl.ds(1, 1), extra] = jnp.zeros((1, 128), f32)
    greet_wait()
    direct_start(buf1, send.at[1], recv.at[1])
    pairs = jnp.broadcast_to(pair_row[...].astype(f32), (256, 256))
    same[...] = (pairs == jnp.transpose(pairs)).astype(f32)
    first = direct_finish(buf1, send.at[1], recv.at[1])
    valid = first[0:1, inner : inner + 1]
    inverse_valid = 1.0 / valid

    def moments(total):
        centre = total[0:1] * inverse_valid
        return centre, lax.rsqrt(total[1:2] * inverse_valid - centre * centre + epsilon)

    def activate(src, norm, centre, scale, store):
        gain = norm[0:1, :] * scale
        bias = norm[1:2, :] - centre * gain

        @pl.loop(0, ROWS // 32)
        def _(k):
            rows = pl.ds(pl.multiple_of(k * 32, 32), 32)
            level = src[rows, :] * gain + bias
            store(k, columns_of(mask[rows, :], inner) * (level * sigmoid(level)))

    centre1, scale1 = moments(first[:, :inner])
    stats[pl.ds(0, 1), pl.ds(0, inner)] = centre1
    stats[pl.ds(1, 1), pl.ds(0, inner)] = scale1

    def store_wide(k, value):
        wide[pl.ds(pl.multiple_of(k * 32 + 8, 8), 32), :] = value
        shifted[pl.ds(pl.multiple_of(k * 32 + 64, 32), 32), pl.ds(inner, inner)] = value.astype(bf16)

    activate(reduced, norm_reduce, centre1, scale1, store_wide)

    @pl.loop(0, ROWS // 32)
    def _(k):
        for b in (0, 2):
            rows = wide[pl.ds(pl.multiple_of(k * 32 + 8 * b, 8), 32), :]
            shifted[pl.ds(pl.multiple_of(k * 32 + 64, 32), 32), pl.ds(b * inner, inner)] = rows.astype(bf16)

    loads[2].wait()

    @pl.loop(0, inner // 256)
    def _(n):
        cols = pl.ds(pl.multiple_of(n * 256, 256), 256)

        left = jnp.concatenate([shifted[pl.ds(64 * a, ROWS), :] for a in range(3)], axis=1)
        got = mm(left, ws[:, cols]) * columns_of(mask[...], 256)
        spatial[:, cols] = got
        buf2[me, pl.ds(0, 1), cols] = jnp.sum(got, axis=0, keepdims=True)
        buf2[me, pl.ds(1, 1), cols] = jnp.sum(got * got, axis=0, keepdims=True)

    direct_start(buf2, send.at[2], recv.at[2])
    loads[5].start()
    loads[6].start()
    act1[...] = jnp.transpose(wide[pl.ds(8, ROWS), :]).astype(bf16)
    centre2, scale2 = moments(direct_finish(buf2, send.at[2], recv.at[2]))
    stats[pl.ds(2, 1), pl.ds(0, inner)] = centre2
    stats[pl.ds(3, 1), pl.ds(0, inner)] = scale2

    def store_act2(k, value):
        wide[pl.ds(pl.multiple_of(k * 32 + 8, 8), 32), :] = value
        act2_rows[pl.ds(pl.multiple_of(k * 32, 32), 32), :] = value.astype(bf16)

    activate(spatial, norm_spatial, centre2, scale2, store_act2)
    loads[3].wait()

    @pl.loop(0, width // 256)
    def _(n):
        cols = pl.ds(pl.multiple_of(n * 256, 256), 256)
        got = mm(act2_rows[...], we[:, cols])
        normed[:, cols] = got
        pair[sub, pl.ds(0, 1), cols] = jnp.sum(got, axis=0, keepdims=True)
        pair[sub, pl.ds(1, 1), cols] = jnp.sum(got * got, axis=0, keepdims=True)

    third = tree_gen(pair, plane, line, send.at[pl.ds(3, 3)], recv.at[pl.ds(3, 3)], totals)
    next(third)
    next(third)
    act2[...] = jnp.transpose(wide[pl.ds(8, ROWS), :]).astype(bf16)
    next(third)
    next(third, None)
    centre3, scale3 = moments(totals[...])
    stats[pl.ds(4, 1), :] = centre3
    stats[pl.ds(5, 1), :] = scale3
    stats[pl.ds(6, 1), :] = jnp.broadcast_to(valid, (1, width))
    stats[pl.ds(7, 1), :] = jnp.zeros((1, width), f32)
    inverse_counts = 1.0 / counts[...]

    def last_norm(cols, rows):
        gain, bias = norm_expand[pl.ds(0, 1), cols], norm_expand[pl.ds(1, 1), cols]
        n3 = (normed[rows, cols] - stats[pl.ds(4, 1), cols]) * stats[pl.ds(5, 1), cols]
        total = masked[rows, cols].astype(f32) + gain * n3 + bias
        sig = sigmoid(total)
        return n3, sig, total * sig

    @pl.loop(0, width // 256)
    def _(n):
        cols = pl.ds(pl.multiple_of(n * 256, 256), 256)
        pool = jnp.zeros((8, 256), f32)
        for k in range(SIDE):
            rows = pl.ds(64 * k, 64)
            _, _, out = last_norm(cols, rows)
            pool = pool + fold8(columns_of(mask[rows, :], 256) * out)
        own[:, cols] = pool * columns_of(inverse_counts, 256)

    def slopes(lo, hi):
        @pl.loop(lo, hi)
        def _(n):
            cols = pl.ds(pl.multiple_of(n * 256, 256), 256)
            s1 = s2 = jnp.zeros((8, 256), f32)
            for k in range(SIDE):
                rows = pl.ds(64 * k, 64)
                n3, sig, out = last_norm(cols, rows)
                slope3 = columns_of(mask[rows, :], 256) * (sig + out * (1.0 - sig))
                normed[rows, cols] = n3
                slope[rows, cols] = slope3
                s1, s2 = s1 + fold8(slope3), s2 + fold8(slope3 * n3)
            sums[pl.ds(0, 8), cols] = s1
            sums[pl.ds(8, 8), cols] = s2

    rows_all = 256
    for k in (4, 5, 6):
        loads[k].wait()
    high = own[...].astype(bf16).astype(f32)
    both_terms = jnp.concatenate([high, own[...] - high], axis=0).astype(bf16)

    @pl.loop(0, proj // 256)
    def _(n):
        cols = pl.ds(pl.multiple_of(n * 256, 256), 256)
        rows = pl.ds(pl.multiple_of((n // 2) * width, 256), width)
        value = mm(both_terms, ws[rows, pl.ds(pl.multiple_of(lax.rem(n, 2) * 256, 256), 256)])
        own_proj[:, cols] = value[0:8] + value[8:16]

    proj_all[z, lax.rem(dp, 4), sub] = own_proj[...]
    proj_movers = gather_rows(own_proj, proj_all, gsend, grecv, proj * 3 // 4, (1, 1, 1, 1))
    pool_movers = gather_rows(own, pooled_out, hsend, hrecv, 1536, (1, 0, 1, 1))

    def move(movers):
        for mover in movers:
            next(mover, None)

    mine = pltpu.make_async_copy(own, pooled_out.at[z, lax.rem(dp, 4), sub], load.at[0])
    mine.start()
    move(proj_movers)
    slopes(0, 3)
    move(proj_movers)
    move(pool_movers)
    slopes(3, 6)
    move(proj_movers)
    slopes(6, 8)
    mine.wait()
    move(proj_movers)
    move(proj_movers)
    move(pool_movers)

    share = 1.0 / rows_all
    codes_buf[...] = jnp.zeros_like(codes_buf)

    @pl.loop(0, proj // 256)
    def _(n):
        cols = pl.ds(pl.multiple_of(n * 256, 256), 256)
        value = proj_all[:, :, :, :, cols].reshape(rows_all, 256)
        centre = jnp.sum(value, axis=0, keepdims=True) * share
        square = jnp.sum(value * value, axis=0, keepdims=True) * share
        scale = lax.rsqrt(square - centre * centre + epsilon)
        normal_here = (value - centre) * scale
        level_here = norm_project[pl.ds(0, 1), cols] * normal_here + norm_project[pl.ds(1, 1), cols]
        block(1, n)[...] = normal_here
        block(0, n)[...] = level_here
        value = level_here * sigmoid(level_here)
        block(2, n)[...] = value
        high, low = split(value)
        codes_buf[...] += mm(high, wc[cols, :]) + mm(low, wc[cols, :])
        upstream[pl.ds(0, 1), cols] = scale * norm_project[pl.ds(0, 1), cols]

    codes = codes_buf[...]

    centre = jnp.sum(codes, axis=0, keepdims=True) * share
    moved = codes - centre
    cov = exact(moved, moved, ((0,), (0,))) * share
    size = cov.shape[0]
    row = lax.broadcasted_iota(jnp.int32, (size, size), 0)
    column = lax.broadcasted_iota(jnp.int32, (size, size), 1)
    inverse = factor_inverse(cov + jnp.where(row == column, whiten_floor, 0.0))
    move(pool_movers)
    white = exact(moved, inverse, ((1,), (1,)))
    unit_scale = lax.rsqrt(jnp.sum(white * white, axis=1, keepdims=True) + epsilon)
    unit = white * unit_scale
    gap = 2.0 * unit - exact(same[...], unit, ((1,), (0,)))
    loss_out[...] = jnp.broadcast_to(jnp.sum(jnp.sum(gap * gap, axis=1, keepdims=True), axis=0, keepdims=True) * share, (8, 128))
    grad_white = unit_scale * (gap - unit * jnp.sum(unit * gap, axis=1, keepdims=True))
    gram = exact(grad_white, white, ((0,), (0,)))
    half = jnp.where(row > column, gram, jnp.where(row == column, 0.5 * gram, 0.0))
    both = half + jnp.transpose(half)
    grad_moved = exact(grad_white - exact(white, both, ((1,), (0,))) * share, inverse, ((1,), (0,)))
    dcodes = grad_moved - jnp.sum(grad_moved, axis=0, keepdims=True) * share

    move(pool_movers)
    high, low = split(dcodes)

    @pl.loop(0, proj // 256)
    def _(n):
        cols = pl.ds(pl.multiple_of(n * 256, 256), 256)
        right = wc[cols, :]
        grad = mm_nt(high, right) + mm_nt(low, right)
        level_here = block(0, n)[...]
        sig = sigmoid(level_here)
        grad = grad * (sig * (1.0 + level_here * (1.0 - sig)))
        normal_here = block(1, n)[...]
        total = jnp.sum(grad, axis=0, keepdims=True)
        dot = jnp.sum(grad * normal_here, axis=0, keepdims=True)
        grad_norm_out[pl.ds(0, 1), cols] = dot
        grad_norm_out[pl.ds(1, 1), cols] = total
        block(3, n)[...] = upstream[pl.ds(0, 1), cols] * (grad - (total + normal_here * dot) * share)

    move(pool_movers)
    own_rows = [gr[pl.ds(pl.multiple_of(1536 + 256 * h + me * 8, 8), 8), :] for h in range(2)]
    mine = jnp.concatenate(own_rows, axis=1)
    high = mine.astype(bf16).astype(f32)
    both_terms = jnp.concatenate([high, mine - high], axis=0).astype(bf16)

    @pl.loop(0, width // 256)
    def _(n):
        cols = pl.ds(pl.multiple_of(n * 256, 256), 256)
        value = mm_nt(both_terms[:, :half_proj], ws[cols, :])
        value = value + mm_nt(both_terms[:, half_proj:], ws[pl.ds(pl.multiple_of(width + n * 256, 256), 256), :])
        up = (value[0:8] + value[8:16]) * columns_of(inverse_counts, 256)
        upstream[:, cols] = up
        pair4[sub, pl.ds(0, 1), cols] = jnp.sum(up * sums[pl.ds(0, 8), cols], axis=0, keepdims=True)
        pair4[sub, pl.ds(1, 1), cols] = jnp.sum(up * sums[pl.ds(8, 8), cols], axis=0, keepdims=True)

    loads[7].start()
    fourth = tree_gen(pair4, plane4, line4, send.at[pl.ds(6, 3)], recv.at[pl.ds(6, 3)], third_sums)
    next(fourth)
    code_out = []
    code_high, code_low = split(dcodes)
    code_terms = jnp.concatenate([code_high, code_high, code_low], axis=0)
    for n in range(proj // 256):
        high, low = split(block(2, n)[...])
        place_at = codes_buf if n == 2 else same.at[:, pl.ds(128 * (n % 2), 128)]
        if n == 3:
            code_out[1].wait()
        place_at[...] = mm_tn(jnp.concatenate([high, low, high], axis=0), code_terms)
        code_out.append(pltpu.make_async_copy(place_at, projector.at[pl.ds(width + 256 * n, 256), pl.ds(0, codes_buf.shape[1])], save.at[1 + n]))
        code_out[n].start()
    next(fourth)
    saves.extend(code_out[k] for k in (0, 2, 3))
    for mover in pool_movers:
        for _ in mover:
            pass
    next(fourth)
    next(fourth, None)
    third_grad[pl.ds(0, 1), :] = third_sums[pl.ds(1, 1), :]
    third_grad[pl.ds(1, 1), :] = third_sums[pl.ds(0, 1), :]


    def third_part(lo, hi):
        @pl.loop(lo, hi)
        def _(n):
            cols = pl.ds(pl.multiple_of(n * 256, 256), 256)
            share = 1.0 / stats[pl.ds(6, 1), cols]
            total, dot = third_sums[pl.ds(0, 1), cols] * share, third_sums[pl.ds(1, 1), cols] * share
            gain = norm_expand[pl.ds(0, 1), cols] * stats[pl.ds(5, 1), cols]
            up = upstream[:, cols]
            for k in range(SIDE):
                rows = pl.ds(64 * k, 64)
                value = (dsum[rows, cols].reshape(8, 8, 256) * up[None]).reshape(64, 256)
                dsum[rows, cols] = value
                value = (value - total - normed[rows, cols] * dot) * gain
                dexp[rows, cols] = (columns_of(mask[rows, :], 256) * value).astype(bf16)

        @pl.loop(lo, hi)
        def _(n):
            cols = pl.ds(pl.multiple_of(n * 256, 256), 256)
            big[:, cols] = mm(act2[...], dexp[:, cols])

    def third_norm():
        for copy in saves:
            copy.wait()
        third_part(0, width // 512)

    def third_rest():
        third_part(width // 512, width // 256)

    def slope_pass(values, source, norm, at, buf):
        centre, scale = stats[pl.ds(at, 1), pl.ds(0, inner)], stats[pl.ds(at + 1, 1), pl.ds(0, inner)]

        def block(k, carry):
            s1, s2 = carry
            rows = pl.ds(pl.multiple_of(k * 32, 32), 32)
            normal = (source[rows, :] - centre) * scale
            point = norm[pl.ds(0, 1), :] * normal + norm[pl.ds(1, 1), :]
            sig = sigmoid(point)
            value = columns_of(mask[rows, :], inner) * values[rows, :] * (sig * (1.0 + point * (1.0 - sig)))
            values[rows, :] = value
            return s1 + fold8(value), s2 + fold8(value * normal)

        zero = jnp.zeros((8, inner), f32)
        s1, s2 = lax.fori_loop(0, ROWS // 32, block, (zero, zero))
        buf[me, pl.ds(0, 1), :] = jnp.sum(s1, axis=0, keepdims=True)
        buf[me, pl.ds(1, 1), :] = jnp.sum(s2, axis=0, keepdims=True)

    def norm_pass(values, source, norm, at, total, grad_norm, store):
        centre, scale = stats[pl.ds(at, 1), pl.ds(0, inner)], stats[pl.ds(at + 1, 1), pl.ds(0, inner)]
        share = 1.0 / stats[pl.ds(6, 1), pl.ds(0, inner)]
        grad_norm[pl.ds(0, 1), :] = total[1:2]
        grad_norm[pl.ds(1, 1), :] = total[0:1]
        gain = norm[pl.ds(0, 1), :] * scale
        mean, dot = total[0:1] * share, total[1:2] * share

        @pl.loop(0, ROWS // 32)
        def _(k):
            rows = pl.ds(pl.multiple_of(k * 32, 32), 32)
            normal = (source[rows, :] - centre) * scale
            value = values[rows, :] - mean - normal * dot
            store(k, columns_of(mask[rows, :], inner) * (value * gain))

    def spatial_level():

        @pl.loop(0, inner // 256)
        def _(n):
            cols = pl.ds(pl.multiple_of(n * 256, 256), 256)
            level[:, cols] = mm_nt(dexp[...], we[cols, :])

        loads[8].start()
        slope_pass(level, spatial, norm_spatial, 2, buf5)
        direct_start(buf5, send.at[9], recv.at[9])

    def spatial_norm():
        total = direct_finish(buf5, send.at[9], recv.at[9])

        def store(k, value):
            wide[pl.ds(pl.multiple_of(k * 32 + 8, 8), 32), :] = value
            shifted[pl.ds(pl.multiple_of(k * 32 + 64, 32), 32), pl.ds(inner, inner)] = value.astype(bf16)

        norm_pass(level, spatial, norm_spatial, 2, total, grad_norm_spatial, store)

        @pl.loop(0, ROWS // 32)
        def _(k):
            for b in (0, 2):
                rows = wide[pl.ds(pl.multiple_of(k * 32 + 16 - 8 * b, 8), 32), :]
                shifted[pl.ds(pl.multiple_of(k * 32 + 64, 32), 32), pl.ds(b * inner, inner)] = rows.astype(bf16)

    def spatial_weights():
        @pl.loop(0, 9)
        def _(tap):
            rows = pl.ds(pl.multiple_of(128 - 64 * (tap // 3), 64), ROWS)
            right = shifted[rows, pl.ds(pl.multiple_of(lax.rem(tap, 3) * inner, inner), inner)]
            gs[pl.ds(pl.multiple_of(tap * inner, inner), inner), :] = mm(act1[...], right)

    def reduce_level():
        loads[7].wait()

        @pl.loop(0, inner // 256)
        def _(n):
            cols = pl.ds(pl.multiple_of(n * 256, 256), 256)

            left = jnp.concatenate([shifted[pl.ds(128 - 64 * a, ROWS), :] for a in range(3)], axis=1)
            right = [ws[pl.ds(pl.multiple_of(tap * inner + n * 256, 256), 256), :] for tap in range(9)]
            level[:, cols] = mm_nt(left, jnp.concatenate(right, axis=1))

        slope_pass(level, reduced, norm_reduce, 0, buf6)
        direct_start(buf6, send.at[10], recv.at[10])

    def reduce_norm():
        total = direct_finish(buf6, send.at[10], recv.at[10])

        def store(k, value):
            dred[pl.ds(pl.multiple_of(k * 32, 32), 32), :] = value.astype(bf16)

        norm_pass(level, reduced, norm_reduce, 0, total, grad_norm_reduce, store)

    def reduce_weights():
        loads[8].wait()

        @pl.loop(0, width // 256)
        def _(n):
            cols = pl.ds(pl.multiple_of(n * 256, 256), 256)
            gr[cols, :] = mm_tn(masked[:, cols], dred[...])

    def image_values():
        @pl.loop(0, width // 256)
        def _(n):
            cols = pl.ds(pl.multiple_of(n * 256, 256), 256)
            value = dsum[:, cols] + mm_nt(dred[...], wr[cols, :])
            dsum[:, cols] = value * columns_of(mask[...], 256)


    def pooled_part(h):
        cols = pl.ds(h * half_proj * 2, half_proj * 2)
        return pltpu.make_async_copy(pooled_out.at[:, :, :, :, cols], proj_all, load.at[9 + h])

    def project_terms():
        pooled_part(0).start()
        for h in range(2):
            high, low = split(gr[pl.ds(1536 + 256 * h, 256), :])
            for k, part in enumerate((high, high, low)):
                ws[pl.ds(768 * h + 256 * k, 256), :] = part

    project_out = []

    def project_block(m):
        spare = ((level, 0), (reduced, 0)) if m % 2 == 0 else ((spatial, 0), (wide, 8))
        if m == 0:
            pooled_part(0).wait()
        if m == 4:
            pooled_part(1).start()
            pooled_part(1).wait()
        for copy in project_out[2 * m - 4 : 2 * m - 2] if m >= 2 else []:
            copy.wait()
        block_rows = proj_all[:, :, :, :, pl.ds(256 * (m % 4), 256)].reshape(256, 256)
        high, low = split(jnp.transpose(block_rows))
        left = jnp.concatenate([high, low, high], axis=1)
        for h, (ref, start) in enumerate(spare):
            ref[pl.ds(start, 256), :] = mm(left, ws[pl.ds(768 * h, 768), :])
            copy = pltpu.make_async_copy(
                ref.at[pl.ds(start, 256)],
                projector.at[pl.ds(256 * m, 256), pl.ds(512 * h, 512)],
                wsem.at[m, h],
            )
            copy.start()
            project_out.append(copy)

    grads = (gs, gr, big)
    lands = (land_s, land_r, land_e)

    def make_job(j):
        k, r0, rows, c0, cols, ring_first = JOBS[j]
        half = grads[k].shape[0] // 2

        def cut(ref, base):
            return ref.at[pl.ds(pl.multiple_of(base + r0, 8), rows), pl.ds(c0, cols)]

        return Job(
            ring_first,
            rows,
            cut(grads[k], sub * half),
            cut(grads[k], (1 - sub) * half),
            cut(lands[k], 0),
            scratches[j],
            jsend.at[j],
            jrecv.at[j],
            jfree.at[j],
        ).run()

    steps = (
        third_norm, third_rest, spatial_level, spatial_norm, spatial_weights,
        reduce_level, reduce_norm, reduce_weights, image_values, project_terms,
        *[functools.partial(project_block, m) for m in range(8)],
    )
    jobs = [make_job(j) for j in range(len(JOBS))]
    for item in ORDER:
        if item < 0:
            steps[-1 - item]()
        else:
            next(jobs[item], None)
    for job in jobs:
        for _ in job:
            pass
    for copy in project_out[-4:]:
        copy.wait()


def training_step(
    images, pixel_mask, pair_row, w_reduce, w_spatial, w_expand, w_project, w_code,
    norm_reduce, norm_spatial, norm_expand, norm_project,
):
    width, inner = w_reduce.shape
    proj, code = w_code.shape
    hbm = pl.BlockSpec(memory_space=pl.ANY)
    vmem = pl.BlockSpec(memory_space=pltpu.VMEM)
    shape = jax.ShapeDtypeStruct
    landings = [
        pltpu.VMEM((landing_rows(ring_first, rows), cols), f32) for _, _, rows, _, cols, ring_first in JOBS
    ]
    return pl.pallas_call(
        step_kernel,
        out_shape=[
            shape((4, 4, 2, 8, width), f32),
            shape((PROJECTOR_ROWS, proj), f32),
            shape((ROWS, width), bf16),
            pltpu.VMEM((8, 128), f32),
            pltpu.VMEM((2, proj), f32),
            pltpu.VMEM((2, width), f32),
            pltpu.VMEM((2, inner), f32),
            pltpu.VMEM((2, inner), f32),
            pltpu.VMEM((ROWS, width), f32),
            pltpu.VMEM((9 * inner, inner), f32),
            pltpu.VMEM((width, inner), f32),
            pltpu.VMEM((inner, width), f32),
        ],
        in_specs=[hbm, vmem, vmem] + [hbm] * 5 + [vmem] * 4,
        out_specs=[hbm] * 3 + [vmem] * 9,
        scratch_shapes=[
            pltpu.VMEM((49, 8, width), bf16),
            pltpu.VMEM((width, inner), bf16),
            pltpu.VMEM((9 * inner, inner), bf16),
            pltpu.VMEM((inner, width), bf16),
            pltpu.VMEM((proj, code), bf16),
            pltpu.VMEM((ROWS, width), bf16),
            pltpu.VMEM((ROWS, inner), f32),
            pltpu.VMEM((ROWS, inner), f32),
            pltpu.VMEM((inner, ROWS), bf16),
            pltpu.VMEM((inner, ROWS), bf16),
            pltpu.VMEM((ROWS, inner), bf16),
            pltpu.VMEM((ROWS, inner), f32),
            pltpu.VMEM((ROWS + 16, inner), f32),
            pltpu.VMEM((ROWS + 128, 3 * inner), bf16),
            pltpu.VMEM((ROWS, 128), f32),
            pltpu.VMEM((8, width), f32),
            pltpu.VMEM((8, width), f32),
            pltpu.VMEM((8, proj), f32),
            pltpu.VMEM((4, 4, 2, 8, proj), f32),
            pltpu.VMEM((256, 256), f32),
            pltpu.VMEM((256, code), f32),
            pltpu.VMEM((8, 128), f32),
            pltpu.VMEM((16, width), f32),
            pltpu.VMEM((2, width), f32),
            pltpu.VMEM((2, width), f32),
            pltpu.VMEM((8, width), f32),
            pltpu.VMEM((32, 2, inner + 128), f32),
            pltpu.VMEM((32, 2, inner), f32),
            pltpu.VMEM((32, 2, inner), f32),
            pltpu.VMEM((32, 2, inner), f32),
            pltpu.VMEM((2, 2, width), f32),
            pltpu.VMEM((4, 2, width), f32),
            pltpu.VMEM((4, 2, width), f32),
            pltpu.VMEM((2, 2, width), f32),
            pltpu.VMEM((4, 2, width), f32),
            pltpu.VMEM((4, 2, width), f32),
            pltpu.VMEM((9 * inner // 2, inner), f32),
            pltpu.VMEM((width // 2, inner), f32),
            pltpu.VMEM((inner // 2, width), f32),
            *landings,
            pltpu.SemaphoreType.DMA((11,)),
            pltpu.SemaphoreType.DMA((6,)),
            pltpu.SemaphoreType.DMA((11,)),
            pltpu.SemaphoreType.DMA((11,)),
            pltpu.SemaphoreType.DMA((2, 14)),
            pltpu.SemaphoreType.DMA((2, 14)),
            pltpu.SemaphoreType.DMA((2, 14)),
            pltpu.SemaphoreType.DMA((2, 14)),
            pltpu.SemaphoreType.DMA((len(JOBS), JOB_SEMS)),
            pltpu.SemaphoreType.DMA((len(JOBS), JOB_SEMS)),
            pltpu.SemaphoreType.REGULAR((len(JOBS),)),
            pltpu.SemaphoreType.DMA((8, 2)),
        ],
        compiler_params=pltpu.CompilerParams(
            collective_id=20, has_side_effects=True, vmem_limit_bytes=VM << 20
        ),
    )(
        images, pixel_mask, pair_row, w_reduce, w_spatial, w_expand, w_project, w_code,
        norm_reduce, norm_spatial, norm_expand, norm_project,
    )


PARTS = 2


def finish_kernel(
    projector, loss, n1, n2, n3, n4, g1, g2, g3, g4,
    project_out, code_out, loss_out, o1, o2, o3, o4, h1, h2, h3, h4,
    held, held_code, sems, load, save,
):
    steps = held.shape[0] // 256

    def through(m):
        at = pl.ds(256 * m, 256)
        return (
            pltpu.make_async_copy(projector.at[at], held.at[at], load.at[m]),
            pltpu.make_async_copy(held.at[at], project_out.at[at], save.at[m]),
        )

    pairs = [through(m) for m in range(steps)]
    pairs.append(
        (
            pltpu.make_async_copy(
                projector.at[pl.ds(held.shape[0], held_code.shape[0]), pl.ds(0, held_code.shape[1])],
                held_code,
                load.at[steps],
            ),
            pltpu.make_async_copy(held_code, code_out, save.at[steps]),
        )
    )
    for read, _ in pairs:
        read.start()
    copies = [
        pltpu.make_async_copy(g1.at[pl.ds(64 * r, 56)], h1.at[pl.ds(56 * r, 56)], sems.at[r]) for r in range(SIDE)
    ]
    for k, (a, b) in enumerate([(g2, h2), (g3, h3), (g4, h4)]):
        part = a.shape[0] // PARTS
        for i in range(PARTS):
            at = pl.ds(part * i, part)
            copies.append(pltpu.make_async_copy(a.at[at], b.at[at], sems.at[SIDE + PARTS * k + i]))
    for copy in copies:
        copy.start()
    loss_out[...] = loss[pl.ds(0, 1), pl.ds(0, 1)]
    o1[...] = n1[...]
    o2[...] = n2[...]
    o3[...] = n3[...]
    o4[...] = n4[...]
    for read, write in pairs:
        read.wait()
        write.start()
    for _, write in pairs:
        write.wait()
    for copy in copies:
        copy.wait()


def finish(projector, project, code, loss, norms, grads):
    width = grads[0].shape[1]
    hbm = pl.BlockSpec(memory_space=pl.ANY)
    vmem = pl.BlockSpec(memory_space=pltpu.VMEM)
    shape = jax.ShapeDtypeStruct
    return pl.pallas_call(
        finish_kernel,
        out_shape=[shape(project, f32), shape(code, f32), shape((1, 1), f32)]
        + [shape(x.shape, f32) for x in norms]
        + [shape((392, width), f32)]
        + [shape(x.shape, f32) for x in grads[1:]],
        in_specs=[hbm] + [vmem] * 9,
        out_specs=[hbm] * 2 + [vmem] * 5 + [hbm] * 4,
        scratch_shapes=[
            pltpu.VMEM(project, f32),
            pltpu.VMEM(code, f32),
            pltpu.SemaphoreType.DMA((SIDE + 3 * PARTS,)),
            pltpu.SemaphoreType.DMA((project[0] // 256 + 1,)),
            pltpu.SemaphoreType.DMA((project[0] // 256 + 1,)),
        ],
        compiler_params=pltpu.CompilerParams(vmem_limit_bytes=14 << 20),
    )(projector, loss, *norms, *grads)


def whiten(codes, pairing):
    highest = lax.Precision.HIGHEST
    total = codes.shape[0]
    centre = jnp.sum(codes, axis=0) / total
    moved = codes - centre
    covariance = jnp.dot(moved.T, moved, precision=highest) / total
    covariance = covariance + whiten_floor * jnp.eye(codes.shape[1], dtype=jnp.float32)
    factor = jnp.linalg.cholesky(covariance)
    inverse = lax.linalg.triangular_solve(factor, jnp.eye(codes.shape[1], dtype=jnp.float32), left_side=True, lower=True)
    white = jnp.dot(moved, inverse.T, precision=highest)
    scale = lax.rsqrt(jnp.sum(white * white, axis=1, keepdims=True) + epsilon)
    unit = white * scale
    same = (pairing[:, None] == pairing[None, :]).astype(jnp.float32)
    gap = 2.0 * unit - jnp.dot(same, unit, precision=highest)
    loss_value = jnp.sum(gap * gap) / total
    grad_unit = 0.5 * (2.0 * gap - jnp.dot(same, gap, precision=highest))
    grad_white = scale * grad_unit - white * scale * scale * scale * jnp.sum(white * grad_unit, axis=1, keepdims=True)
    gram = jnp.dot(grad_white.T, white, precision=highest)
    row = lax.broadcasted_iota(jnp.int32, gram.shape, 0)
    column = lax.broadcasted_iota(jnp.int32, gram.shape, 1)
    lower = jnp.where(row > column, gram, jnp.where(row == column, 0.5 * gram, 0.0))
    both = lower + lower.T
    grad_moved = jnp.dot(grad_white - jnp.dot(white, both, precision=highest) / total, inverse, precision=highest)
    return loss_value, grad_moved - jnp.sum(grad_moved, axis=0) / total


def silu_slope(values):
    sigmoid_value = jax.nn.sigmoid(values)
    return sigmoid_value * (1.0 + values * (1.0 - sigmoid_value))


def moments(sum_value, sum_square, total_count):
    centre = sum_value / total_count
    return (centre, lax.rsqrt(sum_square / total_count - centre * centre + epsilon))


def make_columns(activation):
    images_here, pixel_count, inner_width = activation.shape
    grid_map = activation.reshape(images_here, SIDE, SIDE, inner_width)
    padded = jnp.pad(grid_map, ((0, 0), (1, 1), (1, 1), (0, 0)))
    pieces = [
        padded[:, tap_row : tap_row + SIDE, tap_col : tap_col + SIDE, :]
        for tap_row in range(3)
        for tap_col in range(3)
    ]
    return jnp.concatenate(pieces, axis=3).reshape(images_here * pixel_count, 9 * inner_width)


def fold_columns(columns, images_here, inner_width):
    tap_grads = columns.reshape(images_here, SIDE, SIDE, 9, inner_width)
    padded = jnp.zeros((images_here, SIDE + 2, SIDE + 2, inner_width), jnp.float32)
    for tap_row in range(3):
        for tap_col in range(3):
            padded = padded.at[:, tap_row : tap_row + SIDE, tap_col : tap_col + SIDE, :].add(
                tap_grads[:, :, :, 3 * tap_row + tap_col, :]
            )
    return padded[:, 1 : SIDE + 1, 1 : SIDE + 1, :].reshape(images_here, SIDE * SIDE, inner_width)


def pixel_sums(values, weight):
    return (jnp.sum(values * weight, axis=(0, 1)), jnp.sum(values * values * weight, axis=(0, 1)))


def front(
    masked_low,
    weight,
    counts,
    w_reduce,
    w_spatial,
    w_expand,
    norm_reduce,
    norm_spatial,
    norm_expand,
):
    images_here, pixel_count, width = masked_low.shape
    inner_width = w_reduce.shape[1]
    rows_here = images_here * pixel_count
    reduced = jnp.dot(
        masked_low.reshape(rows_here, width), w_reduce, preferred_element_type=jnp.float32
    ).reshape(images_here, pixel_count, inner_width)
    sum_reduce, square_reduce = pixel_sums(reduced, weight)
    sum_reduce, square_reduce, valid_total = lax.psum((sum_reduce, square_reduce, jnp.sum(counts)), ("dp", "sub"))
    centre_reduce, scale_reduce = moments(sum_reduce, square_reduce, valid_total)
    normed_reduce = (reduced - centre_reduce) * scale_reduce
    level_reduce = norm_reduce[0] * normed_reduce + norm_reduce[1]
    act_reduce = (weight * jax.nn.silu(level_reduce)).astype(jnp.bfloat16)
    columns = make_columns(act_reduce)
    spatial = jnp.dot(
        columns, w_spatial.reshape(9 * inner_width, inner_width), preferred_element_type=jnp.float32
    ).reshape(images_here, pixel_count, inner_width)
    sum_spatial, square_spatial = pixel_sums(spatial, weight)
    sum_spatial, square_spatial = lax.psum((sum_spatial, square_spatial), ("dp", "sub"))
    centre_spatial, scale_spatial = moments(sum_spatial, square_spatial, valid_total)
    normed_spatial = (spatial - centre_spatial) * scale_spatial
    level_spatial = norm_spatial[0] * normed_spatial + norm_spatial[1]
    act_spatial = (weight * jax.nn.silu(level_spatial)).astype(jnp.bfloat16)
    expanded = jnp.dot(
        act_spatial.reshape(rows_here, inner_width), w_expand, preferred_element_type=jnp.float32
    ).reshape(images_here, pixel_count, width)
    sum_expand, square_expand = pixel_sums(expanded, weight)
    sum_expand, square_expand = lax.psum((sum_expand, square_expand), ("dp", "sub"))
    centre_expand, scale_expand = moments(sum_expand, square_expand, valid_total)
    normed_expand = (expanded - centre_expand) * scale_expand
    summed = masked_low.astype(jnp.float32) + norm_expand[0] * normed_expand + norm_expand[1]
    stats = (
        valid_total,
        centre_reduce,
        scale_reduce,
        centre_spatial,
        scale_spatial,
        centre_expand,
        scale_expand,
    )
    return (
        (
            normed_reduce,
            level_reduce,
            columns,
            normed_spatial,
            level_spatial,
            act_spatial,
            normed_expand,
            summed,
        ),
        stats,
    )


def norm_back(upstream, normed, gain, scale_value, sum_grad, dot_grad, total_count):
    return gain * scale_value * (upstream - (sum_grad + normed * dot_grad) / total_count)


def plain_shards(
    images,
    pixel_mask,
    pairing,
    w_reduce,
    w_spatial,
    w_expand,
    w_project,
    w_code,
    norm_reduce,
    norm_spatial,
    norm_expand,
    norm_project,
):
    images_here, pixel_count, width = images.shape
    inner_width = w_reduce.shape[1]
    images_total = pairing.shape[0]
    rows_here = images_here * pixel_count
    highest = lax.Precision.HIGHEST
    weight = pixel_mask.astype(jnp.float32)[:, :, None]
    counts = jnp.sum(weight, axis=1)
    masked_low = images * weight.astype(jnp.bfloat16)
    project_full = w_project.astype(jnp.float32)
    code_full = w_code.astype(jnp.float32)
    saved, stats = front(
        masked_low,
        weight,
        counts,
        w_reduce,
        w_spatial,
        w_expand,
        norm_reduce,
        norm_spatial,
        norm_expand,
    )
    (
        normed_reduce,
        level_reduce,
        columns,
        normed_spatial,
        level_spatial,
        act_spatial,
        normed_expand,
        summed,
    ) = saved
    (
        valid_total,
        centre_reduce,
        scale_reduce,
        centre_spatial,
        scale_spatial,
        centre_expand,
        scale_expand,
    ) = stats
    output = weight * jax.nn.silu(summed)
    own_pooled = jnp.sum(output, axis=1) / counts
    pooled = lax.all_gather(own_pooled, ("dp", "sub"), axis=0, tiled=True)
    projected = jnp.dot(pooled, project_full, precision=highest)
    centre_project, scale_project = moments(
        jnp.sum(projected, axis=0), jnp.sum(projected * projected, axis=0), float(images_total)
    )
    normed_project = (projected - centre_project) * scale_project
    level_project = norm_project[0] * normed_project + norm_project[1]
    hidden = jax.nn.silu(level_project)
    codes = jnp.dot(hidden, code_full, precision=highest)
    loss_value, grad_codes = whiten(codes, pairing)
    grad_w_code = jnp.dot(hidden.T, grad_codes, precision=highest)
    grad_hidden = jnp.dot(grad_codes, code_full.T, precision=highest)
    grad_level_project = grad_hidden * silu_slope(level_project)
    sum_project_grad = jnp.sum(grad_level_project, axis=0)
    dot_project_grad = jnp.sum(grad_level_project * normed_project, axis=0)
    grad_norm_project = jnp.stack([dot_project_grad, sum_project_grad])
    grad_projected = norm_back(
        grad_level_project,
        normed_project,
        norm_project[0],
        scale_project,
        sum_project_grad,
        dot_project_grad,
        float(images_total),
    )
    grad_w_project = jnp.dot(pooled.T, grad_projected, precision=highest)
    own_start = lax.axis_index(("dp", "sub")) * images_here
    own_projected = lax.dynamic_slice_in_dim(grad_projected, own_start, images_here, 0)
    grad_pooled = jnp.dot(own_projected, project_full.T, precision=highest)
    grad_summed = weight * (grad_pooled / counts)[:, None, :] * silu_slope(summed)
    sum_expand_grad, dot_expand_grad = lax.psum(
        (jnp.sum(grad_summed, axis=(0, 1)), jnp.sum(grad_summed * normed_expand, axis=(0, 1))), ("dp", "sub")
    )
    grad_norm_expand = jnp.stack([dot_expand_grad, sum_expand_grad])
    grad_expanded = (
        (
            weight
            * norm_back(
                grad_summed,
                normed_expand,
                norm_expand[0],
                scale_expand,
                sum_expand_grad,
                dot_expand_grad,
                valid_total,
            )
        )
        .astype(jnp.bfloat16)
        .reshape(rows_here, width)
    )
    grad_w_expand = jnp.einsum(
        "rm,rc->mc",
        act_spatial.reshape(rows_here, inner_width),
        grad_expanded,
        preferred_element_type=jnp.float32,
    )
    grad_act_spatial = jnp.einsum(
        "rc,mc->rm", grad_expanded, w_expand, preferred_element_type=jnp.float32
    ).reshape(images_here, pixel_count, inner_width)
    grad_level_spatial = grad_act_spatial * weight * silu_slope(level_spatial)
    sum_spatial_grad, dot_spatial_grad = lax.psum(
        (
            jnp.sum(grad_level_spatial, axis=(0, 1)),
            jnp.sum(grad_level_spatial * normed_spatial, axis=(0, 1)),
        ),
        ("dp", "sub"),
    )
    grad_norm_spatial = jnp.stack([dot_spatial_grad, sum_spatial_grad])
    grad_spatial_out = (
        (
            weight
            * norm_back(
                grad_level_spatial,
                normed_spatial,
                norm_spatial[0],
                scale_spatial,
                sum_spatial_grad,
                dot_spatial_grad,
                valid_total,
            )
        )
        .astype(jnp.bfloat16)
        .reshape(rows_here, inner_width)
    )
    grad_w_spatial = jnp.einsum(
        "rk,rm->km", columns, grad_spatial_out, preferred_element_type=jnp.float32
    ).reshape(3, 3, inner_width, inner_width)
    grad_columns = jnp.einsum(
        "rm,km->rk",
        grad_spatial_out,
        w_spatial.reshape(9 * inner_width, inner_width),
        preferred_element_type=jnp.float32,
    )
    grad_act_reduce = fold_columns(grad_columns, images_here, inner_width)
    grad_level_reduce = grad_act_reduce * weight * silu_slope(level_reduce)
    sum_reduce_grad, dot_reduce_grad = lax.psum(
        (
            jnp.sum(grad_level_reduce, axis=(0, 1)),
            jnp.sum(grad_level_reduce * normed_reduce, axis=(0, 1)),
        ),
        ("dp", "sub"),
    )
    grad_norm_reduce = jnp.stack([dot_reduce_grad, sum_reduce_grad])
    grad_reduced = (
        (
            weight
            * norm_back(
                grad_level_reduce,
                normed_reduce,
                norm_reduce[0],
                scale_reduce,
                sum_reduce_grad,
                dot_reduce_grad,
                valid_total,
            )
        )
        .astype(jnp.bfloat16)
        .reshape(rows_here, inner_width)
    )
    grad_w_reduce = jnp.einsum(
        "rc,rm->cm",
        masked_low.reshape(rows_here, width),
        grad_reduced,
        preferred_element_type=jnp.float32,
    )
    grad_input = jnp.einsum(
        "rm,cm->rc", grad_reduced, w_reduce, preferred_element_type=jnp.float32
    ).reshape(images_here, pixel_count, width)
    grad_images = weight * (grad_summed + grad_input)
    grad_w_spatial, grad_w_reduce, grad_w_expand = lax.psum(
        (grad_w_spatial, grad_w_reduce, grad_w_expand), ("dp", "sub")
    )
    return (
        loss_value,
        grad_images,
        grad_w_reduce,
        grad_w_spatial.reshape(3, 3, inner_width, inner_width),
        grad_w_expand,
        grad_w_project,
        grad_w_code,
        grad_norm_reduce,
        grad_norm_spatial,
        grad_norm_expand,
        grad_norm_project,
    )


def shards(
    images,
    pixel_mask,
    pairing,
    w_reduce,
    w_spatial,
    w_expand,
    w_project,
    w_code,
    norm_reduce,
    norm_spatial,
    norm_expand,
    norm_project,
):
    width, inner = w_reduce.shape
    taps = w_spatial.reshape(9 * inner, inner)
    (
        _, projector, _, loss,
        grad_norm_project, grad_norm_expand, grad_norm_reduce, grad_norm_spatial,
        grad_images, grad_spatial, grad_reduce, grad_expand,
    ) = training_step(
        jnp.transpose(images, (1, 0, 2)),
        pixel_mask,
        pairing.reshape(1, 256),
        w_reduce,
        taps,
        w_expand,
        w_project,
        w_code,
        norm_reduce,
        norm_spatial,
        norm_expand,
        norm_project,
    )
    (
        grad_project, grad_code, loss,
        grad_norm_reduce, grad_norm_spatial, grad_norm_expand, grad_norm_project,
        grad_images, grad_spatial, grad_reduce, grad_expand,
    ) = finish(
        projector,
        w_project.shape,
        w_code.shape,
        loss,
        (grad_norm_reduce, grad_norm_spatial, grad_norm_expand, grad_norm_project),
        (grad_images, grad_spatial, grad_reduce, grad_expand),
    )
    return (
        loss[0, 0],
        jnp.transpose(grad_images.reshape(49, 8, width), (1, 0, 2)),
        grad_reduce,
        grad_spatial.reshape(w_spatial.shape),
        grad_expand,
        grad_project,
        grad_code,
        grad_norm_reduce,
        grad_norm_spatial,
        grad_norm_expand,
        grad_norm_project,
    )


def solution(mesh):
    fits = mesh.shape["dp"] == 16 and mesh.shape["sub"] == 2
    placed = (P(("dp", "sub"), None, None), P(("dp", "sub"), None)) + (P(),) * 10
    return jax.shard_map(
        shards if fits else plain_shards,
        mesh=mesh,
        in_specs=placed,
        out_specs=(P(), P(("dp", "sub"), None, None)) + (P(),) * 9,
        check_vma=False,
    )
```

```python
import functools
import jax
import jax.numpy as jnp
from jax import lax
from jax.experimental import pallas as pl
from jax.experimental.pallas import tpu as pltpu
from jax.sharding import PartitionSpec as P

MESH = pl.DeviceIdType.MESH
SIDE = 7
SLOTS = 56
ROWS = 448
epsilon = 1e-05
whiten_floor = 0.001
f32 = jnp.float32
bf16 = jnp.bfloat16


def place():
    dp = lax.axis_index("dp")
    sub = lax.axis_index("sub")
    z = dp // 4
    y = lax.rem(dp // 2, 2)
    x = lax.rem(dp, 2)
    ring = 3 * y + x - 2 * x * y
    return dp, sub, z, ring


def plane_of(ring):
    ring = lax.rem(ring + 4, 4)
    y = ring // 2
    odd = lax.rem(ring, 2)
    return y * 2 + odd + y - 2 * odd * y


def ring_dp(z, ring):
    return z * 4 + plane_of(ring)


def dev(dp, sub):
    return {"dp": dp, "sub": sub}


def greet_start():
    dp, sub, _, _ = place()
    me = dp * 2 + sub
    barrier = pltpu.get_barrier_semaphore()

    @pl.loop(1, 32)
    def _(step):
        other = lax.rem(me + step, 32)
        pl.semaphore_signal(
            barrier, inc=1, device_id=dev(other // 2, lax.rem(other, 2)), device_id_type=MESH
        )


def greet_wait():
    pl.semaphore_wait(pltpu.get_barrier_semaphore(), 31)


def remote(src, dst, send, recv, where):
    return pltpu.make_async_remote_copy(
        src_ref=src,
        dst_ref=dst,
        send_sem=send,
        recv_sem=recv,
        device_id=dev(*where),
        device_id_type=MESH,
    )


def arrived(ref, sem):
    pltpu.make_async_copy(ref, ref, sem).wait()


def direct_start(buf, send, recv):
    dp, sub, _, _ = place()
    me = dp * 2 + sub

    @pl.loop(1, 32)
    def _(step):
        other = lax.rem(me + step, 32)
        remote(buf.at[me], buf.at[me], send, recv, (other // 2, lax.rem(other, 2))).start()


def direct_finish(buf, send, recv):
    many = buf.at[pl.ds(0, 31)]
    arrived(many, recv)
    total = jnp.sum(buf[...], axis=0)
    arrived(many, send)
    return total


def tree_gen(pair, plane, line, send, recv, result):
    dp, sub, z, _ = place()
    w = lax.rem(dp, 4)
    remote(pair.at[sub], pair.at[sub], send.at[0], recv.at[0], (dp, 1 - sub)).start()
    yield
    arrived(pair.at[0], recv.at[0])
    plane[w] = pair[0] + pair[1]
    for k in range(1, 4):
        where = (z * 4 + lax.rem(w + k, 4), sub)
        remote(plane.at[w], plane.at[w], send.at[1], recv.at[1], where).start()
    yield
    arrived(plane.at[pl.ds(0, 3)], recv.at[1])
    line[z] = (plane[0] + plane[1]) + (plane[2] + plane[3])
    for k in range(1, 4):
        where = (lax.rem(z + k, 4) * 4 + w, sub)
        remote(line.at[z], line.at[z], send.at[2], recv.at[2], where).start()
    yield
    arrived(line.at[pl.ds(0, 3)], recv.at[2])
    result[...] = (line[0] + line[1]) + (line[2] + line[3])
    arrived(pair.at[0], send.at[0])
    arrived(plane.at[pl.ds(0, 3)], send.at[1])
    arrived(line.at[pl.ds(0, 3)], send.at[2])


class Mover:
    def __init__(self, send, recv):
        self.send, self.recv, self.pending = send, recv, []

    def go(self, cond, src, dst, s, r, where):
        def body():
            remote(src, dst, self.send.at[s], self.recv.at[r], where).start()

        if cond is None:
            body()
        else:
            pl.when(cond)(body)
        self.pending.append((cond, src, s))

    def got(self, cond, ref, r, then=None):
        def body():
            arrived(ref, self.recv.at[r])
            if then is not None:
                then()

        if cond is None:
            body()
        else:
            pl.when(cond)(body)

    def drain(self):
        for cond, ref, s in self.pending:

            def body(ref=ref, s=s):
                arrived(ref, self.send.at[s])

            if cond is None:
                body()
            else:
                pl.when(cond)(body)
        self.pending = []

    def settle(self, s):
        for cond, ref, other in self.pending:
            if other == s:
                arrived(ref, self.send.at[s])
        self.pending = [item for item in self.pending if item[2] != s]

    def line_gather(self, at, first, base):
        dp, sub, z, _ = place()
        up, down = (dp + 4, sub), (dp - 4, sub)
        hold = lambda j: at(jnp.clip(j, 0, 3))
        for t in range(3):
            from_up = first if t == 0 and first is not None else hold(z - t)
            from_down = first if t == 0 and first is not None else hold(z + t)
            self.go(jnp.logical_and(z <= 2, z >= t), from_up, hold(z - t), base + t, base + t, up)
            self.go(
                jnp.logical_and(z >= 1, z <= 3 - t),
                from_down,
                hold(z + t),
                base + 3 + t,
                base + 3 + t,
                down,
            )
            yield
            self.got(z >= t + 1, hold(z - 1 - t), base + t)
            self.got(z <= 2 - t, hold(z + 1 + t), base + 3 + t)

    def line_direct(self, at, first, base):
        dp, sub, z, _ = place()
        w = lax.rem(dp, 4)
        for k in range(1, 4):
            where = (lax.rem(z + k, 4) * 4 + w, sub)
            self.go(None, first, at(z), base + k - 1, base + k - 1, where)
        yield
        for k in range(1, 4):
            self.got(None, at(lax.rem(z + 4 - k, 4)), base + k - 1)

    def ring_direct(self, blk, first, base, after):
        dp, sub, z, q = place()
        src = first if first is not None else blk(0, None)
        for k in range(1, 4):
            self.go(None, src, blk(0, None), base + k - 1, base + k - 1, (ring_dp(z, q + k), sub))
        yield
        for k in range(1, 4):
            self.got(None, blk(4 - k, None), base + k - 1)
            after(blk(4 - k, None), 3 - k)

    def ring_gather(self, blk, first, base, after):
        dp, sub, z, q = place()
        after_me, before_me = (ring_dp(z, q + 1), sub), (ring_dp(z, q + 3), sub)
        src = first if first is not None else blk(0, None)
        self.go(None, src, blk(0, None), base, base, after_me)
        self.go(None, src, blk(0, None), base + 1, base + 1, before_me)
        yield
        self.got(None, blk(3, None), base)
        self.go(None, blk(3, 0), blk(3, 0), base + 2, base + 2, after_me)
        after(blk(3, None), 0)
        self.got(None, blk(1, None), base + 1)
        self.go(None, blk(1, 1), blk(1, 1), base + 3, base + 3, before_me)
        after(blk(1, None), 1)
        yield
        self.got(None, blk(2, 0), base + 2)
        self.got(None, blk(2, 1), base + 3)
        after(blk(2, None), 2)


def run_all(gens, starts=None):
    live = dict(enumerate(gens))
    tick = 0
    while live:
        for j in sorted(live):
            if starts is None or tick >= starts[j]:
                try:
                    next(live[j])
                except StopIteration:
                    live.pop(j)
        tick += 1


def gather_rows(own, out, send, recv, split, direct=(1, 0, 1, 1)):
    dp, sub, z, q = place()
    width = out.shape[-1]
    sib = (dp, 1 - sub)

    def first_line():
        cols = pl.ds(0, split)
        mid = split // 2
        mover = Mover(send.at[0], recv.at[0])
        at = lambda j: out.at[j, plane_of(q), sub, :, cols]

        def blk(k, h):
            ring = plane_of(q + k)
            if h is None:
                return out.at[:, ring, sub, :, cols]
            return out.at[pl.ds(2 * h, 2), ring, sub, :, cols]

        def share(ref, s):
            mover.go(None, ref, ref, 10 + s, 10, sib)

        line = mover.line_direct if direct[0] else mover.line_gather
        yield from line(at, own.at[:, cols], 0)
        share(blk(0, None), 3)
        ring = mover.ring_direct if direct[1] else mover.ring_gather
        yield from ring(blk, None, 6, share)
        yield
        arrived(out.at[:, :, 1 - sub, :, cols], recv.at[0, 10])
        mover.drain()

    def first_ring():
        cols = pl.ds(split, width - split)
        mid = (width - split) // 2
        mover = Mover(send.at[1], recv.at[1])

        def blk(k, h):
            ring = plane_of(q + k)
            if h is None:
                return out.at[z, ring, sub, :, cols]
            return out.at[z, ring, sub, :, pl.ds(split + h * mid, mid)]

        at = lambda j: out.at[j, :, sub, :, cols]

        def share(ref, s):
            mover.go(None, ref, ref, 10 + s, 10, sib)

        ring = mover.ring_direct if direct[2] else mover.ring_gather
        yield from ring(blk, own.at[:, cols], 0, lambda ref, s: None)
        share(at(z), 3)
        line = mover.line_direct if direct[3] else mover.line_gather
        yield from line(at, at(z), 4)
        for k in range(1, 4):
            share(at(lax.rem(z + k, 4)), k - 1)
        yield
        arrived(out.at[:, :, 1 - sub, :, cols], recv.at[1, 10])
        mover.drain()

    return [first_line(), first_ring()]


def mm(a, b):
    return jnp.dot(a, b, preferred_element_type=f32)


def mm_nt(a, b):
    return lax.dot_general(a, b, (((1,), (1,)), ((), ())), preferred_element_type=f32)


def mm_tn(a, b):
    return lax.dot_general(a, b, (((0,), (0,)), ((), ())), preferred_element_type=f32)


def sigmoid(v):
    return 0.5 + 0.5 * jnp.tanh(0.5 * v)


def split(v):
    high = v.astype(bf16)
    return high, (v - high.astype(f32)).astype(bf16)


def exact(a, b, dims):
    return lax.dot_general(
        a, b, (dims, ((), ())), precision=lax.Precision.HIGHEST, preferred_element_type=f32
    )


def three_terms(a, b):
    a_high, a_low = split(a)
    b_high, b_low = split(b)
    return mm(a_high, b_high) + mm(a_low, b_high) + mm(a_high, b_low)


def factor_inverse(cov, block=8):
    size = cov.shape[0]
    tiles = size // 8
    row = lax.broadcasted_iota(jnp.int32, (8, size), 0)
    column = lax.broadcasted_iota(jnp.int32, (8, size), 1)
    left = [cov[8 * t : 8 * t + 8, :] for t in range(tiles)]
    right = [jnp.where(row + 8 * t == column, 1.0, 0.0) for t in range(tiles)]
    wide = lambda v: jnp.broadcast_to(v, (8, size))
    for j in range(0, size, block):
        t0, s = j // 8, j % 8
        columns = [[wide(left[t][:, j + k : j + k + 1]) for k in range(block)] for t in range(t0, tiles)]
        lefts = [wide(left[t0][s + k : s + k + 1, :]) for k in range(block)]
        rights = [wide(right[t0][s + k : s + k + 1, :]) for k in range(block)]
        entry = [[wide(columns[0][k][s + m : s + m + 1, :]) for k in range(m + 1)] for m in range(block)]
        lower = [[None] * block for _ in range(block)]
        inverses = []
        for k in range(block):
            inverse = 1.0 / entry[k][k]
            inverses.append(inverse)
            for m in range(k + 1, block):
                lower[m][k] = entry[m][k] * inverse
            for m in range(k + 1, block):
                for n in range(k + 1, m + 1):
                    entry[m][n] = entry[m][n] - lower[m][k] * entry[n][k]
        for m in range(block):
            for k in range(m):
                lefts[m] = lefts[m] - lower[m][k] * lefts[k]
                rights[m] = rights[m] - lower[m][k] * rights[k]
        scaled_left = [a * b for a, b in zip(lefts, inverses)]
        scaled_right = [a * b for a, b in zip(rights, inverses)]
        for t in range(t0, tiles):
            if t == t0 and s + block == 8 and block == 1:
                continue
            own = columns[t - t0]
            for m in range(block):
                for k in range(m):
                    own[m] = own[m] - lower[m][k] * own[k]
            for m in range(block):
                factor = own[m]
                if t == t0:
                    factor = jnp.where(row > s + m, factor, 0.0)
                left[t] = left[t] - factor * scaled_left[m]
                right[t] = right[t] - factor * scaled_right[m]
    out = []
    for t in range(tiles):
        pivots = jnp.sum(jnp.where(row + 8 * t == column, left[t], 0.0), axis=1, keepdims=True)
        out.append(right[t] * lax.rsqrt(pivots))
    return jnp.concatenate(out, axis=0)


def fold8(v):
    rows, cols = v.shape
    return jnp.sum(v.reshape(rows // 8, 8, cols), axis=0)


def columns_of(mask, cols):
    return jnp.concatenate([mask] * (cols // 128), axis=1)


def halves(ref, h):
    cols = ref.shape[1] // 2
    return ref.at[:, pl.ds(h * cols, cols)]


class Job:
    def __init__(self, ring_first, rows, acc, other, land, scratch, send, recv, free):
        self.ring_first, self.rows, self.acc, self.other = ring_first, rows, acc, other
        self.land, self.scratch, self.free = land, scratch, free
        self.mover = Mover(send, recv)
        self.taken = 0

    def take(self, rows):
        ref = rows_at(self.scratch, self.taken, rows)
        self.taken += rows
        return ref

    def ring_reduce(self, base, block):
        dp, sub, z, q = place()
        go, got = self.mover.go, self.mover.got
        after_me, before_me = (ring_dp(z, q + 1), sub), (ring_dp(z, q + 3), sub)
        r0 = self.take(block)
        r1a, r1b = self.take(block), self.take(block)

        def blk(k):
            return rows_at(self.land, base + lax.rem(q + k, 4) * block, block)

        go(None, halves(blk(2), 0), halves(r0, 0), 1, 1, after_me)
        go(None, halves(blk(2), 1), halves(r0, 1), 2, 2, before_me)
        yield
        got(None, halves(r0, 0), 1)
        add_into(halves(blk(1), 0), halves(r0, 0), block)
        go(None, blk(1), r1a, 3, 3, after_me)
        got(None, halves(r0, 1), 2)
        add_into(halves(blk(3), 1), halves(r0, 1), block)
        go(None, blk(3), r1b, 4, 4, before_me)
        yield
        got(None, r1a, 3)
        got(None, r1b, 4)
        add_into(blk(0), r1a, block, r1b)

    def line_reduce(self, base, chunk):
        dp, sub, z, _ = place()
        go, got = self.mover.go, self.mover.got
        up, down = (dp + 4, sub), (dp - 4, sub)
        low = [self.take(chunk) for _ in range(3)]
        high = [low[0], self.take(chunk), self.take(chunk)]

        def at(j):
            return rows_at(self.land, base + jnp.clip(j, 0, 3) * chunk, chunk)

        for t in range(3):
            go(z <= t, at(3 + z - t), low[t], 5 + t, 5 + t, up)
            go(z >= 3 - t, at(z - 3 + t), high[t], 8 + t, 8 + t, down)
            yield
            got(
                jnp.logical_and(z >= 1, z <= t + 1),
                low[t],
                5 + t,
                lambda: add_into(at(2 + z - t), low[t], chunk),
            )
            got(
                jnp.logical_and(z <= 2, z >= 2 - t),
                high[t],
                8 + t,
                lambda: add_into(at(z - 2 + t), high[t], chunk),
            )

    def run(self):
        dp, sub, z, q = place()
        sib = (dp, 1 - sub)
        mover, acc, rows = self.mover, self.acc, self.rows
        mover.go(None, self.other, self.land, 0, 0, sib)
        yield
        mover.got(None, self.land, 0)
        add_into(self.land, acc, rows)
        big, small = rows // 4, rows // 16

        def hand_over():
            mover.settle(0)
            pl.semaphore_signal(self.free, inc=1, device_id=dev(*sib), device_id_type=MESH)

        def total(start):
            copy_into(rows_at(acc, start, small), rows_at(self.land, start, small), small)

        def share(ref, k):
            mover.go(None, ref, ref, 21 + k, 21, sib)

        if self.ring_first:
            yield from self.ring_reduce(0, big)
            hand_over()
            yield from self.line_reduce(q * big, small)
            total(q * big + z * small)
            at = lambda j: rows_at(acc, q * big + j * small, small)
            yield from mover.line_gather(at, None, 11)
            pl.semaphore_wait(self.free, 1)
            share(rows_at(acc, q * big, big), 3)

            def blk(k, h):
                ref = rows_at(acc, lax.rem(q + k, 4) * big, big)
                return ref if h is None else halves(ref, h)

            yield from mover.ring_gather(blk, None, 17, share)
        else:
            yield from self.line_reduce(0, big)
            hand_over()
            yield from self.ring_reduce(z * big, small)
            total(z * big + q * small)

            def blk(k, h):
                ref = rows_at(acc, z * big + lax.rem(q + k, 4) * small, small)
                return ref if h is None else halves(ref, h)

            yield from mover.ring_gather(blk, None, 17, lambda ref, k: None)
            pl.semaphore_wait(self.free, 1)
            share(rows_at(acc, z * big, big), 3)
            at = lambda j: rows_at(acc, j * big, big)
            yield from mover.line_gather(at, None, 11)
            for k in range(1, 4):
                share(rows_at(acc, lax.rem(z + k, 4) * big, big), k - 1)
        yield
        arrived(self.other, mover.recv.at[21])
        mover.drain()


JOB_SEMS = 25


def add_into(dst, src, rows, more=None):
    step = 16 if rows % 16 == 0 else 8

    @pl.loop(0, rows // step)
    def _(k):
        at = pl.ds(pl.multiple_of(k * step, 8), step)
        value = dst[at, :] + src[at, :]
        dst[at, :] = value if more is None else value + more[at, :]


def copy_into(dst, src, rows):
    @pl.loop(0, rows // 8)
    def _(k):
        at = pl.ds(pl.multiple_of(k * 8, 8), 8)
        dst[at, :] = src[at, :]


def rows_at(ref, start, size):
    return ref.at[pl.ds(pl.multiple_of(start, 8), size)]


def landing_rows(ring_first, rows):
    big, small = rows // 4, rows // 16
    return 3 * big + 5 * small if ring_first else 3 * small + 5 * big


JOBS = (
    (2, 0, 256, 0, 1536, True),
    (2, 0, 256, 1536, 512, False),
    (0, 0, 512, 0, 512, True),
    (0, 512, 256, 0, 512, False),
    (0, 768, 512, 0, 512, True),
    (0, 1280, 256, 0, 512, False),
    (0, 1536, 512, 0, 512, True),
    (0, 2048, 256, 0, 512, False),
    (1, 0, 768, 0, 512, True),
    (1, 768, 256, 0, 512, False),
)

ORDER = (
    -1, -2, 0, -3, 1, 1, 0, -4, 1, -5, 3, 0, 1, 3, 2, 7, 4, -6, 7, 1, 2, 3, 6, 7,
    1, 4, 0, 3, -7, 1, 4, -10, 0, -8, 1, 7, 2, 0, -9, 5, 4, 1, 7, 8, 6, -11, 0, 4,
    3, 2, 7, 8, 1, 4, 9, 0, 7, 5, 6, 2, 1, 3, 4, 9, 0, 7, 5, -12, 8, 2, 6, 4,
    7, -13, 3, 4, 5, 2, 0, 6, 7, -14, 8, 2, 9, 4, -15, 6, 1, 5, 2, 8, 3, 7, 9, 6,
    2, 8, 5, 3, -16, 9, 6, 4, -17, 8, 9, 0, 6, 3, 9, 8, 5, 2, 3, 9, 4, 5, 6, 8,
    5, 0, 2, 7, -18, 9, 3, 8, 6, 5, 3, 7, 4, 9, 5, 8, 5, 9, 1, 6, 6, 5, 9, 2,
    8, 0, 9, 8,
)

VM = 43

PROJECTOR_ROWS = 12288


def step_kernel(
    images, pixel_mask, pair_row, w_reduce, w_spatial, w_expand, w_project, w_code,
    norm_reduce, norm_spatial, norm_expand, norm_project,
    pooled_out, projector, masked_out, loss_out,
    grad_norm_out, third_grad, grad_norm_reduce, grad_norm_spatial, dsum, gs, gr, big,
    img, wr, ws, we, wc, masked, reduced, spatial, act1, act2, dred, level, wide, shifted, mask, stats,
    own, own_proj, proj_all, same, codes_buf, counts, sums, totals, third_sums, upstream,
    buf1, buf2, buf5, buf6, pair, plane, line, pair4, plane4, line4, land_s, land_r, land_e, *rest,
):
    scratches = rest[: len(JOBS)]
    load, save, send, recv, gsend, grecv, hsend, hrecv, jsend, jrecv, jfree, wsem = rest[len(JOBS) :]
    dp, sub, z, q = place()
    me = dp * 2 + sub
    width, inner = wr.shape
    proj = wc.shape[0]
    normed = big.at[pl.ds(0, ROWS)]
    slope, dexp, act2_rows = dsum, masked, dred
    half_proj = proj // 2
    loads = [
        pltpu.make_async_copy(a, b, load.at[k])
        for k, (a, b) in enumerate(
            [(images, img), (w_reduce, wr), (w_spatial, ws), (w_expand, we), (w_code, wc)]
            + [
                (w_project.at[:, pl.ds(h * half_proj, half_proj)], ws.at[pl.ds(h * width, width)])
                for h in range(2)
            ]
            + [(w_spatial, ws), (masked_out, masked)]
        )
    ]

    def block(k, n):
        start = pl.multiple_of(512 * k + 256 * (n // 2), 256)
        return gr.at[pl.ds(start, 256), pl.ds(pl.multiple_of(lax.rem(n, 2) * 256, 256), 256)]

    loads[0].start()
    loads[1].start()
    greet_start()
    here = pixel_mask[...].astype(f32)
    counts[...] = jnp.broadcast_to(jnp.sum(here, axis=1, keepdims=True), (8, 128))
    for slot in range(SLOTS):
        r, c = slot // 8, slot % 8
        if c == SIDE:
            value = jnp.zeros((8, 128), f32)
        else:
            value = jnp.broadcast_to(here[:, SIDE * r + c : SIDE * r + c + 1], (8, 128))
        mask[pl.ds(8 * slot, 8), :] = value
    wide[pl.ds(0, 8), :] = jnp.zeros((8, inner), f32)
    wide[pl.ds(ROWS + 8, 8), :] = jnp.zeros((8, inner), f32)
    shifted[pl.ds(0, 64), :] = jnp.zeros((64, 3 * inner), bf16)
    shifted[pl.ds(512, 64), :] = jnp.zeros((64, 3 * inner), bf16)
    loads[0].wait()
    for copy in loads[2:5]:
        copy.start()
    gap = jnp.zeros((8, 256), f32)

    @pl.loop(0, width // 256)
    def _(n):
        cols = pl.ds(pl.multiple_of(n * 256, 256), 256)
        for r in range(SIDE):
            rows = img[pl.ds(SIDE * r, SIDE), :, cols].astype(f32).reshape(SIDE * 8, 256)
            rows = rows * columns_of(mask[pl.ds(64 * r, 56), :], 256)
            masked[pl.ds(64 * r, 64), cols] = jnp.concatenate([rows, gap], axis=0).astype(bf16)

    saves = []

    def keep(a, b):
        copy = pltpu.make_async_copy(a, b, save.at[len(saves)])
        copy.start()
        saves.append(copy)

    keep(masked, masked_out)
    loads[1].wait()

    @pl.loop(0, inner // 256)
    def _(n):
        cols = pl.ds(pl.multiple_of(n * 256, 256), 256)
        got = mm(masked[...], wr[:, cols])
        reduced[:, cols] = got
        buf1[me, pl.ds(0, 1), cols] = jnp.sum(got, axis=0, keepdims=True)
        buf1[me, pl.ds(1, 1), cols] = jnp.sum(got * got, axis=0, keepdims=True)

    extra = pl.ds(inner, 128)
    buf1[me, pl.ds(0, 1), extra] = jnp.sum(counts[...], axis=0, keepdims=True)
    buf1[me, pl.ds(1, 1), extra] = jnp.zeros((1, 128), f32)
    greet_wait()
    direct_start(buf1, send.at[1], recv.at[1])
    pairs = jnp.broadcast_to(pair_row[...].astype(f32), (256, 256))
    same[...] = (pairs == jnp.transpose(pairs)).astype(f32)
    first = direct_finish(buf1, send.at[1], recv.at[1])
    valid = first[0:1, inner : inner + 1]
    inverse_valid = 1.0 / valid

    def moments(total):
        centre = total[0:1] * inverse_valid
        return centre, lax.rsqrt(total[1:2] * inverse_valid - centre * centre + epsilon)

    def activate(src, norm, centre, scale, store):
        gain = norm[0:1, :] * scale
        bias = norm[1:2, :] - centre * gain

        @pl.loop(0, ROWS // 32)
        def _(k):
            rows = pl.ds(pl.multiple_of(k * 32, 32), 32)
            level = src[rows, :] * gain + bias
            store(k, columns_of(mask[rows, :], inner) * (level * sigmoid(level)))

    centre1, scale1 = moments(first[:, :inner])
    stats[pl.ds(0, 1), pl.ds(0, inner)] = centre1
    stats[pl.ds(1, 1), pl.ds(0, inner)] = scale1

    def store_wide(k, value):
        wide[pl.ds(pl.multiple_of(k * 32 + 8, 8), 32), :] = value
        shifted[pl.ds(pl.multiple_of(k * 32 + 64, 32), 32), pl.ds(inner, inner)] = value.astype(bf16)

    activate(reduced, norm_reduce, centre1, scale1, store_wide)

    @pl.loop(0, ROWS // 32)
    def _(k):
        for b in (0, 2):
            rows = wide[pl.ds(pl.multiple_of(k * 32 + 8 * b, 8), 32), :]
            shifted[pl.ds(pl.multiple_of(k * 32 + 64, 32), 32), pl.ds(b * inner, inner)] = rows.astype(bf16)

    loads[2].wait()

    @pl.loop(0, inner // 256)
    def _(n):
        cols = pl.ds(pl.multiple_of(n * 256, 256), 256)

        left = jnp.concatenate([shifted[pl.ds(64 * a, ROWS), :] for a in range(3)], axis=1)
        got = mm(left, ws[:, cols]) * columns_of(mask[...], 256)
        spatial[:, cols] = got
        buf2[me, pl.ds(0, 1), cols] = jnp.sum(got, axis=0, keepdims=True)
        buf2[me, pl.ds(1, 1), cols] = jnp.sum(got * got, axis=0, keepdims=True)

    direct_start(buf2, send.at[2], recv.at[2])
    loads[5].start()
    loads[6].start()
    act1[...] = jnp.transpose(wide[pl.ds(8, ROWS), :]).astype(bf16)
    centre2, scale2 = moments(direct_finish(buf2, send.at[2], recv.at[2]))
    stats[pl.ds(2, 1), pl.ds(0, inner)] = centre2
    stats[pl.ds(3, 1), pl.ds(0, inner)] = scale2

    def store_act2(k, value):
        wide[pl.ds(pl.multiple_of(k * 32 + 8, 8), 32), :] = value
        act2_rows[pl.ds(pl.multiple_of(k * 32, 32), 32), :] = value.astype(bf16)

    activate(spatial, norm_spatial, centre2, scale2, store_act2)
    loads[3].wait()

    @pl.loop(0, width // 256)
    def _(n):
        cols = pl.ds(pl.multiple_of(n * 256, 256), 256)
        got = mm(act2_rows[...], we[:, cols])
        normed[:, cols] = got
        pair[sub, pl.ds(0, 1), cols] = jnp.sum(got, axis=0, keepdims=True)
        pair[sub, pl.ds(1, 1), cols] = jnp.sum(got * got, axis=0, keepdims=True)

    third = tree_gen(pair, plane, line, send.at[pl.ds(3, 3)], recv.at[pl.ds(3, 3)], totals)
    next(third)
    next(third)
    act2[...] = jnp.transpose(wide[pl.ds(8, ROWS), :]).astype(bf16)
    next(third)
    next(third, None)
    centre3, scale3 = moments(totals[...])
    stats[pl.ds(4, 1), :] = centre3
    stats[pl.ds(5, 1), :] = scale3
    stats[pl.ds(6, 1), :] = jnp.broadcast_to(valid, (1, width))
    stats[pl.ds(7, 1), :] = jnp.zeros((1, width), f32)
    inverse_counts = 1.0 / counts[...]

    def last_norm(cols, rows):
        gain, bias = norm_expand[pl.ds(0, 1), cols], norm_expand[pl.ds(1, 1), cols]
        n3 = (normed[rows, cols] - stats[pl.ds(4, 1), cols]) * stats[pl.ds(5, 1), cols]
        total = masked[rows, cols].astype(f32) + gain * n3 + bias
        sig = sigmoid(total)
        return n3, sig, total * sig

    @pl.loop(0, width // 256)
    def _(n):
        cols = pl.ds(pl.multiple_of(n * 256, 256), 256)
        pool = jnp.zeros((8, 256), f32)
        for k in range(SIDE):
            rows = pl.ds(64 * k, 64)
            _, _, out = last_norm(cols, rows)
            pool = pool + fold8(columns_of(mask[rows, :], 256) * out)
        own[:, cols] = pool * columns_of(inverse_counts, 256)

    def slopes(lo, hi):
        @pl.loop(lo, hi)
        def _(n):
            cols = pl.ds(pl.multiple_of(n * 256, 256), 256)
            s1 = s2 = jnp.zeros((8, 256), f32)
            for k in range(SIDE):
                rows = pl.ds(64 * k, 64)
                n3, sig, out = last_norm(cols, rows)
                slope3 = columns_of(mask[rows, :], 256) * (sig + out * (1.0 - sig))
                normed[rows, cols] = n3
                slope[rows, cols] = slope3
                s1, s2 = s1 + fold8(slope3), s2 + fold8(slope3 * n3)
            sums[pl.ds(0, 8), cols] = s1
            sums[pl.ds(8, 8), cols] = s2

    rows_all = 256
    for k in (4, 5, 6):
        loads[k].wait()
    high = own[...].astype(bf16).astype(f32)
    both_terms = jnp.concatenate([high, own[...] - high], axis=0).astype(bf16)

    @pl.loop(0, proj // 256)
    def _(n):
        cols = pl.ds(pl.multiple_of(n * 256, 256), 256)
        rows = pl.ds(pl.multiple_of((n // 2) * width, 256), width)
        value = mm(both_terms, ws[rows, pl.ds(pl.multiple_of(lax.rem(n, 2) * 256, 256), 256)])
        own_proj[:, cols] = value[0:8] + value[8:16]

    proj_all[z, lax.rem(dp, 4), sub] = own_proj[...]
    proj_movers = gather_rows(own_proj, proj_all, gsend, grecv, proj * 3 // 4, (1, 1, 1, 1))
    pool_movers = gather_rows(own, pooled_out, hsend, hrecv, 1536, (1, 0, 1, 1))

    def move(movers):
        for mover in movers:
            next(mover, None)

    mine = pltpu.make_async_copy(own, pooled_out.at[z, lax.rem(dp, 4), sub], load.at[0])
    mine.start()
    move(proj_movers)
    slopes(0, 3)
    move(proj_movers)
    move(pool_movers)
    slopes(3, 6)
    move(proj_movers)
    slopes(6, 8)
    mine.wait()
    move(proj_movers)
    move(proj_movers)
    move(pool_movers)

    share = 1.0 / rows_all
    codes_buf[...] = jnp.zeros_like(codes_buf)

    @pl.loop(0, proj // 256)
    def _(n):
        cols = pl.ds(pl.multiple_of(n * 256, 256), 256)
        value = proj_all[:, :, :, :, cols].reshape(rows_all, 256)
        centre = jnp.sum(value, axis=0, keepdims=True) * share
        square = jnp.sum(value * value, axis=0, keepdims=True) * share
        scale = lax.rsqrt(square - centre * centre + epsilon)
        normal_here = (value - centre) * scale
        level_here = norm_project[pl.ds(0, 1), cols] * normal_here + norm_project[pl.ds(1, 1), cols]
        block(1, n)[...] = normal_here
        block(0, n)[...] = level_here
        value = level_here * sigmoid(level_here)
        block(2, n)[...] = value
        high, low = split(value)
        codes_buf[...] += mm(high, wc[cols, :]) + mm(low, wc[cols, :])
        upstream[pl.ds(0, 1), cols] = scale * norm_project[pl.ds(0, 1), cols]

    codes = codes_buf[...]

    centre = jnp.sum(codes, axis=0, keepdims=True) * share
    moved = codes - centre
    cov = exact(moved, moved, ((0,), (0,))) * share
    size = cov.shape[0]
    row = lax.broadcasted_iota(jnp.int32, (size, size), 0)
    column = lax.broadcasted_iota(jnp.int32, (size, size), 1)
    inverse = factor_inverse(cov + jnp.where(row == column, whiten_floor, 0.0))
    move(pool_movers)
    white = exact(moved, inverse, ((1,), (1,)))
    unit_scale = lax.rsqrt(jnp.sum(white * white, axis=1, keepdims=True) + epsilon)
    unit = white * unit_scale
    pairs_low = same[...].astype(bf16)
    high, low = split(unit)
    pair_sum = mm(pairs_low, high) + mm(pairs_low, low)
    gap = 2.0 * unit - pair_sum
    loss_out[...] = jnp.broadcast_to(jnp.sum(jnp.sum(gap * gap, axis=1, keepdims=True), axis=0, keepdims=True) * share, (8, 128))
    grad_white = unit_scale * (gap - unit * jnp.sum(unit * gap, axis=1, keepdims=True))
    gram = exact(grad_white, white, ((0,), (0,)))
    half = jnp.where(row > column, gram, jnp.where(row == column, 0.5 * gram, 0.0))
    both = half + jnp.transpose(half)
    grad_moved = exact(grad_white - three_terms(white, both) * share, inverse, ((1,), (0,)))
    dcodes = grad_moved - jnp.sum(grad_moved, axis=0, keepdims=True) * share

    move(pool_movers)
    high, low = split(dcodes)

    @pl.loop(0, proj // 256)
    def _(n):
        cols = pl.ds(pl.multiple_of(n * 256, 256), 256)
        right = wc[cols, :]
        grad = mm_nt(high, right) + mm_nt(low, right)
        level_here = block(0, n)[...]
        sig = sigmoid(level_here)
        grad = grad * (sig * (1.0 + level_here * (1.0 - sig)))
        normal_here = block(1, n)[...]
        total = jnp.sum(grad, axis=0, keepdims=True)
        dot = jnp.sum(grad * normal_here, axis=0, keepdims=True)
        grad_norm_out[pl.ds(0, 1), cols] = dot
        grad_norm_out[pl.ds(1, 1), cols] = total
        block(3, n)[...] = upstream[pl.ds(0, 1), cols] * (grad - (total + normal_here * dot) * share)

    move(pool_movers)
    own_rows = [gr[pl.ds(pl.multiple_of(1536 + 256 * h + me * 8, 8), 8), :] for h in range(2)]
    mine = jnp.concatenate(own_rows, axis=1)
    high = mine.astype(bf16).astype(f32)
    both_terms = jnp.concatenate([high, mine - high], axis=0).astype(bf16)

    @pl.loop(0, width // 256)
    def _(n):
        cols = pl.ds(pl.multiple_of(n * 256, 256), 256)
        value = mm_nt(both_terms[:, :half_proj], ws[cols, :])
        value = value + mm_nt(both_terms[:, half_proj:], ws[pl.ds(pl.multiple_of(width + n * 256, 256), 256), :])
        up = (value[0:8] + value[8:16]) * columns_of(inverse_counts, 256)
        upstream[:, cols] = up
        pair4[sub, pl.ds(0, 1), cols] = jnp.sum(up * sums[pl.ds(0, 8), cols], axis=0, keepdims=True)
        pair4[sub, pl.ds(1, 1), cols] = jnp.sum(up * sums[pl.ds(8, 8), cols], axis=0, keepdims=True)

    loads[7].start()
    fourth = tree_gen(pair4, plane4, line4, send.at[pl.ds(6, 3)], recv.at[pl.ds(6, 3)], third_sums)
    next(fourth)
    code_out = []
    code_high, code_low = split(dcodes)
    code_terms = jnp.concatenate([code_high, code_high, code_low], axis=0)
    for n in range(proj // 256):
        high, low = split(block(2, n)[...])
        place_at = codes_buf if n == 2 else same.at[:, pl.ds(128 * (n % 2), 128)]
        if n == 3:
            code_out[1].wait()
        place_at[...] = mm_tn(jnp.concatenate([high, low, high], axis=0), code_terms)
        code_out.append(pltpu.make_async_copy(place_at, projector.at[pl.ds(width + 256 * n, 256), pl.ds(0, codes_buf.shape[1])], save.at[1 + n]))
        code_out[n].start()
    next(fourth)
    saves.extend(code_out[k] for k in (0, 2, 3))
    for mover in pool_movers:
        for _ in mover:
            pass
    next(fourth)
    next(fourth, None)
    third_grad[pl.ds(0, 1), :] = third_sums[pl.ds(1, 1), :]
    third_grad[pl.ds(1, 1), :] = third_sums[pl.ds(0, 1), :]


    def third_part(lo, hi):
        @pl.loop(lo, hi)
        def _(n):
            cols = pl.ds(pl.multiple_of(n * 256, 256), 256)
            share = 1.0 / stats[pl.ds(6, 1), cols]
            total, dot = third_sums[pl.ds(0, 1), cols] * share, third_sums[pl.ds(1, 1), cols] * share
            gain = norm_expand[pl.ds(0, 1), cols] * stats[pl.ds(5, 1), cols]
            up = upstream[:, cols]
            for k in range(SIDE):
                rows = pl.ds(64 * k, 64)
                value = (dsum[rows, cols].reshape(8, 8, 256) * up[None]).reshape(64, 256)
                dsum[rows, cols] = value
                value = (value - total - normed[rows, cols] * dot) * gain
                dexp[rows, cols] = (columns_of(mask[rows, :], 256) * value).astype(bf16)

        @pl.loop(lo, hi)
        def _(n):
            cols = pl.ds(pl.multiple_of(n * 256, 256), 256)
            big[:, cols] = mm(act2[...], dexp[:, cols])

    def third_norm():
        for copy in saves:
            copy.wait()
        third_part(0, width // 512)

    def third_rest():
        third_part(width // 512, width // 256)

    def slope_pass(values, source, norm, at, buf):
        centre, scale = stats[pl.ds(at, 1), pl.ds(0, inner)], stats[pl.ds(at + 1, 1), pl.ds(0, inner)]

        def block(k, carry):
            s1, s2 = carry
            rows = pl.ds(pl.multiple_of(k * 32, 32), 32)
            normal = (source[rows, :] - centre) * scale
            point = norm[pl.ds(0, 1), :] * normal + norm[pl.ds(1, 1), :]
            sig = sigmoid(point)
            value = columns_of(mask[rows, :], inner) * values[rows, :] * (sig * (1.0 + point * (1.0 - sig)))
            values[rows, :] = value
            return s1 + fold8(value), s2 + fold8(value * normal)

        zero = jnp.zeros((8, inner), f32)
        s1, s2 = lax.fori_loop(0, ROWS // 32, block, (zero, zero))
        buf[me, pl.ds(0, 1), :] = jnp.sum(s1, axis=0, keepdims=True)
        buf[me, pl.ds(1, 1), :] = jnp.sum(s2, axis=0, keepdims=True)

    def norm_pass(values, source, norm, at, total, grad_norm, store):
        centre, scale = stats[pl.ds(at, 1), pl.ds(0, inner)], stats[pl.ds(at + 1, 1), pl.ds(0, inner)]
        share = 1.0 / stats[pl.ds(6, 1), pl.ds(0, inner)]
        grad_norm[pl.ds(0, 1), :] = total[1:2]
        grad_norm[pl.ds(1, 1), :] = total[0:1]
        gain = norm[pl.ds(0, 1), :] * scale
        mean, dot = total[0:1] * share, total[1:2] * share

        @pl.loop(0, ROWS // 32)
        def _(k):
            rows = pl.ds(pl.multiple_of(k * 32, 32), 32)
            normal = (source[rows, :] - centre) * scale
            value = values[rows, :] - mean - normal * dot
            store(k, columns_of(mask[rows, :], inner) * (value * gain))

    def spatial_level():

        @pl.loop(0, inner // 256)
        def _(n):
            cols = pl.ds(pl.multiple_of(n * 256, 256), 256)
            level[:, cols] = mm_nt(dexp[...], we[cols, :])

        loads[8].start()
        slope_pass(level, spatial, norm_spatial, 2, buf5)
        direct_start(buf5, send.at[9], recv.at[9])

    def spatial_norm():
        total = direct_finish(buf5, send.at[9], recv.at[9])

        def store(k, value):
            wide[pl.ds(pl.multiple_of(k * 32 + 8, 8), 32), :] = value
            shifted[pl.ds(pl.multiple_of(k * 32 + 64, 32), 32), pl.ds(inner, inner)] = value.astype(bf16)

        norm_pass(level, spatial, norm_spatial, 2, total, grad_norm_spatial, store)

        @pl.loop(0, ROWS // 32)
        def _(k):
            for b in (0, 2):
                rows = wide[pl.ds(pl.multiple_of(k * 32 + 16 - 8 * b, 8), 32), :]
                shifted[pl.ds(pl.multiple_of(k * 32 + 64, 32), 32), pl.ds(b * inner, inner)] = rows.astype(bf16)

    def spatial_weights():
        @pl.loop(0, 9)
        def _(tap):
            rows = pl.ds(pl.multiple_of(128 - 64 * (tap // 3), 64), ROWS)
            right = shifted[rows, pl.ds(pl.multiple_of(lax.rem(tap, 3) * inner, inner), inner)]
            gs[pl.ds(pl.multiple_of(tap * inner, inner), inner), :] = mm(act1[...], right)

    def reduce_level():
        loads[7].wait()

        @pl.loop(0, inner // 256)
        def _(n):
            cols = pl.ds(pl.multiple_of(n * 256, 256), 256)

            left = jnp.concatenate([shifted[pl.ds(128 - 64 * a, ROWS), :] for a in range(3)], axis=1)
            right = [ws[pl.ds(pl.multiple_of(tap * inner + n * 256, 256), 256), :] for tap in range(9)]
            level[:, cols] = mm_nt(left, jnp.concatenate(right, axis=1))

        slope_pass(level, reduced, norm_reduce, 0, buf6)
        direct_start(buf6, send.at[10], recv.at[10])

    def reduce_norm():
        total = direct_finish(buf6, send.at[10], recv.at[10])

        def store(k, value):
            dred[pl.ds(pl.multiple_of(k * 32, 32), 32), :] = value.astype(bf16)

        norm_pass(level, reduced, norm_reduce, 0, total, grad_norm_reduce, store)

    def reduce_weights():
        loads[8].wait()

        @pl.loop(0, width // 256)
        def _(n):
            cols = pl.ds(pl.multiple_of(n * 256, 256), 256)
            gr[cols, :] = mm_tn(masked[:, cols], dred[...])

    def image_values():
        @pl.loop(0, width // 256)
        def _(n):
            cols = pl.ds(pl.multiple_of(n * 256, 256), 256)
            value = dsum[:, cols] + mm_nt(dred[...], wr[cols, :])
            dsum[:, cols] = value * columns_of(mask[...], 256)


    def pooled_part(h):
        cols = pl.ds(h * half_proj * 2, half_proj * 2)
        return pltpu.make_async_copy(pooled_out.at[:, :, :, :, cols], proj_all, load.at[9 + h])

    def project_terms():
        pooled_part(0).start()
        for h in range(2):
            high, low = split(gr[pl.ds(1536 + 256 * h, 256), :])
            for k, part in enumerate((high, high, low)):
                ws[pl.ds(768 * h + 256 * k, 256), :] = part

    project_out = []

    def project_block(m):
        spare = ((level, 0), (reduced, 0)) if m % 2 == 0 else ((spatial, 0), (wide, 8))
        if m == 0:
            pooled_part(0).wait()
        if m == 4:
            pooled_part(1).start()
            pooled_part(1).wait()
        for copy in project_out[2 * m - 4 : 2 * m - 2] if m >= 2 else []:
            copy.wait()
        block_rows = proj_all[:, :, :, :, pl.ds(256 * (m % 4), 256)].reshape(256, 256)
        high, low = split(jnp.transpose(block_rows))
        left = jnp.concatenate([high, low, high], axis=1)
        for h, (ref, start) in enumerate(spare):
            ref[pl.ds(start, 256), :] = mm(left, ws[pl.ds(768 * h, 768), :])
            copy = pltpu.make_async_copy(
                ref.at[pl.ds(start, 256)],
                projector.at[pl.ds(256 * m, 256), pl.ds(512 * h, 512)],
                wsem.at[m, h],
            )
            copy.start()
            project_out.append(copy)

    grads = (gs, gr, big)
    lands = (land_s, land_r, land_e)

    def make_job(j):
        k, r0, rows, c0, cols, ring_first = JOBS[j]
        half = grads[k].shape[0] // 2

        def cut(ref, base):
            return ref.at[pl.ds(pl.multiple_of(base + r0, 8), rows), pl.ds(c0, cols)]

        return Job(
            ring_first,
            rows,
            cut(grads[k], sub * half),
            cut(grads[k], (1 - sub) * half),
            cut(lands[k], 0),
            scratches[j],
            jsend.at[j],
            jrecv.at[j],
            jfree.at[j],
        ).run()

    steps = (
        third_norm, third_rest, spatial_level, spatial_norm, spatial_weights,
        reduce_level, reduce_norm, reduce_weights, image_values, project_terms,
        *[functools.partial(project_block, m) for m in range(8)],
    )
    jobs = [make_job(j) for j in range(len(JOBS))]
    for item in ORDER:
        if item < 0:
            steps[-1 - item]()
        else:
            next(jobs[item], None)
    for job in jobs:
        for _ in job:
            pass
    for copy in project_out[-4:]:
        copy.wait()


def training_step(
    images, pixel_mask, pair_row, w_reduce, w_spatial, w_expand, w_project, w_code,
    norm_reduce, norm_spatial, norm_expand, norm_project,
):
    width, inner = w_reduce.shape
    proj, code = w_code.shape
    hbm = pl.BlockSpec(memory_space=pl.ANY)
    vmem = pl.BlockSpec(memory_space=pltpu.VMEM)
    shape = jax.ShapeDtypeStruct
    landings = [
        pltpu.VMEM((landing_rows(ring_first, rows), cols), f32) for _, _, rows, _, cols, ring_first in JOBS
    ]
    return pl.pallas_call(
        step_kernel,
        out_shape=[
            shape((4, 4, 2, 8, width), f32),
            shape((PROJECTOR_ROWS, proj), f32),
            shape((ROWS, width), bf16),
            pltpu.VMEM((8, 128), f32),
            pltpu.VMEM((2, proj), f32),
            pltpu.VMEM((2, width), f32),
            pltpu.VMEM((2, inner), f32),
            pltpu.VMEM((2, inner), f32),
            pltpu.VMEM((ROWS, width), f32),
            pltpu.VMEM((9 * inner, inner), f32),
            pltpu.VMEM((width, inner), f32),
            pltpu.VMEM((inner, width), f32),
        ],
        in_specs=[hbm, vmem, vmem] + [hbm] * 5 + [vmem] * 4,
        out_specs=[hbm] * 3 + [vmem] * 9,
        scratch_shapes=[
            pltpu.VMEM((49, 8, width), bf16),
            pltpu.VMEM((width, inner), bf16),
            pltpu.VMEM((9 * inner, inner), bf16),
            pltpu.VMEM((inner, width), bf16),
            pltpu.VMEM((proj, code), bf16),
            pltpu.VMEM((ROWS, width), bf16),
            pltpu.VMEM((ROWS, inner), f32),
            pltpu.VMEM((ROWS, inner), f32),
            pltpu.VMEM((inner, ROWS), bf16),
            pltpu.VMEM((inner, ROWS), bf16),
            pltpu.VMEM((ROWS, inner), bf16),
            pltpu.VMEM((ROWS, inner), f32),
            pltpu.VMEM((ROWS + 16, inner), f32),
            pltpu.VMEM((ROWS + 128, 3 * inner), bf16),
            pltpu.VMEM((ROWS, 128), f32),
            pltpu.VMEM((8, width), f32),
            pltpu.VMEM((8, width), f32),
            pltpu.VMEM((8, proj), f32),
            pltpu.VMEM((4, 4, 2, 8, proj), f32),
            pltpu.VMEM((256, 256), f32),
            pltpu.VMEM((256, code), f32),
            pltpu.VMEM((8, 128), f32),
            pltpu.VMEM((16, width), f32),
            pltpu.VMEM((2, width), f32),
            pltpu.VMEM((2, width), f32),
            pltpu.VMEM((8, width), f32),
            pltpu.VMEM((32, 2, inner + 128), f32),
            pltpu.VMEM((32, 2, inner), f32),
            pltpu.VMEM((32, 2, inner), f32),
            pltpu.VMEM((32, 2, inner), f32),
            pltpu.VMEM((2, 2, width), f32),
            pltpu.VMEM((4, 2, width), f32),
            pltpu.VMEM((4, 2, width), f32),
            pltpu.VMEM((2, 2, width), f32),
            pltpu.VMEM((4, 2, width), f32),
            pltpu.VMEM((4, 2, width), f32),
            pltpu.VMEM((9 * inner // 2, inner), f32),
            pltpu.VMEM((width // 2, inner), f32),
            pltpu.VMEM((inner // 2, width), f32),
            *landings,
            pltpu.SemaphoreType.DMA((11,)),
            pltpu.SemaphoreType.DMA((6,)),
            pltpu.SemaphoreType.DMA((11,)),
            pltpu.SemaphoreType.DMA((11,)),
            pltpu.SemaphoreType.DMA((2, 14)),
            pltpu.SemaphoreType.DMA((2, 14)),
            pltpu.SemaphoreType.DMA((2, 14)),
            pltpu.SemaphoreType.DMA((2, 14)),
            pltpu.SemaphoreType.DMA((len(JOBS), JOB_SEMS)),
            pltpu.SemaphoreType.DMA((len(JOBS), JOB_SEMS)),
            pltpu.SemaphoreType.REGULAR((len(JOBS),)),
            pltpu.SemaphoreType.DMA((8, 2)),
        ],
        compiler_params=pltpu.CompilerParams(
            collective_id=20, has_side_effects=True, vmem_limit_bytes=VM << 20
        ),
    )(
        images, pixel_mask, pair_row, w_reduce, w_spatial, w_expand, w_project, w_code,
        norm_reduce, norm_spatial, norm_expand, norm_project,
    )


PARTS = 2


def finish_kernel(
    projector, loss, n1, n2, n3, n4, g1, g2, g3, g4,
    project_out, code_out, loss_out, o1, o2, o3, o4, h1, h2, h3, h4,
    held, held_code, sems, load, save,
):
    steps = held.shape[0] // 256

    def through(m):
        at = pl.ds(256 * m, 256)
        return (
            pltpu.make_async_copy(projector.at[at], held.at[at], load.at[m]),
            pltpu.make_async_copy(held.at[at], project_out.at[at], save.at[m]),
        )

    pairs = [through(m) for m in range(steps)]
    pairs.append(
        (
            pltpu.make_async_copy(
                projector.at[pl.ds(held.shape[0], held_code.shape[0]), pl.ds(0, held_code.shape[1])],
                held_code,
                load.at[steps],
            ),
            pltpu.make_async_copy(held_code, code_out, save.at[steps]),
        )
    )
    for read, _ in pairs:
        read.start()
    copies = [
        pltpu.make_async_copy(g1.at[pl.ds(64 * r, 56)], h1.at[pl.ds(56 * r, 56)], sems.at[r]) for r in range(SIDE)
    ]
    for k, (a, b) in enumerate([(g2, h2), (g3, h3), (g4, h4)]):
        part = a.shape[0] // PARTS
        for i in range(PARTS):
            at = pl.ds(part * i, part)
            copies.append(pltpu.make_async_copy(a.at[at], b.at[at], sems.at[SIDE + PARTS * k + i]))
    for copy in copies:
        copy.start()
    loss_out[...] = loss[pl.ds(0, 1), pl.ds(0, 1)]
    o1[...] = n1[...]
    o2[...] = n2[...]
    o3[...] = n3[...]
    o4[...] = n4[...]
    for read, write in pairs:
        read.wait()
        write.start()
    for _, write in pairs:
        write.wait()
    for copy in copies:
        copy.wait()


def finish(projector, project, code, loss, norms, grads):
    width = grads[0].shape[1]
    hbm = pl.BlockSpec(memory_space=pl.ANY)
    vmem = pl.BlockSpec(memory_space=pltpu.VMEM)
    shape = jax.ShapeDtypeStruct
    return pl.pallas_call(
        finish_kernel,
        out_shape=[shape(project, f32), shape(code, f32), shape((1, 1), f32)]
        + [shape(x.shape, f32) for x in norms]
        + [shape((392, width), f32)]
        + [shape(x.shape, f32) for x in grads[1:]],
        in_specs=[hbm] + [vmem] * 9,
        out_specs=[hbm] * 2 + [vmem] * 5 + [hbm] * 4,
        scratch_shapes=[
            pltpu.VMEM(project, f32),
            pltpu.VMEM(code, f32),
            pltpu.SemaphoreType.DMA((SIDE + 3 * PARTS,)),
            pltpu.SemaphoreType.DMA((project[0] // 256 + 1,)),
            pltpu.SemaphoreType.DMA((project[0] // 256 + 1,)),
        ],
        compiler_params=pltpu.CompilerParams(vmem_limit_bytes=14 << 20),
    )(projector, loss, *norms, *grads)


def whiten(codes, pairing):
    highest = lax.Precision.HIGHEST
    total = codes.shape[0]
    centre = jnp.sum(codes, axis=0) / total
    moved = codes - centre
    covariance = jnp.dot(moved.T, moved, precision=highest) / total
    covariance = covariance + whiten_floor * jnp.eye(codes.shape[1], dtype=jnp.float32)
    factor = jnp.linalg.cholesky(covariance)
    inverse = lax.linalg.triangular_solve(factor, jnp.eye(codes.shape[1], dtype=jnp.float32), left_side=True, lower=True)
    white = jnp.dot(moved, inverse.T, precision=highest)
    scale = lax.rsqrt(jnp.sum(white * white, axis=1, keepdims=True) + epsilon)
    unit = white * scale
    same = (pairing[:, None] == pairing[None, :]).astype(jnp.float32)
    gap = 2.0 * unit - jnp.dot(same, unit, precision=highest)
    loss_value = jnp.sum(gap * gap) / total
    grad_unit = 0.5 * (2.0 * gap - jnp.dot(same, gap, precision=highest))
    grad_white = scale * grad_unit - white * scale * scale * scale * jnp.sum(white * grad_unit, axis=1, keepdims=True)
    gram = jnp.dot(grad_white.T, white, precision=highest)
    row = lax.broadcasted_iota(jnp.int32, gram.shape, 0)
    column = lax.broadcasted_iota(jnp.int32, gram.shape, 1)
    lower = jnp.where(row > column, gram, jnp.where(row == column, 0.5 * gram, 0.0))
    both = lower + lower.T
    grad_moved = jnp.dot(grad_white - jnp.dot(white, both, precision=highest) / total, inverse, precision=highest)
    return loss_value, grad_moved - jnp.sum(grad_moved, axis=0) / total


def silu_slope(values):
    sigmoid_value = jax.nn.sigmoid(values)
    return sigmoid_value * (1.0 + values * (1.0 - sigmoid_value))


def moments(sum_value, sum_square, total_count):
    centre = sum_value / total_count
    return (centre, lax.rsqrt(sum_square / total_count - centre * centre + epsilon))


def make_columns(activation):
    images_here, pixel_count, inner_width = activation.shape
    grid_map = activation.reshape(images_here, SIDE, SIDE, inner_width)
    padded = jnp.pad(grid_map, ((0, 0), (1, 1), (1, 1), (0, 0)))
    pieces = [
        padded[:, tap_row : tap_row + SIDE, tap_col : tap_col + SIDE, :]
        for tap_row in range(3)
        for tap_col in range(3)
    ]
    return jnp.concatenate(pieces, axis=3).reshape(images_here * pixel_count, 9 * inner_width)


def fold_columns(columns, images_here, inner_width):
    tap_grads = columns.reshape(images_here, SIDE, SIDE, 9, inner_width)
    padded = jnp.zeros((images_here, SIDE + 2, SIDE + 2, inner_width), jnp.float32)
    for tap_row in range(3):
        for tap_col in range(3):
            padded = padded.at[:, tap_row : tap_row + SIDE, tap_col : tap_col + SIDE, :].add(
                tap_grads[:, :, :, 3 * tap_row + tap_col, :]
            )
    return padded[:, 1 : SIDE + 1, 1 : SIDE + 1, :].reshape(images_here, SIDE * SIDE, inner_width)


def pixel_sums(values, weight):
    return (jnp.sum(values * weight, axis=(0, 1)), jnp.sum(values * values * weight, axis=(0, 1)))


def front(
    masked_low,
    weight,
    counts,
    w_reduce,
    w_spatial,
    w_expand,
    norm_reduce,
    norm_spatial,
    norm_expand,
):
    images_here, pixel_count, width = masked_low.shape
    inner_width = w_reduce.shape[1]
    rows_here = images_here * pixel_count
    reduced = jnp.dot(
        masked_low.reshape(rows_here, width), w_reduce, preferred_element_type=jnp.float32
    ).reshape(images_here, pixel_count, inner_width)
    sum_reduce, square_reduce = pixel_sums(reduced, weight)
    sum_reduce, square_reduce, valid_total = lax.psum((sum_reduce, square_reduce, jnp.sum(counts)), ("dp", "sub"))
    centre_reduce, scale_reduce = moments(sum_reduce, square_reduce, valid_total)
    normed_reduce = (reduced - centre_reduce) * scale_reduce
    level_reduce = norm_reduce[0] * normed_reduce + norm_reduce[1]
    act_reduce = (weight * jax.nn.silu(level_reduce)).astype(jnp.bfloat16)
    columns = make_columns(act_reduce)
    spatial = jnp.dot(
        columns, w_spatial.reshape(9 * inner_width, inner_width), preferred_element_type=jnp.float32
    ).reshape(images_here, pixel_count, inner_width)
    sum_spatial, square_spatial = pixel_sums(spatial, weight)
    sum_spatial, square_spatial = lax.psum((sum_spatial, square_spatial), ("dp", "sub"))
    centre_spatial, scale_spatial = moments(sum_spatial, square_spatial, valid_total)
    normed_spatial = (spatial - centre_spatial) * scale_spatial
    level_spatial = norm_spatial[0] * normed_spatial + norm_spatial[1]
    act_spatial = (weight * jax.nn.silu(level_spatial)).astype(jnp.bfloat16)
    expanded = jnp.dot(
        act_spatial.reshape(rows_here, inner_width), w_expand, preferred_element_type=jnp.float32
    ).reshape(images_here, pixel_count, width)
    sum_expand, square_expand = pixel_sums(expanded, weight)
    sum_expand, square_expand = lax.psum((sum_expand, square_expand), ("dp", "sub"))
    centre_expand, scale_expand = moments(sum_expand, square_expand, valid_total)
    normed_expand = (expanded - centre_expand) * scale_expand
    summed = masked_low.astype(jnp.float32) + norm_expand[0] * normed_expand + norm_expand[1]
    stats = (
        valid_total,
        centre_reduce,
        scale_reduce,
        centre_spatial,
        scale_spatial,
        centre_expand,
        scale_expand,
    )
    return (
        (
            normed_reduce,
            level_reduce,
            columns,
            normed_spatial,
            level_spatial,
            act_spatial,
            normed_expand,
            summed,
        ),
        stats,
    )


def norm_back(upstream, normed, gain, scale_value, sum_grad, dot_grad, total_count):
    return gain * scale_value * (upstream - (sum_grad + normed * dot_grad) / total_count)


def plain_shards(
    images,
    pixel_mask,
    pairing,
    w_reduce,
    w_spatial,
    w_expand,
    w_project,
    w_code,
    norm_reduce,
    norm_spatial,
    norm_expand,
    norm_project,
):
    images_here, pixel_count, width = images.shape
    inner_width = w_reduce.shape[1]
    images_total = pairing.shape[0]
    rows_here = images_here * pixel_count
    highest = lax.Precision.HIGHEST
    weight = pixel_mask.astype(jnp.float32)[:, :, None]
    counts = jnp.sum(weight, axis=1)
    masked_low = images * weight.astype(jnp.bfloat16)
    project_full = w_project.astype(jnp.float32)
    code_full = w_code.astype(jnp.float32)
    saved, stats = front(
        masked_low,
        weight,
        counts,
        w_reduce,
        w_spatial,
        w_expand,
        norm_reduce,
        norm_spatial,
        norm_expand,
    )
    (
        normed_reduce,
        level_reduce,
        columns,
        normed_spatial,
        level_spatial,
        act_spatial,
        normed_expand,
        summed,
    ) = saved
    (
        valid_total,
        centre_reduce,
        scale_reduce,
        centre_spatial,
        scale_spatial,
        centre_expand,
        scale_expand,
    ) = stats
    output = weight * jax.nn.silu(summed)
    own_pooled = jnp.sum(output, axis=1) / counts
    pooled = lax.all_gather(own_pooled, ("dp", "sub"), axis=0, tiled=True)
    projected = jnp.dot(pooled, project_full, precision=highest)
    centre_project, scale_project = moments(
        jnp.sum(projected, axis=0), jnp.sum(projected * projected, axis=0), float(images_total)
    )
    normed_project = (projected - centre_project) * scale_project
    level_project = norm_project[0] * normed_project + norm_project[1]
    hidden = jax.nn.silu(level_project)
    codes = jnp.dot(hidden, code_full, precision=highest)
    loss_value, grad_codes = whiten(codes, pairing)
    grad_w_code = jnp.dot(hidden.T, grad_codes, precision=highest)
    grad_hidden = jnp.dot(grad_codes, code_full.T, precision=highest)
    grad_level_project = grad_hidden * silu_slope(level_project)
    sum_project_grad = jnp.sum(grad_level_project, axis=0)
    dot_project_grad = jnp.sum(grad_level_project * normed_project, axis=0)
    grad_norm_project = jnp.stack([dot_project_grad, sum_project_grad])
    grad_projected = norm_back(
        grad_level_project,
        normed_project,
        norm_project[0],
        scale_project,
        sum_project_grad,
        dot_project_grad,
        float(images_total),
    )
    grad_w_project = jnp.dot(pooled.T, grad_projected, precision=highest)
    own_start = lax.axis_index(("dp", "sub")) * images_here
    own_projected = lax.dynamic_slice_in_dim(grad_projected, own_start, images_here, 0)
    grad_pooled = jnp.dot(own_projected, project_full.T, precision=highest)
    grad_summed = weight * (grad_pooled / counts)[:, None, :] * silu_slope(summed)
    sum_expand_grad, dot_expand_grad = lax.psum(
        (jnp.sum(grad_summed, axis=(0, 1)), jnp.sum(grad_summed * normed_expand, axis=(0, 1))), ("dp", "sub")
    )
    grad_norm_expand = jnp.stack([dot_expand_grad, sum_expand_grad])
    grad_expanded = (
        (
            weight
            * norm_back(
                grad_summed,
                normed_expand,
                norm_expand[0],
                scale_expand,
                sum_expand_grad,
                dot_expand_grad,
                valid_total,
            )
        )
        .astype(jnp.bfloat16)
        .reshape(rows_here, width)
    )
    grad_w_expand = jnp.einsum(
        "rm,rc->mc",
        act_spatial.reshape(rows_here, inner_width),
        grad_expanded,
        preferred_element_type=jnp.float32,
    )
    grad_act_spatial = jnp.einsum(
        "rc,mc->rm", grad_expanded, w_expand, preferred_element_type=jnp.float32
    ).reshape(images_here, pixel_count, inner_width)
    grad_level_spatial = grad_act_spatial * weight * silu_slope(level_spatial)
    sum_spatial_grad, dot_spatial_grad = lax.psum(
        (
            jnp.sum(grad_level_spatial, axis=(0, 1)),
            jnp.sum(grad_level_spatial * normed_spatial, axis=(0, 1)),
        ),
        ("dp", "sub"),
    )
    grad_norm_spatial = jnp.stack([dot_spatial_grad, sum_spatial_grad])
    grad_spatial_out = (
        (
            weight
            * norm_back(
                grad_level_spatial,
                normed_spatial,
                norm_spatial[0],
                scale_spatial,
                sum_spatial_grad,
                dot_spatial_grad,
                valid_total,
            )
        )
        .astype(jnp.bfloat16)
        .reshape(rows_here, inner_width)
    )
    grad_w_spatial = jnp.einsum(
        "rk,rm->km", columns, grad_spatial_out, preferred_element_type=jnp.float32
    ).reshape(3, 3, inner_width, inner_width)
    grad_columns = jnp.einsum(
        "rm,km->rk",
        grad_spatial_out,
        w_spatial.reshape(9 * inner_width, inner_width),
        preferred_element_type=jnp.float32,
    )
    grad_act_reduce = fold_columns(grad_columns, images_here, inner_width)
    grad_level_reduce = grad_act_reduce * weight * silu_slope(level_reduce)
    sum_reduce_grad, dot_reduce_grad = lax.psum(
        (
            jnp.sum(grad_level_reduce, axis=(0, 1)),
            jnp.sum(grad_level_reduce * normed_reduce, axis=(0, 1)),
        ),
        ("dp", "sub"),
    )
    grad_norm_reduce = jnp.stack([dot_reduce_grad, sum_reduce_grad])
    grad_reduced = (
        (
            weight
            * norm_back(
                grad_level_reduce,
                normed_reduce,
                norm_reduce[0],
                scale_reduce,
                sum_reduce_grad,
                dot_reduce_grad,
                valid_total,
            )
        )
        .astype(jnp.bfloat16)
        .reshape(rows_here, inner_width)
    )
    grad_w_reduce = jnp.einsum(
        "rc,rm->cm",
        masked_low.reshape(rows_here, width),
        grad_reduced,
        preferred_element_type=jnp.float32,
    )
    grad_input = jnp.einsum(
        "rm,cm->rc", grad_reduced, w_reduce, preferred_element_type=jnp.float32
    ).reshape(images_here, pixel_count, width)
    grad_images = weight * (grad_summed + grad_input)
    grad_w_spatial, grad_w_reduce, grad_w_expand = lax.psum(
        (grad_w_spatial, grad_w_reduce, grad_w_expand), ("dp", "sub")
    )
    return (
        loss_value,
        grad_images,
        grad_w_reduce,
        grad_w_spatial.reshape(3, 3, inner_width, inner_width),
        grad_w_expand,
        grad_w_project,
        grad_w_code,
        grad_norm_reduce,
        grad_norm_spatial,
        grad_norm_expand,
        grad_norm_project,
    )


def shards(
    images,
    pixel_mask,
    pairing,
    w_reduce,
    w_spatial,
    w_expand,
    w_project,
    w_code,
    norm_reduce,
    norm_spatial,
    norm_expand,
    norm_project,
):
    width, inner = w_reduce.shape
    taps = w_spatial.reshape(9 * inner, inner)
    (
        _, projector, _, loss,
        grad_norm_project, grad_norm_expand, grad_norm_reduce, grad_norm_spatial,
        grad_images, grad_spatial, grad_reduce, grad_expand,
    ) = training_step(
        jnp.transpose(images, (1, 0, 2)),
        pixel_mask,
        pairing.reshape(1, 256),
        w_reduce,
        taps,
        w_expand,
        w_project,
        w_code,
        norm_reduce,
        norm_spatial,
        norm_expand,
        norm_project,
    )
    (
        grad_project, grad_code, loss,
        grad_norm_reduce, grad_norm_spatial, grad_norm_expand, grad_norm_project,
        grad_images, grad_spatial, grad_reduce, grad_expand,
    ) = finish(
        projector,
        w_project.shape,
        w_code.shape,
        loss,
        (grad_norm_reduce, grad_norm_spatial, grad_norm_expand, grad_norm_project),
        (grad_images, grad_spatial, grad_reduce, grad_expand),
    )
    return (
        loss[0, 0],
        jnp.transpose(grad_images.reshape(49, 8, width), (1, 0, 2)),
        grad_reduce,
        grad_spatial.reshape(w_spatial.shape),
        grad_expand,
        grad_project,
        grad_code,
        grad_norm_reduce,
        grad_norm_spatial,
        grad_norm_expand,
        grad_norm_project,
    )


def solution(mesh):
    fits = mesh.shape["dp"] == 16 and mesh.shape["sub"] == 2
    placed = (P(("dp", "sub"), None, None), P(("dp", "sub"), None)) + (P(),) * 10
    return jax.shard_map(
        shards if fits else plain_shards,
        mesh=mesh,
        in_specs=placed,
        out_specs=(P(), P(("dp", "sub"), None, None)) + (P(),) * 9,
        check_vma=False,
    )
```
